32 devices in a mesh: group: 8 (over y, x, core), pos: 4 (over z).
Axes of the slice: x: 2, y: 2, z: 4, core: 2. Of those that a mesh axis runs over, the one named last changes fastest.
Arguments:
- potential: float32 [4, 2, 1536, 512], P(None, None, 'group', 'pos'), may hold values from -0.3 to 0.3
- probe: float32 [8, 4, 128, 256], P('group', None, 'pos'), may hold values from -3 to 3
- amplitudes: bfloat16 [8, 4, 3, 128, 128], P('group', 'pos'), may hold values from 0.1 to 8, as said below
- row_offset: int32 [8, 4, 3], P('group', 'pos'), may hold values from 0 to 64
- col_offset: int32 [8, 4, 3], P('group', 'pos'), may hold values from 0 to 127
- counts: int32 [8, 4], P('group', 'pos'), may hold values from 1 to 3, as said below
Outputs:
- object_grad: float32 [4, 2, 1536, 512], P(None, None, 'group', 'pos')
- probe_grad: float32 [8, 4, 128, 256], P('group', None, 'pos')
The draws below stay inside these ranges and needn't reach their ends.
Inputs may be any that keep to these rules, and one draw needn't show every extreme that they name: A tile's positions fill its first counts slots and later slots are unused; at least one tile has 3. `amplitudes`: every entry is positive.
All inputs are finite; a program needn't handle non-finite values.
Results may differ from the reference program's by a relative error of at most 0.02.
The reference program's roundings to bfloat16 on the way count: a program that leaves them out, or rounds other values in their place, can miss the bound.
Values sent between devices are 32-bit elements; how exact they have to be, the bound alone decides.
No kernel may reach another device: no remote copies, remote signals or barrier semaphores. Data moves between devices by JAX's collectives and lax.ppermute only.
A program may use at most 64 MiB of HBM per device.

```python
import math
import jax
import jax.numpy as jnp
from jax import lax

N = 128
MODES = 4
SLICES = 4
PMAX = 3
ROWS = 192
GROUPS = 8
TILES = 4


def draw_counts(key, part):
    base = jax.random.randint(jax.random.fold_in(key, 11), (GROUPS, TILES), 1, PMAX + 1)
    spot = jax.random.randint(jax.random.fold_in(key, 12), (2,), 0, 1 << 20)
    return base.at[spot[0] % GROUPS, spot[1] % TILES].set(PMAX).astype(jnp.int32)


def draw_amplitudes(key, part):
    place = jnp.arange(GROUPS * TILES, dtype=jnp.float32).reshape(GROUPS, TILES)
    fraction = place / max(GROUPS * TILES - 1, 1)
    tile_odd = (jnp.arange(TILES, dtype=jnp.int32) % 2).astype(jnp.float32)[None, :]
    slot_first = (jnp.arange(PMAX, dtype=jnp.int32) == 0).astype(jnp.float32)
    baseline = jax.random.uniform(jax.random.fold_in(key, 22), (GROUPS, TILES, PMAX, N, N), jnp.float32, 0.25, 1.25)
    factor = (1.0 + 2.0 * fraction) * (1.0 + tile_odd)
    slot_factor = 2.0 - slot_first
    value = baseline * factor[:, :, None, None, None] * slot_factor[None, None, :, None, None]
    return jnp.clip(value, 0.1, 8.0).astype(jnp.bfloat16)


def touch_ends(entries, rng, smallest, top_value):
    extent = entries.shape
    index_at = [jax.random.randint(jax.random.fold_in(rng, axis), (), 0, extent[axis]) for axis in range(len(extent))]
    entries = entries.at[tuple(index_at)].set(smallest)
    longest = extent.index(max(extent))
    index_at[longest] = (index_at[longest] + 1) % extent[longest]
    return entries.at[tuple(index_at)].set(top_value)


def steps_of(key, extent, split, least, top_value):
    loudness, own = 1.0, jax.random.fold_in(key, 6)
    for position, blocks in split:
        draws = jnp.exp(jax.random.uniform(jax.random.fold_in(own, position), (blocks,), jnp.float32, least / len(split), top_value / len(split)))
        loudness = loudness * jnp.repeat(draws, extent[position] // blocks).reshape([-1 if axis == position else 1 for axis in range(len(extent))])
    return loudness


def noise(key, dims, spread, bound, cuts=(), kind=jnp.bfloat16):
    level = steps_of(key, dims, cuts, -0.22, 0.18) if cuts else 1.0
    values = jax.random.normal(key, dims, jnp.float32) * spread * level
    return jnp.minimum(jnp.maximum(values, -bound), bound).astype(kind)


def setup_inputs(seed: int = 0) -> dict:
    key_of = jax.random.split(jax.random.key(seed), 7)
    potential = jnp.clip(jax.random.uniform(key_of[0], (SLICES, 2, GROUPS * ROWS, TILES * N), jnp.float32, -0.3, 0.3) * steps_of(key_of[0], (SLICES, 2, GROUPS * ROWS, TILES * N), ((2, 8), (3, 4)), -0.4, 0.0), -0.3, 0.3)
    probe = noise(key_of[1], (GROUPS, MODES, N, 2 * N), 0.5, 3.0, ((0, 8), (2, 4)), jnp.float32)
    amplitudes = draw_amplitudes(jax.random.fold_in(key_of[6], 71), 0)
    row_offset = touch_ends(jax.random.randint(key_of[3], (GROUPS, TILES, PMAX), 0, ROWS - N + 1), jax.random.fold_in(key_of[3], 1), 0, ROWS - N).astype(jnp.int32)
    col_offset = touch_ends(jax.random.randint(key_of[4], (GROUPS, TILES, PMAX), 0, N), jax.random.fold_in(key_of[4], 1), 0, N - 1).astype(jnp.int32)
    counts = draw_counts(jax.random.fold_in(key_of[6], 71), 0)
    return dict(potential=potential, probe=probe, amplitudes=amplitudes, row_offset=row_offset, col_offset=col_offset, counts=counts)


PROP = 0.25
REG = 0.1

def tables(size):
    idx = jnp.arange(size, dtype=jnp.int32)
    prod = idx[:, None] * idx[None, :] % size
    angle = 2.0 * math.pi / size * prod.astype(jnp.float32)
    cosv = jnp.cos(angle) / math.sqrt(size)
    sinv = jnp.sin(angle) / math.sqrt(size)
    forward = jnp.concatenate([jnp.concatenate([cosv, -sinv], 1), jnp.concatenate([sinv, cosv], 1)], 0)
    inverse = jnp.concatenate([jnp.concatenate([cosv, sinv], 1), jnp.concatenate([-sinv, cosv], 1)], 0)
    return (forward.astype(jnp.bfloat16), inverse.astype(jnp.bfloat16))

def propagator(size):
    idx = jnp.arange(size, dtype=jnp.int32)
    freq = jnp.where(idx < size // 2, idx, idx - size).astype(jnp.float32)
    phase = -2.0 * math.pi * PROP / size * (freq[:, None] * freq[:, None] + freq[None, :] * freq[None, :])
    return jnp.concatenate([jnp.cos(phase), jnp.sin(phase)], 1)

def along_last(wave, table):
    size = wave.shape[-2]
    flat = wave.reshape(-1, 2 * size).astype(jnp.bfloat16).astype(jnp.float32)
    out = jnp.dot(flat, table.astype(jnp.float32), precision=lax.Precision.HIGHEST, preferred_element_type=jnp.float32)
    return out.reshape(wave.shape)

def flip(wave):
    lead = wave.shape[:-2]
    size = wave.shape[-2]
    parts = wave.reshape(lead + (size, 2, size))
    return jnp.swapaxes(parts, -3, -1).reshape(lead + (size, 2 * size))

def transform(wave, table):
    return flip(along_last(flip(along_last(wave, table)), table))

def cmul(left, right):
    size = left.shape[-2]
    lre, lim = (left[..., :size], left[..., size:])
    rre, rim = (right[..., :size], right[..., size:])
    return jnp.concatenate([lre * rre - lim * rim, lre * rim + lim * rre], -1)

def cmulc(left, right):
    size = left.shape[-2]
    lre, lim = (left[..., :size], left[..., size:])
    rre, rim = (right[..., :size], right[..., size:])
    return jnp.concatenate([lre * rre + lim * rim, lre * rim - lim * rre], -1)

def transmit(patch):
    magnitude = jnp.exp(-patch[:, 1])
    return jnp.concatenate([magnitude * jnp.cos(patch[:, 0]), magnitude * jnp.sin(patch[:, 0])], -1)

def potential_grad(trans, tgrad):
    size = trans.shape[-2]
    quot = cmulc(trans, tgrad)
    return jnp.stack([quot[:, size:], -quot[:, :size]], 0)

def one_position(carry, extended, whole, observed, row, col, weight, forward, inverse, kernel):
    grad_ext, probe_acc, misfit = carry
    slices = extended.shape[0]
    size = whole.shape[-2]
    zero = jnp.zeros((), jnp.int32)
    start = (zero, zero, row.astype(jnp.int32), col.astype(jnp.int32))
    patch = lax.dynamic_slice(extended, start, (slices, 2, size, size))
    trans = transmit(patch)
    psi = whole
    stored = []
    exit_wave = psi
    for layer in range(slices):
        stored.append(psi)
        exit_wave = cmul(trans[layer][None], psi)
        if layer + 1 < slices:
            psi = transform(cmul(kernel[None], transform(exit_wave, forward)), inverse)
    far = transform(exit_wave, forward)
    real_part, imag_part = (far[..., :size], far[..., size:])
    inten = lax.optimization_barrier(jnp.sum(real_part * real_part + imag_part * imag_part, axis=0))
    model = jnp.sqrt(inten + REG)
    diff = model - observed
    misfit = misfit + weight * jnp.sum(diff * diff)
    ratio = weight * (1.0 - observed / model)
    wave_grad = transform(far * jnp.concatenate([ratio, ratio], -1)[None], inverse)
    pieces = [None] * slices
    psi_grad = wave_grad
    for layer in reversed(range(slices)):
        tgrad = lax.optimization_barrier(jnp.sum(cmulc(stored[layer], wave_grad), axis=0))
        pieces[layer] = potential_grad(trans[layer], tgrad)
        psi_grad = cmulc(trans[layer][None], wave_grad)
        if layer > 0:
            wave_grad = transform(cmulc(kernel[None], transform(psi_grad, forward)), inverse)
    block = jnp.stack(pieces, 0)
    old = lax.dynamic_slice(grad_ext, start, block.shape)
    grad_ext = lax.dynamic_update_slice(grad_ext, old + block, start)
    return (grad_ext, probe_acc + psi_grad, misfit)

def reference(potential, probe, amplitudes, row_offset, col_offset, counts):
    slices = potential.shape[0]
    size = probe.shape[2]
    groups, tiles = counts.shape
    slots = amplitudes.shape[2]
    rows_tile = potential.shape[2] // groups
    padded = jnp.pad(potential, ((0, 0), (0, 0), (0, 0), (0, size)))
    forward, inverse = tables(size)
    kernel = propagator(size)
    zero = jnp.zeros((), jnp.int32)

    def device(index, carry):
        grad_pad, probe_grads, misfit = carry
        index = index.astype(jnp.int32)
        grp = index // tiles
        til = index % tiles
        start = (zero, zero, (grp * rows_tile).astype(jnp.int32), (til * size).astype(jnp.int32))
        extended = lax.dynamic_slice(padded, start, (slices, 2, rows_tile, 2 * size))
        whole = lax.dynamic_index_in_dim(probe, grp, 0, keepdims=False)
        amps = amplitudes[grp, til].astype(jnp.float32)
        rows_here = row_offset[grp, til]
        cols_here = col_offset[grp, til]
        count = counts[grp, til]

        def slot_step(slot, inner):
            weight = (slot < count).astype(jnp.float32)
            return one_position(inner, extended, whole, amps[slot], rows_here[slot], cols_here[slot], weight, forward, inverse, kernel)
        init = (jnp.zeros((slices, 2, rows_tile, 2 * size), jnp.float32), jnp.zeros(whole.shape, jnp.float32), jnp.zeros((), jnp.float32))
        grad_ext, probe_acc, local = lax.fori_loop(0, slots, slot_step, init)
        old = lax.dynamic_slice(grad_pad, start, grad_ext.shape)
        grad_pad = lax.dynamic_update_slice(grad_pad, old + grad_ext, start)
        old_probe = lax.dynamic_index_in_dim(probe_grads, grp, 0, keepdims=False)
        probe_grads = lax.dynamic_update_index_in_dim(probe_grads, old_probe + probe_acc, grp, 0)
        return (grad_pad, probe_grads, misfit + local)
    init = (jnp.zeros(padded.shape, jnp.float32), jnp.zeros(probe.shape, jnp.float32), jnp.zeros((), jnp.float32))
    grad_pad, probe_grads, misfit = lax.fori_loop(0, groups * tiles, device, init)
    total = jnp.sum(counts).astype(jnp.float32)
    scale = 1.0 / jnp.sqrt(misfit / (total * size * size) + 1e-06)
    return (grad_pad[..., :tiles * size] * scale, probe_grads * scale)
```

```python
import functools
import math

import jax
import jax.numpy as jnp
from jax import lax
from jax.experimental import pallas as pl
from jax.experimental.pallas import tpu as pltpu
from jax.sharding import PartitionSpec as P

PROP = 0.25
REG = 0.1
VMEM = pl.BlockSpec(memory_space=pltpu.VMEM)
SMEM = pl.BlockSpec(memory_space=pltpu.SMEM)


def tables(size):
    idx = jnp.arange(size, dtype=jnp.int32)
    prod = idx[:, None] * idx[None, :] % size
    angle = 2.0 * math.pi / size * prod.astype(jnp.float32)
    cosv = jnp.cos(angle) / math.sqrt(size)
    sinv = jnp.sin(angle) / math.sqrt(size)
    forward = jnp.concatenate(
        [jnp.concatenate([cosv, -sinv], 1), jnp.concatenate([sinv, cosv], 1)], 0
    )
    inverse = jnp.concatenate(
        [jnp.concatenate([cosv, sinv], 1), jnp.concatenate([-sinv, cosv], 1)], 0
    )
    return (forward.astype(jnp.bfloat16), inverse.astype(jnp.bfloat16))


def propagator(size):
    idx = jnp.arange(size, dtype=jnp.int32)
    freq = jnp.where(idx < size // 2, idx, idx - size).astype(jnp.float32)
    phase = (
        -2.0
        * math.pi
        * PROP
        / size
        * (freq[:, None] * freq[:, None] + freq[None, :] * freq[None, :])
    )
    return jnp.concatenate([jnp.cos(phase), jnp.sin(phase)], 1)


def mul(a, b):
    return a[0] * b[0] - a[1] * b[1], a[0] * b[1] + a[1] * b[0]


def mulc(a, b):
    return a[0] * b[0] + a[1] * b[1], a[0] * b[1] - a[1] * b[0]


def sine(x):
    y = x * x
    return x * (1.0 - y * (1 / 6) * (1.0 - y * (1 / 20) * (1.0 - y * (1 / 42) * (1.0 - y * (1 / 72)))))


def cosine(x):
    y = x * x
    return 1.0 - y * 0.5 * (1.0 - y * (1 / 12) * (1.0 - y * (1 / 30) * (1.0 - y * (1 / 56) * (1.0 - y * (1 / 90)))))


def transform(waves, right, left):
    size = waves[0][0].shape[0]
    out = []
    for first in range(0, len(waves), 2):
        pair = waves[first : first + 2]
        rows = jnp.concatenate(
            [jnp.concatenate([re.astype(jnp.bfloat16), im.astype(jnp.bfloat16)], 1) for re, im in pair], 0
        )
        mid = jnp.dot(rows, right, preferred_element_type=jnp.float32).astype(jnp.bfloat16)
        mid = jnp.concatenate(
            [
                jnp.concatenate([mid[i * size : (i + 1) * size, :size], mid[i * size : (i + 1) * size, size:]], 0)
                for i in range(len(pair))
            ],
            1,
        )
        done = jnp.dot(left, mid, preferred_element_type=jnp.float32)
        for i in range(len(pair)):
            out.append((done[:size, i * size : (i + 1) * size], done[size:, i * size : (i + 1) * size]))
    return out


def scan_kernel(
    pieces,
    me_ref,
    row_ref,
    col_ref,
    count_ref,
    own_ref,
    next_ref,
    amps_ref,
    forward_ref,
    inverse_ref,
    kernel_ref,
    *refs,
):
    probe_refs = refs[:pieces]
    grad_ref, spill_ref, misfit_ref = refs[pieces : pieces + 3]
    share_refs = refs[pieces + 3 : 2 * pieces + 3]
    psi_ref, trans_ref, acc_ref = refs[2 * pieces + 3 :]
    slices, _, _, size = own_ref.shape
    modes = probe_refs[0].shape[1]
    part = probe_refs[0].shape[2]
    me = me_ref[0]

    for k in range(pieces):
        place = pl.multiple_of(lax.rem(me + k, pieces) * part, part)
        psi_ref[0, :, pl.ds(place, part), :] = probe_refs[k][0]
    grad_ref[...] = jnp.zeros_like(grad_ref)
    spill_ref[...] = jnp.zeros_like(spill_ref)
    acc_ref[...] = jnp.zeros_like(acc_ref)
    lanes = lax.broadcasted_iota(jnp.int32, (size, size), 1)

    def load(ref, *lead):
        return [(ref[(*lead, m, slice(None), slice(0, size))], ref[(*lead, m, slice(None), slice(size, None))]) for m in range(modes)]

    def slot_step(slot, misfit):
        row = row_ref[slot]
        col = col_ref[slot]
        back = lax.rem(size - col, size)
        for s in range(slices):
            parts = []
            for channel in range(2):
                here = pltpu.roll(own_ref[s, channel, pl.ds(row, size), :], back, 1)
                there = pltpu.roll(next_ref[s, channel, pl.ds(row, size), :], back, 1)
                parts.append(jnp.where(lanes < size - col, here, there))
            magnitude = jnp.exp(-parts[1])
            trans_ref[s, :, :size] = magnitude * cosine(parts[0])
            trans_ref[s, :, size:] = magnitude * sine(parts[0])

        def trans(s):
            return trans_ref[s, :, :size], trans_ref[s, :, size:]

        forward = forward_ref[...]
        inverse = inverse_ref[...]

        def prop():
            return kernel_ref[:, :size], kernel_ref[:, size:]

        for s in range(slices):
            waves = [mul(trans(s), w) for w in load(psi_ref, s)]
            waves = transform(waves, forward, inverse)
            if s + 1 < slices:
                waves = transform([mul(prop(), w) for w in waves], inverse, forward)
                for m, (re, im) in enumerate(waves):
                    psi_ref[s + 1, m, :, :size] = re
                    psi_ref[s + 1, m, :, size:] = im
        inten = sum(re * re + im * im for re, im in waves)
        model = jnp.sqrt(inten + REG)
        observed = amps_ref[slot].astype(jnp.float32)
        diff = model - observed
        misfit = misfit + jnp.sum(diff * diff, axis=0, keepdims=True)
        ratio = 1.0 - observed / model
        waves = transform([(ratio * re, ratio * im) for re, im in waves], inverse, forward)
        for s in reversed(range(slices)):
            waves = [mulc(trans(s), w) for w in waves]
            quot = [mulc(p, w) for p, w in zip(load(psi_ref, s), waves)]
            values = sum(im for _, im in quot), -sum(re for re, _ in quot)
            for channel in range(2):
                turned = pltpu.roll(values[channel], col, 1)
                inside = lanes >= col
                grad_ref[s, channel, pl.ds(row, size), :] += jnp.where(inside, turned, 0.0)
                spill_ref[s, channel, pl.ds(row, size), :] += jnp.where(inside, 0.0, turned)
            if s > 0:
                waves = transform(waves, forward, inverse)
                waves = transform([mulc(prop(), w) for w in waves], inverse, forward)
        for m, (re, im) in enumerate(waves):
            acc_ref[m, :, :size] += re
            acc_ref[m, :, size:] += im
        return misfit

    count = count_ref[0]
    misfit = lax.fori_loop(0, count, slot_step, jnp.zeros((1, size), jnp.float32))
    total = jnp.sum(misfit, axis=1, keepdims=True)
    lane = lax.broadcasted_iota(jnp.int32, misfit_ref.shape, 1)
    misfit_ref[...] = jnp.where(lane == 0, total, jnp.where(lane == 1, count.astype(jnp.float32), 0.0))
    for k in range(pieces):
        place = pl.multiple_of(lax.rem(me + k, pieces) * part, part)
        share_refs[k][...] = acc_ref[:, pl.ds(place, part), :]


def total_over(value, axis):
    n = lax.axis_size(axis)
    if n & (n - 1):
        return lax.psum(value, axis)
    step = 1
    while step < n:
        value = value + lax.ppermute(value, axis, [(i, i ^ step) for i in range(n)])
        step *= 2
    return value


def body(potential, probe, amplitudes, row_offset, col_offset, counts):
    slices, _, rows, size = potential.shape
    modes = probe.shape[1]
    pieces = lax.axis_size("pos")
    part = probe.shape[2]
    me = lax.axis_index("pos").astype(jnp.int32).reshape(1)
    parts = [probe] + [
        lax.ppermute(probe, "pos", [((i + k) % pieces, i) for i in range(pieces)]) for k in range(1, pieces)
    ]
    neighbour = lax.ppermute(potential, "pos", [(i, i - 1) for i in range(1, pieces)])
    forward, inverse = tables(size)
    kernel = propagator(size)
    f32 = jnp.float32
    out = pl.pallas_call(
        functools.partial(scan_kernel, pieces),
        out_shape=[
            jax.ShapeDtypeStruct(potential.shape, f32),
            jax.ShapeDtypeStruct(potential.shape, f32),
            jax.ShapeDtypeStruct((1, size), f32),
        ]
        + [jax.ShapeDtypeStruct((modes, part, 2 * size), f32)] * pieces,
        in_specs=[SMEM] * 4 + [VMEM] * (6 + pieces),
        out_specs=[VMEM] * (3 + pieces),
        scratch_shapes=[
            pltpu.VMEM((slices, modes, size, 2 * size), f32),
            pltpu.VMEM((slices, size, 2 * size), f32),
            pltpu.VMEM((modes, size, 2 * size), f32),
        ],
        compiler_params=pltpu.CompilerParams(vmem_limit_bytes=40 * 2**20),
        name="scan",
    )(
        me,
        row_offset[0, 0],
        col_offset[0, 0],
        counts[0],
        potential,
        neighbour,
        amplitudes[0, 0],
        forward,
        inverse,
        kernel,
        *parts,
    )
    grad, spill, sums = out[:3]
    shares = out[3:]
    arrived = lax.ppermute(spill, "pos", [(i, i + 1) for i in range(pieces - 1)])
    sums = total_over(total_over(sums, "group"), "pos")
    scale = 1.0 / jnp.sqrt(sums[0, 0] / (sums[0, 1] * size * size) + 1e-06)
    share = shares[0]
    for k in range(1, pieces):
        share = share + lax.ppermute(shares[k], "pos", [(i, (i + k) % pieces) for i in range(pieces)])
    return ((grad + arrived) * scale, (share * scale)[None])


def solution(mesh):
    placed = (
        P(None, None, "group", "pos"),
        P("group", None, "pos", None),
        P("group", "pos", None, None, None),
        P("group", "pos", None),
        P("group", "pos", None),
        P("group", "pos"),
    )
    return jax.shard_map(
        body,
        mesh=mesh,
        in_specs=placed,
        out_specs=(P(None, None, "group", "pos"), P("group", None, "pos", None)),
        check_vma=False,
    )
```

```python
import functools
import math

import jax
import jax.numpy as jnp
import ml_dtypes
import numpy as np
from jax import lax
from jax.experimental import pallas as pl
from jax.experimental.pallas import tpu as pltpu
from jax.sharding import PartitionSpec as P

PROP = 0.25
REG = 0.1
VMEM = pl.BlockSpec(memory_space=pltpu.VMEM)
SMEM = pl.BlockSpec(memory_space=pltpu.SMEM)


@functools.lru_cache(maxsize=None)
def tables(size):
    idx = np.arange(size)
    angle = np.float32(2.0 * math.pi / size) * (idx[:, None] * idx[None, :] % size).astype(np.float32)
    cosv = (np.cos(angle) / np.float32(math.sqrt(size))).astype(ml_dtypes.bfloat16).astype(np.float64)
    sinv = (np.sin(angle) / np.float32(math.sqrt(size))).astype(ml_dtypes.bfloat16).astype(np.float64)
    forward = np.block([[cosv, -sinv], [sinv, cosv]])
    inverse = np.block([[cosv, sinv], [-sinv, cosv]])
    freq = np.where(idx < size // 2, idx, idx - size).astype(np.float64)
    phase = -2.0 * math.pi * PROP / size * freq * freq
    real, imag = np.diag(np.cos(phase)), np.diag(np.sin(phase))
    ahead = forward @ np.block([[real, imag], [-imag, real]]) @ inverse
    behind = forward @ np.block([[real, -imag], [imag, real]]) @ inverse
    return [np.ascontiguousarray(t).astype(ml_dtypes.bfloat16) for t in (forward, inverse, ahead, ahead.T, behind, behind.T)]


def mul(a, b):
    return a[0] * b[0] - a[1] * b[1], a[0] * b[1] + a[1] * b[0]


def mulc(a, b):
    return a[0] * b[0] + a[1] * b[1], a[0] * b[1] - a[1] * b[0]


def sine(x):
    y = x * x
    return x * (1.0 - y * (1 / 6) * (1.0 - y * (1 / 20) * (1.0 - y * (1 / 42) * (1.0 - y * (1 / 72)))))


def cosine(x):
    y = x * x
    return 1.0 - y * 0.5 * (1.0 - y * (1 / 12) * (1.0 - y * (1 / 30) * (1.0 - y * (1 / 56) * (1.0 - y * (1 / 90)))))


def transform(waves, right, left):
    size = waves[0][0].shape[0]
    pairs = [waves[first : first + 2] for first in range(0, len(waves), 2)]
    mids = []
    for pair in pairs:
        rows = jnp.concatenate(
            [jnp.concatenate([re.astype(jnp.bfloat16), im.astype(jnp.bfloat16)], 1) for re, im in pair], 0
        )
        mid = jnp.dot(rows, right, preferred_element_type=jnp.float32).astype(jnp.bfloat16)
        cut = [mid[i * size : (i + 1) * size] for i in range(len(pair))]
        mids.append(jnp.concatenate([jnp.concatenate([m[:, :size], m[:, size:]], 0) for m in cut], 1))
    out = []
    for pair, mid in zip(pairs, mids):
        done = jnp.dot(left, mid, preferred_element_type=jnp.float32)
        for i in range(len(pair)):
            out.append((done[:size, i * size : (i + 1) * size], done[size:, i * size : (i + 1) * size]))
    return out


def scan_kernel(
    pieces,
    me_ref,
    row_ref,
    col_ref,
    count_ref,
    own_ref,
    next_ref,
    amps_ref,
    forward_ref,
    inverse_ref,
    ahead_ref,
    ahead_left_ref,
    behind_ref,
    behind_left_ref,
    *refs,
):
    probe_refs = refs[:pieces]
    grad_ref, spill_ref, misfit_ref = refs[pieces : pieces + 3]
    share_refs = refs[pieces + 3 : 2 * pieces + 3]
    psi_ref, trans_ref, acc_ref = refs[2 * pieces + 3 :]
    slices, _, _, size = own_ref.shape
    modes = probe_refs[0].shape[1]
    part = probe_refs[0].shape[2]
    me = me_ref[0]

    for k in range(pieces):
        place = pl.multiple_of(lax.rem(me + k, pieces) * part, part)
        psi_ref[0, :, pl.ds(place, part), :] = probe_refs[k][0]
    grad_ref[...] = jnp.zeros_like(grad_ref)
    spill_ref[...] = jnp.zeros_like(spill_ref)
    acc_ref[...] = jnp.zeros_like(acc_ref)
    lanes = lax.broadcasted_iota(jnp.int32, (size, size), 1)

    def load(ref, *lead):
        return [(ref[(*lead, m, slice(None), slice(0, size))], ref[(*lead, m, slice(None), slice(size, None))]) for m in range(modes)]

    def slot_step(slot, misfit):
        row = row_ref[slot]
        col = col_ref[slot]
        back = lax.rem(size - col, size)
        for s in range(slices):
            parts = []
            for channel in range(2):
                here = pltpu.roll(own_ref[s, channel, pl.ds(row, size), :], back, 1)
                there = pltpu.roll(next_ref[s, channel, pl.ds(row, size), :], back, 1)
                parts.append(jnp.where(lanes < size - col, here, there))
            magnitude = jnp.exp(-parts[1])
            trans_ref[s, :, :size] = magnitude * cosine(parts[0])
            trans_ref[s, :, size:] = magnitude * sine(parts[0])

        def trans(s):
            return trans_ref[s, :, :size], trans_ref[s, :, size:]

        forward = forward_ref[...]
        inverse = inverse_ref[...]

        for s in range(slices):
            waves = [mul(trans(s), w) for w in load(psi_ref, s)]
            if s + 1 == slices:
                waves = transform(waves, forward, inverse)
            else:
                waves = transform(waves, ahead_ref[...], ahead_left_ref[...])
                for m, (re, im) in enumerate(waves):
                    psi_ref[s + 1, m, :, :size] = re
                    psi_ref[s + 1, m, :, size:] = im
        inten = sum(re * re + im * im for re, im in waves)
        model = jnp.sqrt(inten + REG)
        observed = amps_ref[slot].astype(jnp.float32)
        diff = model - observed
        misfit = misfit + jnp.sum(diff * diff, axis=0, keepdims=True)
        ratio = 1.0 - observed / model
        waves = transform([(ratio * re, ratio * im) for re, im in waves], inverse, forward)
        for s in reversed(range(slices)):
            waves = [mulc(trans(s), w) for w in waves]
            quot = [mulc(p, w) for p, w in zip(load(psi_ref, s), waves)]
            values = sum(im for _, im in quot), -sum(re for re, _ in quot)
            for channel in range(2):
                turned = pltpu.roll(values[channel], col, 1)
                inside = lanes >= col
                grad_ref[s, channel, pl.ds(row, size), :] += jnp.where(inside, turned, 0.0)
                spill_ref[s, channel, pl.ds(row, size), :] += jnp.where(inside, 0.0, turned)
            if s > 0:
                waves = transform(waves, behind_ref[...], behind_left_ref[...])
        for m, (re, im) in enumerate(waves):
            acc_ref[m, :, :size] += re
            acc_ref[m, :, size:] += im
        return misfit

    count = count_ref[0]
    misfit = lax.fori_loop(0, count, slot_step, jnp.zeros((1, size), jnp.float32))
    total = jnp.sum(misfit, axis=1, keepdims=True)
    lane = lax.broadcasted_iota(jnp.int32, misfit_ref.shape, 1)
    misfit_ref[...] = jnp.where(lane == 0, total, jnp.where(lane == 1, count.astype(jnp.float32), 0.0))
    for k in range(pieces):
        place = pl.multiple_of(lax.rem(me + k, pieces) * part, part)
        share_refs[k][...] = acc_ref[:, pl.ds(place, part), :]


def total_over(value, axis):
    n = lax.axis_size(axis)
    if n & (n - 1):
        return lax.psum(value, axis)
    step = 1
    while step < n:
        value = value + lax.ppermute(value, axis, [(i, i ^ step) for i in range(n)])
        step *= 2
    return value


def body(potential, probe, amplitudes, row_offset, col_offset, counts):
    slices, _, rows, size = potential.shape
    modes = probe.shape[1]
    pieces = lax.axis_size("pos")
    part = probe.shape[2]
    me = lax.axis_index("pos").astype(jnp.int32).reshape(1)
    parts = [probe] + [
        lax.ppermute(probe, "pos", [((i + k) % pieces, i) for i in range(pieces)]) for k in range(1, pieces)
    ]
    neighbour = lax.ppermute(potential, "pos", [(i, i - 1) for i in range(1, pieces)])
    f32 = jnp.float32
    out = pl.pallas_call(
        functools.partial(scan_kernel, pieces),
        out_shape=[
            jax.ShapeDtypeStruct(potential.shape, f32),
            jax.ShapeDtypeStruct(potential.shape, f32),
            jax.ShapeDtypeStruct((1, size), f32),
        ]
        + [jax.ShapeDtypeStruct((modes, part, 2 * size), f32)] * pieces,
        in_specs=[SMEM] * 4 + [VMEM] * (9 + pieces),
        out_specs=[VMEM] * (3 + pieces),
        scratch_shapes=[
            pltpu.VMEM((slices, modes, size, 2 * size), f32),
            pltpu.VMEM((slices, size, 2 * size), f32),
            pltpu.VMEM((modes, size, 2 * size), f32),
        ],
        compiler_params=pltpu.CompilerParams(vmem_limit_bytes=40 * 2**20),
        name="scan",
    )(
        me,
        row_offset[0, 0],
        col_offset[0, 0],
        counts[0],
        potential,
        neighbour,
        amplitudes[0, 0],
        *tables(size),
        *parts,
    )
    grad, spill, sums = out[:3]
    shares = out[3:]
    arrived = lax.ppermute(spill, "pos", [(i, i + 1) for i in range(pieces - 1)])
    sums = total_over(total_over(sums, "group"), "pos")
    scale = 1.0 / jnp.sqrt(sums[0, 0] / (sums[0, 1] * size * size) + 1e-06)
    share = shares[0]
    for k in range(1, pieces):
        share = share + lax.ppermute(shares[k], "pos", [(i, (i + k) % pieces) for i in range(pieces)])
    return ((grad + arrived) * scale, (share * scale)[None])


def solution(mesh):
    placed = (
        P(None, None, "group", "pos"),
        P("group", None, "pos", None),
        P("group", "pos", None, None, None),
        P("group", "pos", None),
        P("group", "pos", None),
        P("group", "pos"),
    )
    return jax.shard_map(
        body,
        mesh=mesh,
        in_specs=placed,
        out_specs=(P(None, None, "group", "pos"), P("group", None, "pos", None)),
        check_vma=False,
    )
```

```python
import functools
import math

import jax
import jax.numpy as jnp
import ml_dtypes
import numpy as np
from jax import lax
from jax.experimental import pallas as pl
from jax.experimental.pallas import tpu as pltpu
from jax.sharding import PartitionSpec as P

PROP = 0.25
REG = 0.1
VMEM = pl.BlockSpec(memory_space=pltpu.VMEM)
SMEM = pl.BlockSpec(memory_space=pltpu.SMEM)


@functools.lru_cache(maxsize=None)
def tables(size):
    idx = np.arange(size)
    angle = np.float32(2.0 * math.pi / size) * (idx[:, None] * idx[None, :] % size).astype(np.float32)
    cosv = (np.cos(angle) / np.float32(math.sqrt(size))).astype(ml_dtypes.bfloat16).astype(np.float64)
    sinv = (np.sin(angle) / np.float32(math.sqrt(size))).astype(ml_dtypes.bfloat16).astype(np.float64)
    forward = np.block([[cosv, -sinv], [sinv, cosv]])
    inverse = np.block([[cosv, sinv], [-sinv, cosv]])
    freq = np.where(idx < size // 2, idx, idx - size).astype(np.float64)
    phase = -2.0 * math.pi * PROP / size * freq * freq
    real, imag = np.diag(np.cos(phase)), np.diag(np.sin(phase))
    ahead = forward @ np.block([[real, imag], [-imag, real]]) @ inverse
    behind = forward @ np.block([[real, -imag], [imag, real]]) @ inverse
    return np.stack([forward, inverse, ahead, ahead.T, behind, behind.T]).astype(ml_dtypes.bfloat16)


def mul(a, b):
    return a[0] * b[0] - a[1] * b[1], a[0] * b[1] + a[1] * b[0]


def mulc(a, b):
    return a[0] * b[0] + a[1] * b[1], a[0] * b[1] - a[1] * b[0]


def sine(x):
    y = x * x
    return x * (1.0 - y * (1 / 6) * (1.0 - y * (1 / 20) * (1.0 - y * (1 / 42) * (1.0 - y * (1 / 72)))))


def cosine(x):
    y = x * x
    return 1.0 - y * 0.5 * (1.0 - y * (1 / 12) * (1.0 - y * (1 / 30) * (1.0 - y * (1 / 56) * (1.0 - y * (1 / 90)))))


def transform(waves, right, left):
    size = waves[0][0].shape[0]
    pairs = [waves[first : first + 2] for first in range(0, len(waves), 2)]
    mids = []
    for pair in pairs:
        rows = jnp.concatenate(
            [jnp.concatenate([re.astype(jnp.bfloat16), im.astype(jnp.bfloat16)], 1) for re, im in pair], 0
        )
        mid = jnp.dot(rows, right, preferred_element_type=jnp.float32).astype(jnp.bfloat16)
        cut = [mid[i * size : (i + 1) * size] for i in range(len(pair))]
        mids.append(jnp.concatenate([jnp.concatenate([m[:, :size], m[:, size:]], 0) for m in cut], 1))
    out = []
    for pair, mid in zip(pairs, mids):
        done = jnp.dot(left, mid, preferred_element_type=jnp.float32)
        for i in range(len(pair)):
            out.append((done[:size, i * size : (i + 1) * size], done[size:, i * size : (i + 1) * size]))
    return out


def swap(values, half):
    return pltpu.roll(values, half, values.ndim - 1)


def low_lanes(shape):
    return lax.broadcasted_iota(jnp.int32, shape, len(shape) - 1) < shape[-1] // 2


def pack(pair):
    half = pair[0].shape[-1] // 2
    low = low_lanes(pair[0].shape)
    return jnp.where(low, pair[0], swap(pair[1], half)), jnp.where(low, swap(pair[0], half), pair[1])


def unpack(lows, highs):
    half = lows.shape[-1] // 2
    low = low_lanes(lows.shape)
    return jnp.where(low, lows, swap(highs, half)), jnp.where(low, swap(lows, half), highs)


def pack_kernel(groups, potential_ref, amps_ref, sent_ref, *refs):
    for i, group in enumerate(groups):
        for j, s in enumerate(group):
            lows, highs = pack((potential_ref[s, 0], potential_ref[s, 1]))
            refs[2 * i][j] = lows
            refs[2 * i + 1][j] = highs
    sent_ref[...] = amps_ref[...].astype(jnp.float32)


class Names:
    def __init__(self, names, refs):
        self.__dict__.update(zip(names, refs))

    def get(self, name):
        return self.__dict__[name]


def stage_kernel(names, ahead, top, back, pieces, *refs):
    r = Names(names, refs)
    size = r.tables.shape[-1] // 2
    half = size // 2
    rows = r.own_0.shape[-2] if ahead else r.grad_0.shape[-2]
    modes = r.modes_ref.shape[0]
    slots = (r.mine.shape[0] - 1) // 2
    me = r.me[0]
    last = me == pieces - 1
    lanes = lax.broadcasted_iota(jnp.int32, (size, size), 1)

    number = jnp.int32(0)
    for k in range(2 * slots):
        source, p = (r.mine, k) if k < slots else (r.prev, k - slots)
        stays = (source[slots + p] < half) | last if k < slots else source[slots + p] >= half
        held = (p < source[2 * slots]) & stays
        r.held[number] = jnp.int32(k)
        number = number + held.astype(jnp.int32)

    for i, s in enumerate(ahead):
        halo = unpack(r.lows[i], r.highs[i])
        for tile, pair in enumerate(((r.own_0[s, 0], r.own_0[s, 1]), halo)):
            magnitude = jnp.exp(-pair[1])
            r.tiles[i, tile, 0] = magnitude * cosine(pair[0])
            r.tiles[i, tile, 1] = magnitude * sine(pair[0])
        r.tiles[i, 2, 0] = jnp.ones((rows, size), jnp.float32)
        r.tiles[i, 2, 1] = jnp.zeros((rows, size), jnp.float32)
    if 0 in ahead:
        part = r.piece_0.shape[-2]
        for k in range(pieces):
            place = pl.multiple_of(lax.rem(me + k, pieces) * part, part)
            r.psi_0[:, pl.ds(place, part), :] = r.get("piece_%d" % k)[0]
    if back:
        r.grads[...] = jnp.zeros_like(r.grads)
    if 0 in back:
        r.total[...] = jnp.zeros_like(r.total)

    def load(ref, *lead):
        return [(ref[(*lead, m, slice(None), slice(0, size))], ref[(*lead, m, slice(None), slice(size, None))]) for m in range(modes)]

    def store(ref, waves, *lead):
        for m, (re, im) in enumerate(waves):
            ref[(*lead, m, slice(None), slice(0, size))] = re
            ref[(*lead, m, slice(None), slice(size, None))] = im

    def psi(s, at):
        return load(r.psi_0) if s == 0 else load(r.get("psi_%d" % s), at)

    def trans(s, at):
        ref = r.get("trans_%d" % s)
        return ref[at, 0], ref[at, 1]

    def slot_step(at, misfit):
        k = r.held[at]
        p = lax.rem(k, slots)
        own = k < slots
        row = jnp.where(own, r.mine[p], r.prev[p])
        col = jnp.where(own, r.mine[slots + p], r.prev[slots + p])
        left = jnp.where(own, 0, 1)
        right = jnp.where(own, jnp.where(last, 2, 1), 0)
        turn = lax.rem(size - col, size)
        if ahead:
            waves = psi(ahead[0], at)
        for i, s in enumerate(ahead):
            for c in range(2):
                here = pltpu.roll(r.tiles[i, left, c, pl.ds(row, size), :], turn, 1)
                there = pltpu.roll(r.tiles[i, right, c, pl.ds(row, size), :], turn, 1)
                r.get("trans_%d" % s)[at, c] = jnp.where(lanes < size - col, here, there)
            waves = [mul(trans(s, at), w) for w in waves]
            if top and s == ahead[-1]:
                waves = transform(waves, r.tables[0], r.tables[1])
            else:
                waves = transform(waves, r.tables[2], r.tables[3])
                store(r.get("psi_%d" % (s + 1)), waves, at)
        if top:
            inten = sum(re * re + im * im for re, im in waves)
            model = jnp.sqrt(inten + REG)
            observed = jnp.where(own, r.amps[p].astype(jnp.float32), r.amps_prev[p])
            diff = model - observed
            misfit = misfit + jnp.sum(diff * diff, axis=0, keepdims=True)
            ratio = 1.0 - observed / model
            waves = transform([(ratio * re, ratio * im) for re, im in waves], r.tables[1], r.tables[0])
        elif back:
            waves = load(r.wave_in, at)
        for i, s in enumerate(back):
            waves = [mulc(trans(s, at), w) for w in waves]
            quot = [mulc(a, w) for a, w in zip(psi(s, at), waves)]
            values = sum(im for _, im in quot), -sum(re for re, _ in quot)
            for c in range(2):
                turned = pltpu.roll(values[c], col, 1)
                inside = lanes >= col
                r.grads[i, left, c, pl.ds(row, size), :] += jnp.where(inside, turned, 0.0)
                r.grads[i, right, c, pl.ds(row, size), :] += jnp.where(inside, 0.0, turned)
            if s > 0:
                waves = transform(waves, r.tables[4], r.tables[5])
        if 0 in back:
            for m, (re, im) in enumerate(waves):
                r.total[m, :, :size] += re
                r.total[m, :, size:] += im
        elif back:
            store(r.wave_out, waves, at)
        return misfit

    misfit = lax.fori_loop(0, number, slot_step, jnp.zeros((1, size), jnp.float32))
    if top:
        value = jnp.sum(misfit, axis=1, keepdims=True)
        lane = lax.broadcasted_iota(jnp.int32, r.sums.shape, 1)
        count = r.mine[2 * slots].astype(jnp.float32)
        r.sums[...] = jnp.where(lane == 0, value, jnp.where(lane == 1, count, 0.0))
    for i, s in enumerate(back):
        r.grad_0[i] = r.grads[i, 0]
        lows, highs = pack((r.grads[i, 1, 0], r.grads[i, 1, 1]))
        r.to_right[i] = lows
        r.to_left[i] = highs
    if 0 in back:
        part = r.share_0.shape[-2]
        for k in range(pieces):
            place = pl.multiple_of(lax.rem(me + k, pieces) * part, part)
            r.get("share_%d" % k)[...] = r.total[:, pl.ds(place, part), :]


def stage(given, made, scratch, ahead, top, back, pieces, name):
    names = [n for n, _, _ in given] + [n for n, _ in made] + [n for n, _ in scratch]
    out = pl.pallas_call(
        functools.partial(stage_kernel, names, ahead, top, back, pieces),
        out_shape=[jax.ShapeDtypeStruct(shape, jnp.float32) for _, shape in made],
        in_specs=[SMEM if small else VMEM for _, _, small in given],
        out_specs=[VMEM] * len(made),
        scratch_shapes=[x for _, x in scratch],
        compiler_params=pltpu.CompilerParams(vmem_limit_bytes=24 * 2**20),
        cost_estimate=pl.CostEstimate(flops=(len(ahead) + len(back) + 1) * 10**9, bytes_accessed=10**7, transcendentals=0),
        name=name,
    )(*[x for _, x, _ in given])
    return dict(zip([n for n, _ in made], out))


def finish_kernel(groups, pieces, *refs):
    count = len(groups)
    grads, lows, highs = refs[:count], refs[count : 2 * count], refs[2 * count : 3 * count]
    shares = refs[3 * count : 3 * count + pieces]
    sums = refs[3 * count + pieces : 3 * count + 2 * pieces]
    grad_ref, share_ref = refs[3 * count + 2 * pieces :]
    size = grad_ref.shape[-1]
    sums = sum(ref[...] for ref in sums)
    scale = lax.rsqrt(sums[:, 0:1] / (sums[:, 1:2] * (size * size)) + 1e-06)
    for g, group in enumerate(groups):
        for i, s in enumerate(group):
            arrived = unpack(lows[g][i], highs[g][i])
            for c in range(2):
                grad_ref[s, c] = (grads[g][i, c] + arrived[c]) * scale
    share_ref[0] = sum(ref[...] for ref in shares) * scale


def total_over(value, axis):
    n = lax.axis_size(axis)
    if n & (n - 1):
        return lax.psum(value, axis)
    step = 1
    while step < n:
        value = value + lax.ppermute(value, axis, [(i, i ^ step) for i in range(n)])
        step *= 2
    return value


def body(potential, probe, amplitudes, row_offset, col_offset, counts):
    slices, _, rows, size = potential.shape
    modes = probe.shape[1]
    part = probe.shape[2]
    slots = row_offset.shape[-1]
    pieces = lax.axis_size("pos")
    cut = slices // 2
    groups = (tuple(range(cut)), tuple(range(cut, slices)))
    f32 = jnp.float32
    me = lax.axis_index("pos").astype(jnp.int32).reshape(1)
    to_right = [(i, i + 1) for i in range(pieces - 1)]
    to_left = [(i + 1, i) for i in range(pieces - 1)]

    def turned(value, k):
        return lax.ppermute(value, "pos", [((i + k) % pieces, i) for i in range(pieces)])

    mine = jnp.concatenate([row_offset.reshape(-1), col_offset.reshape(-1), counts.reshape(-1)])
    prev = lax.ppermute(mine, "pos", to_right)
    parts = [probe] + [turned(probe, k) for k in range(1, pieces)]
    packed = pl.pallas_call(
        functools.partial(pack_kernel, groups),
        out_shape=[jax.ShapeDtypeStruct((slots, size, size), f32)]
        + [jax.ShapeDtypeStruct((len(g), rows, size), f32) for g in groups for _ in range(2)],
        in_specs=[VMEM] * 2,
        out_specs=[VMEM] * (1 + 2 * len(groups)),
        name="pack",
    )(potential, amplitudes[0, 0])
    lows, highs = [], []
    for g in range(len(groups)):
        lows.append(lax.ppermute(packed[1 + 2 * g], "pos", to_left))
        highs.append(lax.ppermute(packed[2 + 2 * g], "pos", to_right))
    amps_prev = lax.ppermute(packed[0], "pos", to_right)

    wave = (2 * slots, modes, size, 2 * size)
    held = [("held", pltpu.SMEM((2 * slots + 1,), jnp.int32))]
    always = [("me", me, True), ("mine", mine, True), ("prev", prev, True), ("tables", jnp.asarray(tables(size)), False)]
    tiles = lambda n, name: [(name, pltpu.VMEM((n, 3, 2, rows, size), f32))]
    modes_ref = [("modes_ref", pltpu.SMEM((modes,), jnp.int32))]
    trans = (2 * slots, 2, size, size)

    first, second = groups
    a = stage(
        always
        + [("own_0", potential, False), ("lows", lows[0], False), ("highs", highs[0], False)]
        + [("piece_%d" % k, parts[k], False) for k in range(pieces)],
        [("psi_0", wave[1:])]
        + [("psi_%d" % (s + 1), wave) for s in first]
        + [("trans_%d" % s, trans) for s in first],
        held + modes_ref + tiles(len(first), "tiles"),
        first,
        False,
        (),
        pieces,
        "ahead",
    )
    b = stage(
        always
        + [("own_0", potential, False), ("lows", lows[1], False), ("highs", highs[1], False)]
        + [("amps", amplitudes[0, 0], False), ("amps_prev", amps_prev, False)]
        + [("psi_%d" % second[0], a["psi_%d" % second[0]], False)],
        [("sums", (1, size)), ("grad_0", (len(second), 2, rows, size))]
        + [("to_left", (len(second), rows, size)), ("to_right", (len(second), rows, size)), ("wave_out", wave)],
        held
        + modes_ref
        + tiles(len(second), "tiles")
        + tiles(len(second), "grads")
        + [("trans_%d" % s, pltpu.VMEM(trans, f32)) for s in second]
        + [("psi_%d" % s, pltpu.VMEM(wave, f32)) for s in second[1:]],
        second,
        True,
        second[::-1],
        pieces,
        "top",
    )
    c = stage(
        always
        + [("wave_in", b["wave_out"], False), ("psi_0", a["psi_0"], False)]
        + [("psi_%d" % s, a["psi_%d" % s], False) for s in first if s > 0]
        + [("trans_%d" % s, a["trans_%d" % s], False) for s in first],
        [("grad_0", (len(first), 2, rows, size))]
        + [("to_left", (len(first), rows, size)), ("to_right", (len(first), rows, size))]
        + [("share_%d" % k, (modes, part, 2 * size)) for k in range(pieces)],
        held + modes_ref + tiles(len(first), "grads") + [("total", pltpu.VMEM(wave[1:], f32))],
        (),
        False,
        first[::-1],
        pieces,
        "back",
    )
    sums = total_over(b["sums"], "group")
    sums = [sums] + [turned(sums, k) for k in range(1, pieces)]
    got_lows = [lax.ppermute(x["to_right"], "pos", to_right) for x in (b, c)]
    got_highs = [lax.ppermute(x["to_left"], "pos", to_left) for x in (b, c)]
    shares = [c["share_0"]] + [turned(c["share_%d" % (pieces - k)], k) for k in range(1, pieces)]
    return pl.pallas_call(
        functools.partial(finish_kernel, (second[::-1], first[::-1]), pieces),
        out_shape=[jax.ShapeDtypeStruct(potential.shape, f32), jax.ShapeDtypeStruct(probe.shape, f32)],
        in_specs=[VMEM] * (6 + 2 * pieces),
        out_specs=[VMEM] * 2,
        name="finish",
    )(b["grad_0"], c["grad_0"], *got_lows, *got_highs, *shares, *sums)


def solution(mesh):
    placed = (
        P(None, None, "group", "pos"),
        P("group", None, "pos", None),
        P("group", "pos", None, None, None),
        P("group", "pos", None),
        P("group", "pos", None),
        P("group", "pos"),
    )
    return jax.shard_map(
        body,
        mesh=mesh,
        in_specs=placed,
        out_specs=(P(None, None, "group", "pos"), P("group", None, "pos", None)),
        check_vma=False,
    )
```

```python
import functools
import math

import jax
import jax.numpy as jnp
import ml_dtypes
import numpy as np
from jax import lax
from jax.experimental import pallas as pl
from jax.experimental.pallas import tpu as pltpu
from jax.sharding import PartitionSpec as P

PROP = 0.25
REG = 0.1
VMEM = pl.BlockSpec(memory_space=pltpu.VMEM)
SMEM = pl.BlockSpec(memory_space=pltpu.SMEM)


@functools.lru_cache(maxsize=None)
def tables(size):
    idx = np.arange(size)
    angle = np.float32(2.0 * math.pi / size) * (idx[:, None] * idx[None, :] % size).astype(np.float32)
    cosv = (np.cos(angle) / np.float32(math.sqrt(size))).astype(ml_dtypes.bfloat16).astype(np.float64)
    sinv = (np.sin(angle) / np.float32(math.sqrt(size))).astype(ml_dtypes.bfloat16).astype(np.float64)
    forward = np.block([[cosv, -sinv], [sinv, cosv]])
    inverse = np.block([[cosv, sinv], [-sinv, cosv]])
    freq = np.where(idx < size // 2, idx, idx - size).astype(np.float64)
    phase = -2.0 * math.pi * PROP / size * freq * freq
    real, imag = np.diag(np.cos(phase)), np.diag(np.sin(phase))
    ahead = forward @ np.block([[real, imag], [-imag, real]]) @ inverse
    behind = forward @ np.block([[real, -imag], [imag, real]]) @ inverse
    return np.stack([forward, inverse, ahead, ahead.T, behind, behind.T]).astype(ml_dtypes.bfloat16)


def mul(a, b):
    return a[0] * b[0] - a[1] * b[1], a[0] * b[1] + a[1] * b[0]


def mulc(a, b):
    return a[0] * b[0] + a[1] * b[1], a[0] * b[1] - a[1] * b[0]


def sine(x):
    y = x * x
    return x * (1.0 - y * (1 / 6) * (1.0 - y * (1 / 20) * (1.0 - y * (1 / 42) * (1.0 - y * (1 / 72)))))


def cosine(x):
    y = x * x
    return 1.0 - y * 0.5 * (1.0 - y * (1 / 12) * (1.0 - y * (1 / 30) * (1.0 - y * (1 / 56) * (1.0 - y * (1 / 90)))))


def transform(waves, right, left):
    size = waves[0][0].shape[0]
    pairs = [waves[first : first + 2] for first in range(0, len(waves), 2)]
    mids = []
    for pair in pairs:
        rows = jnp.concatenate(
            [jnp.concatenate([re.astype(jnp.bfloat16), im.astype(jnp.bfloat16)], 1) for re, im in pair], 0
        )
        mid = jnp.dot(rows, right, preferred_element_type=jnp.float32).astype(jnp.bfloat16)
        cut = [mid[i * size : (i + 1) * size] for i in range(len(pair))]
        mids.append(jnp.concatenate([jnp.concatenate([m[:, :size], m[:, size:]], 0) for m in cut], 1))
    out = []
    for pair, mid in zip(pairs, mids):
        done = jnp.dot(left, mid, preferred_element_type=jnp.float32)
        for i in range(len(pair)):
            out.append((done[:size, i * size : (i + 1) * size], done[size:, i * size : (i + 1) * size]))
    return out


def swap(values, half):
    return pltpu.roll(values, half, values.ndim - 1)


def low_lanes(shape):
    return lax.broadcasted_iota(jnp.int32, shape, len(shape) - 1) < shape[-1] // 2


def pack(pair):
    half = pair[0].shape[-1] // 2
    low = low_lanes(pair[0].shape)
    return jnp.where(low, pair[0], swap(pair[1], half)), jnp.where(low, swap(pair[0], half), pair[1])


def unpack(lows, highs):
    half = lows.shape[-1] // 2
    low = low_lanes(lows.shape)
    return jnp.where(low, lows, swap(highs, half)), jnp.where(low, swap(lows, half), highs)


def pack_kernel(groups, me_ref, row_ref, col_ref, count_ref, potential_ref, amps_ref, *refs):
    slots = row_ref.shape[0]
    even = lax.rem(me_ref[0], 2) == 0
    _, _, rows, size = potential_ref.shape
    for g, group in enumerate(groups):
        first, second = refs[2 * g : 2 * g + 2]
        for j, s in enumerate(group):
            lows, highs = pack((potential_ref[s, 0], potential_ref[s, 1]))
            first[j * rows : (j + 1) * rows] = jnp.where(even, highs, lows)
            second[j * rows : (j + 1) * rows] = jnp.where(even, lows, highs)
        top = len(group) * rows
        if g == 0:
            lane = lax.broadcasted_iota(jnp.int32, (8, size), 1)
            about = jnp.zeros((8, size), jnp.int32)
            for p in range(slots):
                about = jnp.where(lane == p, row_ref[p], jnp.where(lane == slots + p, col_ref[p], about))
            about = jnp.where(lane == 2 * slots, count_ref[0], about).astype(jnp.float32)
            first[top:] = about
            second[top:] = about
        else:
            for p in range(slots):
                amps = amps_ref[p].astype(jnp.float32)
                first[top + p * size : top + (p + 1) * size] = amps
                second[top + p * size : top + (p + 1) * size] = amps


def transmit(phase, absorption):
    magnitude = jnp.exp(-absorption)
    return magnitude * cosine(phase), magnitude * sine(phase)


def prepare_kernel(potential_ref, tables_ref, amps_ref, trans_ref, tables_out, amps_out):
    for s in range(potential_ref.shape[0]):
        trans_ref[s, 0], trans_ref[s, 1] = transmit(potential_ref[s, 0], potential_ref[s, 1])
    tables_out[...] = tables_ref[...]
    amps_out[...] = amps_ref[...]


class Names:
    def __init__(self, names, refs):
        self.__dict__.update(zip(names, refs))

    def get(self, name):
        return self.__dict__[name]


def stage_kernel(names, ahead, top, back, pieces, *refs):
    r = Names(names, refs)
    size = r.tables.shape[-1] // 2
    half = size // 2
    modes = r.modes_ref.shape[0]
    slots = r.rows.shape[0]
    me = r.me[0]
    last = me == pieces - 1
    even = lax.rem(me, 2) == 0
    lanes = lax.broadcasted_iota(jnp.int32, (size, size), 1)

    def halves(i, start, count):
        one, two = r.across_even[start : start + count], r.across_odd[start : start + count]
        return jnp.where(even, one, two), jnp.where(even, two, one)

    if 0 in ahead:
        height = r.own.shape[-2]
        about = halves(0, len(ahead) * height, 8)[1][0:1].astype(jnp.int32)
        lane = lanes[0:1]
        number = jnp.int32(0)
        for k in range(2 * slots):
            p = k % slots
            if k < slots:
                row, col, count = r.rows[p], r.cols[p], r.count[0]
                stays = (col < half) | last
            else:
                row, col, count = [jnp.sum(jnp.where(lane == at, about, 0)) for at in (p, slots + p, 2 * slots)]
                stays = col >= half
            r.held_out[3 * number + 1] = jnp.int32(k)
            r.held_out[3 * number + 2] = row
            r.held_out[3 * number + 3] = col
            number = number + ((p < count) & stays).astype(jnp.int32)
        r.held_out[0] = number
        held = r.held_out
    else:
        held = r.held
    number = held[0]

    for i, s in enumerate(ahead):
        height = r.own.shape[-2]
        halo = transmit(*unpack(*halves(0, i * height, height)))
        for c in range(2):
            r.tiles[i, 0, c] = r.own[s, c]
            r.tiles[i, 1, c] = halo[c]
            r.tiles[i, 2, c] = jnp.full((height, size), 1.0 - c, jnp.float32)
    if 0 in ahead:
        part = r.pieces.shape[-2]
        for k in range(pieces):
            r.psi_0[:, k * part : (k + 1) * part, :] = r.pieces[k]
    if top:
        begin = len(ahead) * r.own.shape[-2]
        for p in range(slots):
            r.amps_all[p] = r.amps[p].astype(jnp.float32)
            r.amps_all[slots + p] = halves(0, begin + p * size, size)[1]
    if back:
        r.grads[...] = jnp.zeros_like(r.grads)
    if 0 in back:
        r.total[...] = jnp.zeros_like(r.total)

    def load(ref, *lead):
        return [(ref[(*lead, m, slice(None), slice(0, size))], ref[(*lead, m, slice(None), slice(size, None))]) for m in range(modes)]

    def store(ref, waves, *lead):
        for m, (re, im) in enumerate(waves):
            ref[(*lead, m, slice(None), slice(0, size))] = re
            ref[(*lead, m, slice(None), slice(size, None))] = im

    def psi(s, at):
        return load(r.psi_0) if s == 0 else load(r.get("psi_%d" % s), at)

    def trans(s, at):
        ref = r.get("trans_%d" % s)
        return ref[at, 0], ref[at, 1]

    def slot_step(at, misfit):
        k = held[3 * at + 1]
        row = held[3 * at + 2]
        col = held[3 * at + 3]
        own = k < slots
        left = jnp.where(own, 0, 1)
        right = jnp.where(own, jnp.where(last, 2, 1), 0)
        turn = lax.rem(size - col, size)
        if ahead:
            waves = psi(ahead[0], at)
        for i, s in enumerate(ahead):
            for c in range(2):
                here = pltpu.roll(r.tiles[i, left, c, pl.ds(row, size), :], turn, 1)
                there = pltpu.roll(r.tiles[i, right, c, pl.ds(row, size), :], turn, 1)
                r.get("trans_%d" % s)[at, c] = jnp.where(lanes < size - col, here, there)
            waves = [mul(trans(s, at), w) for w in waves]
            if top and s == ahead[-1]:
                waves = transform(waves, r.tables[0], r.tables[1])
            else:
                waves = transform(waves, r.tables[2], r.tables[3])
                store(r.get("psi_%d" % (s + 1)), waves, at)
        if top:
            inten = sum(re * re + im * im for re, im in waves)
            model = jnp.sqrt(inten + REG)
            observed = r.amps_all[k]
            diff = model - observed
            misfit = misfit + jnp.sum(diff * diff, axis=0, keepdims=True)
            ratio = 1.0 - observed / model
            waves = transform([(ratio * re, ratio * im) for re, im in waves], r.tables[1], r.tables[0])
        elif back:
            waves = load(r.wave_in, at)
        for i, s in enumerate(back):
            waves = [mulc(trans(s, at), w) for w in waves]
            quot = [mulc(a, w) for a, w in zip(psi(s, at), waves)]
            values = sum(im for _, im in quot), -sum(re for re, _ in quot)
            for c in range(2):
                turned = pltpu.roll(values[c], col, 1)
                inside = lanes >= col
                r.grads[i, left, c, pl.ds(row, size), :] += jnp.where(inside, turned, 0.0)
                r.grads[i, right, c, pl.ds(row, size), :] += jnp.where(inside, 0.0, turned)
            if s > 0:
                waves = transform(waves, r.tables[4], r.tables[5])
        if 0 in back:
            for m, (re, im) in enumerate(waves):
                r.total[m, :, :size] += re
                r.total[m, :, size:] += im
        elif back:
            store(r.wave_out, waves, at)
        return misfit

    misfit = lax.fori_loop(0, number, slot_step, jnp.zeros((1, size), jnp.float32))
    if top:
        value = jnp.sum(misfit, axis=1, keepdims=True)
        lane = lax.broadcasted_iota(jnp.int32, (1, 1, size), 2)
        count = r.count[0].astype(jnp.float32)
        value = jnp.where(lane == 0, value[None], jnp.where(lane == 1, count, 0.0))
        r.sums[...] = jnp.broadcast_to(value, r.sums.shape)
    for i, s in enumerate(back):
        r.grad[i] = r.grads[i, 0]
        lows, highs = pack((r.grads[i, 1, 0], r.grads[i, 1, 1]))
        height = lows.shape[0]
        r.for_even[i * height : (i + 1) * height] = jnp.where(even, lows, highs)
        r.for_odd[i * height : (i + 1) * height] = jnp.where(even, highs, lows)
    if 0 in back:
        part = r.total.shape[1] // pieces
        sums = jnp.sum(r.sums_in[...], axis=0)
        for k in range(pieces):
            for m in range(modes):
                r.share[k, m * part : (m + 1) * part] = r.total[m, k * part : (k + 1) * part, :]
            r.share[k, modes * part :] = jnp.concatenate([sums, sums], 1)


def stage(given, made, scratch, ahead, top, back, pieces, name):
    names = [n for n, _, _ in given] + [n for n, _ in made] + [n for n, _ in scratch]
    out = pl.pallas_call(
        functools.partial(stage_kernel, names, ahead, top, back, pieces),
        out_shape=[jax.ShapeDtypeStruct(shape, jnp.float32) for _, shape in made],
        in_specs=[SMEM if small else VMEM for _, _, small in given],
        out_specs=[VMEM] * len(made),
        scratch_shapes=[x for _, x in scratch],
        compiler_params=pltpu.CompilerParams(vmem_limit_bytes=24 * 2**20),
        cost_estimate=pl.CostEstimate(flops=(len(ahead) + len(back) + 1) * 10**9, bytes_accessed=10**7, transcendentals=0),
        name=name,
    )(*[x for _, x, _ in given])
    return dict(zip([n for n, _ in made], out))


def finish_kernel(back, modes, me_ref, *refs):
    count = len(back)
    grads, evens, odds = refs[:count], refs[count : 2 * count], refs[2 * count : 3 * count]
    share_in, grad_ref, share_ref = refs[3 * count :]
    even = lax.rem(me_ref[0], 2) == 0
    rows, size = grad_ref.shape[2:]
    part = share_ref.shape[2]
    sums = jnp.sum(share_in[:, modes * part :, :], axis=0)[0:1]
    scale = lax.rsqrt(sums[:, 0:1] / (sums[:, 1:2] * (size * size)) + 1e-06)
    for g, group in enumerate(back):
        for i, s in enumerate(group):
            one, two = evens[g][i * rows : (i + 1) * rows], odds[g][i * rows : (i + 1) * rows]
            arrived = unpack(jnp.where(even, two, one), jnp.where(even, one, two))
            for c in range(2):
                grad_ref[s, c] = (grads[g][i, c] + arrived[c]) * scale
    for m in range(modes):
        share_ref[0, m] = jnp.sum(share_in[:, m * part : (m + 1) * part, :], axis=0) * scale


def body(potential, probe, amplitudes, row_offset, col_offset, counts):
    slices, _, rows, size = potential.shape
    modes = probe.shape[1]
    part = probe.shape[2]
    slots = row_offset.shape[-1]
    pieces = lax.axis_size("pos")
    cut = slices // 2
    groups = (tuple(range(cut)), tuple(range(cut, slices)))
    f32 = jnp.float32
    me = lax.axis_index("pos").astype(jnp.int32).reshape(1)
    here = [row_offset[0, 0], col_offset[0, 0], counts[0]]

    def exchange(value, first):
        edges = [(i, i + 1) for i in range(first, pieces - 1, 2)]
        return lax.ppermute(value, "pos", edges + [(j, i) for i, j in edges])

    def call(kernel, given, out, name, scratch=(), flops=0):
        return pl.pallas_call(
            kernel,
            out_shape=[x[0] if isinstance(x, tuple) else x for x in out],
            in_specs=[SMEM if jnp.issubdtype(x.dtype, jnp.integer) else VMEM for x in given],
            out_specs=[SMEM if jnp.issubdtype(x.dtype, jnp.integer) else VMEM for x in out],
            scratch_shapes=list(scratch),
            compiler_params=pltpu.CompilerParams(vmem_limit_bytes=24 * 2**20),
            cost_estimate=pl.CostEstimate(flops=flops, bytes_accessed=10**6, transcendentals=0),
            name=name,
        )(*given)

    def array(shape, dtype=f32):
        return jax.ShapeDtypeStruct(shape, dtype)

    def stage(given, made, scratch, ahead, top, back, name):
        given = dict(me=me, rows=here[0], cols=here[1], count=here[2], tables=tables_here, **given)
        scratch = dict(modes_ref=pltpu.SMEM((modes,), jnp.int32), **scratch)
        names = list(given) + list(made) + list(scratch)
        kernel = functools.partial(stage_kernel, names, ahead, top, back, pieces)
        flops = (len(ahead) + len(back) + 1) * 2 * 10**9
        return dict(zip(made, call(kernel, list(given.values()), list(made.values()), name, scratch.values(), flops)))

    gathered = lax.all_to_all(jnp.broadcast_to(probe, (pieces,) + probe.shape[1:]), "pos", 0, 0)
    heights = [len(groups[0]) * rows + 8, len(groups[1]) * rows + slots * size]
    packed = call(
        functools.partial(pack_kernel, groups),
        [me, *here, potential, amplitudes[0, 0]],
        [array((heights[i // 2], size)) for i in range(4)],
        "pack",
    )
    came = [exchange(packed[i], i % 2) for i in range(4)]
    trans_own, tables_here, amps = call(
        prepare_kernel,
        [potential, jnp.asarray(tables(size)), amplitudes[0, 0]],
        [array(potential.shape), array((6, 2 * size, 2 * size), jnp.bfloat16), array((slots, size, size), jnp.bfloat16)],
        "prepare",
        flops=10**9,
    )

    wave = (2 * slots, modes, size, 2 * size)
    trans = (2 * slots, 2, size, size)
    tiles = lambda n: pltpu.VMEM((n, 3, 2, rows, size), f32)
    sides = lambda n: dict(grad=array((n, 2, rows, size)), for_even=array((n * rows, size)), for_odd=array((n * rows, size)))

    first, second = groups
    a = stage(
        dict(own=trans_own, across_even=came[0], across_odd=came[1], pieces=gathered),
        dict(held_out=array((6 * slots + 4,), jnp.int32), psi_0=array(wave[1:]))
        | {"psi_%d" % (s + 1): array(wave) for s in first}
        | {"trans_%d" % s: array(trans) for s in first},
        dict(tiles=tiles(len(first))),
        first,
        False,
        (),
        "ahead",
    )
    held = a["held_out"]
    back = [second[::-1], first[:0:-1], first[:1]]
    b = stage(
        dict(own=trans_own, across_even=came[2], across_odd=came[3], amps=amps, held=held)
        | {"psi_%d" % second[0]: a["psi_%d" % second[0]]},
        dict(sums=array((lax.axis_size("group"), 8, size)), wave_out=array(wave)) | sides(len(second)),
        dict(tiles=tiles(len(second)), grads=tiles(len(second)), amps_all=pltpu.VMEM((2 * slots, size, size), f32))
        | {"trans_%d" % s: pltpu.VMEM(trans, f32) for s in second}
        | {"psi_%d" % s: pltpu.VMEM(wave, f32) for s in second[1:]},
        second,
        True,
        back[0],
        "top",
    )
    sums = lax.all_to_all(b["sums"], "group", 0, 0)
    c = stage(
        dict(held=held, wave_in=b["wave_out"])
        | {"psi_%d" % s: a["psi_%d" % s] for s in back[1]}
        | {"trans_%d" % s: a["trans_%d" % s] for s in back[1]},
        dict(wave_out=array(wave)) | sides(len(back[1])),
        dict(grads=tiles(len(back[1]))),
        (),
        False,
        back[1],
        "middle",
    )
    d = stage(
        dict(held=held, wave_in=c["wave_out"], psi_0=a["psi_0"], trans_0=a["trans_0"], sums_in=sums),
        dict(share=array((pieces, modes * part + 8, 2 * size))) | sides(1),
        dict(grads=tiles(1), total=pltpu.VMEM(wave[1:], f32)),
        (),
        False,
        back[2],
        "back",
    )
    join = lambda name: jnp.concatenate([x[name] for x in (b, c, d)], 0)
    got = [exchange(join("for_even"), 0), exchange(join("for_odd"), 1)]
    shares = lax.all_to_all(d["share"], "pos", 0, 0)
    return call(
        functools.partial(finish_kernel, (back[0] + back[1] + back[2],), modes),
        [me, join("grad"), *got, shares],
        [array(potential.shape), array(probe.shape)],
        "finish",
    )


def solution(mesh):
    placed = (
        P(None, None, "group", "pos"),
        P("group", None, "pos", None),
        P("group", "pos", None, None, None),
        P("group", "pos", None),
        P("group", "pos", None),
        P("group", "pos"),
    )
    return jax.shard_map(
        body,
        mesh=mesh,
        in_specs=placed,
        out_specs=(P(None, None, "group", "pos"), P("group", None, "pos", None)),
        check_vma=False,
    )
```

```python
import functools
import math

import jax
import jax.numpy as jnp
import ml_dtypes
import numpy as np
from jax import lax
from jax.experimental import pallas as pl
from jax.experimental.pallas import tpu as pltpu
from jax.sharding import PartitionSpec as P

PROP = 0.25
REG = 0.1
VMEM = pl.BlockSpec(memory_space=pltpu.VMEM)
SMEM = pl.BlockSpec(memory_space=pltpu.SMEM)


@functools.lru_cache(maxsize=None)
def tables(size):
    idx = np.arange(size)
    angle = np.float32(2.0 * math.pi / size) * (idx[:, None] * idx[None, :] % size).astype(np.float32)
    cosv = (np.cos(angle) / np.float32(math.sqrt(size))).astype(ml_dtypes.bfloat16).astype(np.float64)
    sinv = (np.sin(angle) / np.float32(math.sqrt(size))).astype(ml_dtypes.bfloat16).astype(np.float64)
    forward = np.block([[cosv, -sinv], [sinv, cosv]])
    inverse = np.block([[cosv, sinv], [-sinv, cosv]])
    freq = np.where(idx < size // 2, idx, idx - size).astype(np.float64)
    phase = -2.0 * math.pi * PROP / size * freq * freq
    real, imag = np.diag(np.cos(phase)), np.diag(np.sin(phase))
    ahead = forward @ np.block([[real, imag], [-imag, real]]) @ inverse
    behind = forward @ np.block([[real, -imag], [imag, real]]) @ inverse
    return np.stack([forward, inverse, ahead, ahead.T, behind, behind.T]).astype(ml_dtypes.bfloat16)


def mul(a, b):
    return a[0] * b[0] - a[1] * b[1], a[0] * b[1] + a[1] * b[0]


def mulc(a, b):
    return a[0] * b[0] + a[1] * b[1], a[0] * b[1] - a[1] * b[0]


def sine(x):
    y = x * x
    return x * (1.0 - y * (1 / 6) * (1.0 - y * (1 / 20) * (1.0 - y * (1 / 42) * (1.0 - y * (1 / 72)))))


def cosine(x):
    y = x * x
    return 1.0 - y * 0.5 * (1.0 - y * (1 / 12) * (1.0 - y * (1 / 30) * (1.0 - y * (1 / 56) * (1.0 - y * (1 / 90)))))


def transform(waves, right, left):
    size = waves[0][0].shape[0]
    pairs = [waves[first : first + 2] for first in range(0, len(waves), 2)]
    mids = []
    for pair in pairs:
        rows = jnp.concatenate(
            [jnp.concatenate([re.astype(jnp.bfloat16), im.astype(jnp.bfloat16)], 1) for re, im in pair], 0
        )
        mid = jnp.dot(rows, right, preferred_element_type=jnp.float32).astype(jnp.bfloat16)
        cut = [mid[i * size : (i + 1) * size] for i in range(len(pair))]
        mids.append(jnp.concatenate([jnp.concatenate([m[:, :size], m[:, size:]], 0) for m in cut], 1))
    out = []
    for pair, mid in zip(pairs, mids):
        done = jnp.dot(left, mid, preferred_element_type=jnp.float32)
        for i in range(len(pair)):
            out.append((done[:size, i * size : (i + 1) * size], done[size:, i * size : (i + 1) * size]))
    return out


def swap(values, half):
    return pltpu.roll(values, half, values.ndim - 1)


def low_lanes(shape):
    return lax.broadcasted_iota(jnp.int32, shape, len(shape) - 1) < shape[-1] // 2


def pack(pair):
    half = pair[0].shape[-1] // 2
    low = low_lanes(pair[0].shape)
    return jnp.where(low, pair[0], swap(pair[1], half)), jnp.where(low, swap(pair[0], half), pair[1])


def unpack(lows, highs):
    half = lows.shape[-1] // 2
    low = low_lanes(lows.shape)
    return jnp.where(low, lows, swap(highs, half)), jnp.where(low, swap(lows, half), highs)


def pack_kernel(groups, me_ref, row_ref, col_ref, count_ref, potential_ref, amps_ref, *refs):
    slots = row_ref.shape[0]
    even = lax.rem(me_ref[0], 2) == 0
    _, _, rows, size = potential_ref.shape
    for g, group in enumerate(groups):
        first, second = refs[2 * g : 2 * g + 2]
        for j, s in enumerate(group):
            lows, highs = pack((potential_ref[s, 0], potential_ref[s, 1]))
            first[j * rows : (j + 1) * rows] = jnp.where(even, highs, lows)
            second[j * rows : (j + 1) * rows] = jnp.where(even, lows, highs)
        top = len(group) * rows
        if g == 0:
            lane = lax.broadcasted_iota(jnp.int32, (8, size), 1)
            about = jnp.zeros((8, size), jnp.int32)
            for p in range(slots):
                about = jnp.where(lane == p, row_ref[p], jnp.where(lane == slots + p, col_ref[p], about))
            about = jnp.where(lane == 2 * slots, count_ref[0], about).astype(jnp.float32)
            first[top:] = about
            second[top:] = about
        else:
            for p in range(slots):
                amps = amps_ref[p].astype(jnp.float32)
                first[top + p * size : top + (p + 1) * size] = amps
                second[top + p * size : top + (p + 1) * size] = amps


def transmit(phase, absorption):
    magnitude = jnp.exp(-absorption)
    return magnitude * cosine(phase), magnitude * sine(phase)


def prepare_kernel(potential_ref, tables_ref, amps_ref, pieces_ref, trans_ref, tables_out, amps_out, probe_ref):
    part = pieces_ref.shape[2]
    for k in range(pieces_ref.shape[0]):
        probe_ref[:, k * part : (k + 1) * part, :] = pieces_ref[k]
    for s in range(potential_ref.shape[0]):
        trans_ref[s, 0], trans_ref[s, 1] = transmit(potential_ref[s, 0], potential_ref[s, 1])
    tables_out[...] = tables_ref[...]
    amps_out[...] = amps_ref[...]


class Names:
    def __init__(self, names, refs):
        self.__dict__.update(zip(names, refs))

    def get(self, name):
        return self.__dict__[name]


def stage_kernel(names, ahead, top, back, pieces, *refs):
    r = Names(names, refs)
    size = r.tables.shape[-1] // 2
    half = size // 2
    modes = r.modes_ref.shape[0]
    slots = r.rows.shape[0]
    me = r.me[0]
    last = me == pieces - 1
    even = lax.rem(me, 2) == 0
    lanes = lax.broadcasted_iota(jnp.int32, (size, size), 1)

    def halves(i, start, count):
        one, two = r.across_even[start : start + count], r.across_odd[start : start + count]
        return jnp.where(even, one, two), jnp.where(even, two, one)

    if 0 in ahead:
        height = r.own.shape[-2]
        about = halves(0, len(ahead) * height, 8)[1][0:1].astype(jnp.int32)
        lane = lanes[0:1]
        number = jnp.int32(0)
        for k in range(2 * slots):
            p = k % slots
            if k < slots:
                row, col, count = r.rows[p], r.cols[p], r.count[0]
                stays = (col < half) | last
            else:
                row, col, count = [jnp.sum(jnp.where(lane == at, about, 0)) for at in (p, slots + p, 2 * slots)]
                stays = col >= half
            r.held_out[3 * number + 1] = jnp.int32(k)
            r.held_out[3 * number + 2] = row
            r.held_out[3 * number + 3] = col
            number = number + ((p < count) & stays).astype(jnp.int32)
        r.held_out[0] = number
        held = r.held_out
    else:
        held = r.held
    number = held[0]

    for i, s in enumerate(ahead):
        height = r.own.shape[-2]
        halo = transmit(*unpack(*halves(0, i * height, height)))
        for c in range(2):
            r.tiles[i, 0, c] = r.own[s, c]
            r.tiles[i, 1, c] = halo[c]
            r.tiles[i, 2, c] = jnp.full((height, size), 1.0 - c, jnp.float32)
    if top:
        begin = len(ahead) * r.own.shape[-2]
        for p in range(slots):
            r.amps_all[p] = r.amps[p].astype(jnp.float32)
            r.amps_all[slots + p] = halves(0, begin + p * size, size)[1]
    if back:
        r.grads[...] = jnp.zeros_like(r.grads)
    if 0 in back:
        r.total[...] = jnp.zeros_like(r.total)

    def load(ref, *lead):
        return [(ref[(*lead, m, slice(None), slice(0, size))], ref[(*lead, m, slice(None), slice(size, None))]) for m in range(modes)]

    def store(ref, waves, *lead):
        for m, (re, im) in enumerate(waves):
            ref[(*lead, m, slice(None), slice(0, size))] = re
            ref[(*lead, m, slice(None), slice(size, None))] = im

    def psi(s, at):
        return load(r.psi_0) if s == 0 else load(r.get("psi_%d" % s), at)

    def trans(s, at):
        ref = r.get("trans_%d" % s)
        return ref[at, 0], ref[at, 1]

    def slot_step(at, misfit):
        k = held[3 * at + 1]
        row = held[3 * at + 2]
        col = held[3 * at + 3]
        own = k < slots
        left = jnp.where(own, 0, 1)
        right = jnp.where(own, jnp.where(last, 2, 1), 0)
        turn = lax.rem(size - col, size)
        if ahead:
            waves = psi(ahead[0], at)
        for i, s in enumerate(ahead):
            for c in range(2):
                here = pltpu.roll(r.tiles[i, left, c, pl.ds(row, size), :], turn, 1)
                there = pltpu.roll(r.tiles[i, right, c, pl.ds(row, size), :], turn, 1)
                r.get("trans_%d" % s)[at, c] = jnp.where(lanes < size - col, here, there)
            waves = [mul(trans(s, at), w) for w in waves]
            if top and s == ahead[-1]:
                waves = transform(waves, r.tables[0], r.tables[1])
            else:
                waves = transform(waves, r.tables[2], r.tables[3])
                store(r.get("psi_%d" % (s + 1)), waves, at)
        if top:
            inten = sum(re * re + im * im for re, im in waves)
            model = jnp.sqrt(inten + REG)
            observed = r.amps_all[k]
            diff = model - observed
            misfit = misfit + jnp.sum(diff * diff, axis=0, keepdims=True)
            ratio = 1.0 - observed / model
            waves = transform([(ratio * re, ratio * im) for re, im in waves], r.tables[1], r.tables[0])
        elif back:
            waves = load(r.wave_in, at)
        for i, s in enumerate(back):
            waves = [mulc(trans(s, at), w) for w in waves]
            quot = [mulc(a, w) for a, w in zip(psi(s, at), waves)]
            values = sum(im for _, im in quot), -sum(re for re, _ in quot)
            for c in range(2):
                turned = pltpu.roll(values[c], col, 1)
                inside = lanes >= col
                r.grads[i, left, c, pl.ds(row, size), :] += jnp.where(inside, turned, 0.0)
                r.grads[i, right, c, pl.ds(row, size), :] += jnp.where(inside, 0.0, turned)
            if s > 0:
                waves = transform(waves, r.tables[4], r.tables[5])
        if 0 in back:
            for m, (re, im) in enumerate(waves):
                r.total[m, :, :size] += re
                r.total[m, :, size:] += im
        elif back or top:
            store(r.wave_out, waves, at)
        return misfit

    misfit = lax.fori_loop(0, number, slot_step, jnp.zeros((1, size), jnp.float32))
    if top:
        value = jnp.sum(misfit, axis=1, keepdims=True)
        lane = lax.broadcasted_iota(jnp.int32, (1, 1, size), 2)
        count = r.count[0].astype(jnp.float32)
        value = jnp.where(lane == 0, value[None], jnp.where(lane == 1, count, 0.0))
        r.sums[...] = jnp.broadcast_to(value[0], r.sums.shape)
    for i, s in enumerate(back):
        r.grad[i] = r.grads[i, 0]
        lows, highs = pack((r.grads[i, 1, 0], r.grads[i, 1, 1]))
        height = lows.shape[0]
        r.for_even[i * height : (i + 1) * height] = jnp.where(even, lows, highs)
        r.for_odd[i * height : (i + 1) * height] = jnp.where(even, highs, lows)
    if 0 in back:
        part = r.total.shape[1] // pieces
        sums = r.sums_in[...]
        for k in range(pieces):
            for m in range(modes):
                r.share[k, m * part : (m + 1) * part] = r.total[m, k * part : (k + 1) * part, :]
            r.share[k, modes * part :] = jnp.concatenate([sums, sums], 1)


def stage(given, made, scratch, ahead, top, back, pieces, name):
    names = [n for n, _, _ in given] + [n for n, _ in made] + [n for n, _ in scratch]
    out = pl.pallas_call(
        functools.partial(stage_kernel, names, ahead, top, back, pieces),
        out_shape=[jax.ShapeDtypeStruct(shape, jnp.float32) for _, shape in made],
        in_specs=[SMEM if small else VMEM for _, _, small in given],
        out_specs=[VMEM] * len(made),
        scratch_shapes=[x for _, x in scratch],
        compiler_params=pltpu.CompilerParams(vmem_limit_bytes=24 * 2**20),
        cost_estimate=pl.CostEstimate(flops=(len(ahead) + len(back) + 1) * 10**9, bytes_accessed=10**7, transcendentals=0),
        name=name,
    )(*[x for _, x, _ in given])
    return dict(zip([n for n, _ in made], out))


def finish_kernel(back, modes, me_ref, *refs):
    count = len(back)
    grads, evens, odds = refs[:count], refs[count : 2 * count], refs[2 * count : 3 * count]
    share_in, grad_ref, share_ref = refs[3 * count :]
    even = lax.rem(me_ref[0], 2) == 0
    rows, size = grad_ref.shape[2:]
    part = share_ref.shape[2]
    sums = jnp.sum(share_in[:, modes * part :, :], axis=0)[0:1]
    scale = lax.rsqrt(sums[:, 0:1] / (sums[:, 1:2] * (size * size)) + 1e-06)
    for g, group in enumerate(back):
        for i, s in enumerate(group):
            one, two = evens[g][i * rows : (i + 1) * rows], odds[g][i * rows : (i + 1) * rows]
            arrived = unpack(jnp.where(even, two, one), jnp.where(even, one, two))
            for c in range(2):
                grad_ref[s, c] = (grads[g][i, c] + arrived[c]) * scale
    for m in range(modes):
        share_ref[0, m] = jnp.sum(share_in[:, m * part : (m + 1) * part, :], axis=0) * scale


def total_over(value, axis):
    n = lax.axis_size(axis)
    if n & (n - 1):
        return lax.psum(value, axis)
    step = 1
    while step < n:
        value = value + lax.ppermute(value, axis, [(i, i ^ step) for i in range(n)])
        step *= 2
    return value


def body(potential, probe, amplitudes, row_offset, col_offset, counts):
    slices, _, rows, size = potential.shape
    modes = probe.shape[1]
    part = probe.shape[2]
    slots = row_offset.shape[-1]
    pieces = lax.axis_size("pos")
    cut = slices // 2
    groups = (tuple(range(cut)), tuple(range(cut, slices)))
    f32 = jnp.float32
    me = lax.axis_index("pos").astype(jnp.int32).reshape(1)
    here = [row_offset[0, 0], col_offset[0, 0], counts[0]]

    def exchange(value, first):
        edges = [(i, i + 1) for i in range(first, pieces - 1, 2)]
        return lax.ppermute(value, "pos", edges + [(j, i) for i, j in edges])

    def call(kernel, given, out, name, scratch=(), flops=0):
        return pl.pallas_call(
            kernel,
            out_shape=[x[0] if isinstance(x, tuple) else x for x in out],
            in_specs=[SMEM if jnp.issubdtype(x.dtype, jnp.integer) else VMEM for x in given],
            out_specs=[SMEM if jnp.issubdtype(x.dtype, jnp.integer) else VMEM for x in out],
            scratch_shapes=list(scratch),
            compiler_params=pltpu.CompilerParams(vmem_limit_bytes=24 * 2**20),
            cost_estimate=pl.CostEstimate(flops=flops, bytes_accessed=10**6, transcendentals=0),
            name=name,
        )(*given)

    def array(shape, dtype=f32):
        return jax.ShapeDtypeStruct(shape, dtype)

    def stage(given, made, scratch, ahead, top, back, name):
        given = dict(me=me, rows=here[0], cols=here[1], count=here[2], tables=tables_here, **given)
        scratch = dict(modes_ref=pltpu.SMEM((modes,), jnp.int32), **scratch)
        names = list(given) + list(made) + list(scratch)
        kernel = functools.partial(stage_kernel, names, ahead, top, back, pieces)
        flops = (len(ahead) + len(back) + 1) * 2 * 10**9
        return dict(zip(made, call(kernel, list(given.values()), list(made.values()), name, scratch.values(), flops)))

    gathered = lax.all_to_all(jnp.broadcast_to(probe, (pieces,) + probe.shape[1:]), "pos", 0, 0)
    heights = [len(groups[0]) * rows + 8, len(groups[1]) * rows + slots * size]
    packed = call(
        functools.partial(pack_kernel, groups),
        [me, *here, potential, amplitudes[0, 0]],
        [array((heights[i // 2], size)) for i in range(4)],
        "pack",
    )
    came = [exchange(packed[i], i % 2) for i in range(4)]
    trans_own, tables_here, amps, probe_all = call(
        prepare_kernel,
        [potential, jnp.asarray(tables(size)), amplitudes[0, 0], gathered],
        [
            array(potential.shape),
            array((6, 2 * size, 2 * size), jnp.bfloat16),
            array((slots, size, size), jnp.bfloat16),
            array((modes, size, 2 * size)),
        ],
        "prepare",
        flops=10**9,
    )

    wave = (2 * slots, modes, size, 2 * size)
    trans = (2 * slots, 2, size, size)
    tiles = lambda n: pltpu.VMEM((n, 3, 2, rows, size), f32)
    sides = lambda n: dict(grad=array((n, 2, rows, size)), for_even=array((n * rows, size)), for_odd=array((n * rows, size)))

    first, second = groups
    a = stage(
        dict(own=trans_own, across_even=came[0], across_odd=came[1], psi_0=probe_all),
        dict(held_out=array((6 * slots + 4,), jnp.int32))
        | {"psi_%d" % (s + 1): array(wave) for s in first}
        | {"trans_%d" % s: array(trans) for s in first},
        dict(tiles=tiles(len(first))),
        first,
        False,
        (),
        "ahead",
    )
    held = a["held_out"]
    b = stage(
        dict(own=trans_own, across_even=came[2], across_odd=came[3], amps=amps, held=held)
        | {"psi_%d" % second[0]: a["psi_%d" % second[0]]},
        dict(sums=array((8, size)), wave_out=array(wave))
        | {"psi_%d" % s: array(wave) for s in second[1:]}
        | {"trans_%d" % s: array(trans) for s in second},
        dict(tiles=tiles(len(second)), amps_all=pltpu.VMEM((2 * slots, size, size), f32)),
        second,
        True,
        (),
        "top",
    )
    sums = total_over(b["sums"], "group")
    state = a | b | dict(psi_0=probe_all)
    done = []
    back = [(slices - 1,), tuple(range(slices - 2, 0, -1)), (0,)]
    for group in back:
        end = 0 in group
        made = dict(share=array((pieces, modes * part + 8, 2 * size))) if end else dict(wave_out=array(wave))
        scratch = dict(total=pltpu.VMEM(wave[1:], f32)) if end else {}
        d = stage(
            dict(held=held, wave_in=state["wave_out"])
            | {"psi_%d" % s: state["psi_%d" % s] for s in group}
            | {"trans_%d" % s: state["trans_%d" % s] for s in group}
            | (dict(sums_in=sums) if end else {}),
            made | sides(len(group)),
            dict(grads=tiles(len(group))) | scratch,
            (),
            False,
            group,
            "back",
        )
        state = state | d
        done.append(d)
    join = lambda name: jnp.concatenate([x[name] for x in done], 0)
    got = [exchange(join("for_even"), 0), exchange(join("for_odd"), 1)]
    shares = lax.all_to_all(d["share"], "pos", 0, 0)
    return call(
        functools.partial(finish_kernel, (sum(back, ()),), modes),
        [me, join("grad"), *got, shares],
        [array(potential.shape), array(probe.shape)],
        "finish",
    )


def solution(mesh):
    placed = (
        P(None, None, "group", "pos"),
        P("group", None, "pos", None),
        P("group", "pos", None, None, None),
        P("group", "pos", None),
        P("group", "pos", None),
        P("group", "pos"),
    )
    return jax.shard_map(
        body,
        mesh=mesh,
        in_specs=placed,
        out_specs=(P(None, None, "group", "pos"), P("group", None, "pos", None)),
        check_vma=False,
    )
```

```python
import functools
import math

import jax
import jax.numpy as jnp
import ml_dtypes
import numpy as np
from jax import lax
from jax.experimental import pallas as pl
from jax.experimental.pallas import tpu as pltpu
from jax.sharding import PartitionSpec as P

PROP = 0.25
REG = 0.1
VMEM = pl.BlockSpec(memory_space=pltpu.VMEM)
SMEM = pl.BlockSpec(memory_space=pltpu.SMEM)


@functools.lru_cache(maxsize=None)
def tables(size):
    idx = np.arange(size)
    angle = np.float32(2.0 * math.pi / size) * (idx[:, None] * idx[None, :] % size).astype(np.float32)
    cosv = (np.cos(angle) / np.float32(math.sqrt(size))).astype(ml_dtypes.bfloat16).astype(np.float64)
    sinv = (np.sin(angle) / np.float32(math.sqrt(size))).astype(ml_dtypes.bfloat16).astype(np.float64)
    forward = np.block([[cosv, -sinv], [sinv, cosv]])
    inverse = np.block([[cosv, sinv], [-sinv, cosv]])
    freq = np.where(idx < size // 2, idx, idx - size).astype(np.float64)
    phase = -2.0 * math.pi * PROP / size * freq * freq
    real, imag = np.diag(np.cos(phase)), np.diag(np.sin(phase))
    ahead = forward @ np.block([[real, imag], [-imag, real]]) @ inverse
    behind = forward @ np.block([[real, -imag], [imag, real]]) @ inverse
    return np.stack([forward, inverse, ahead, ahead.T, behind, behind.T]).astype(ml_dtypes.bfloat16)


def mul(a, b):
    return a[0] * b[0] - a[1] * b[1], a[0] * b[1] + a[1] * b[0]


def mulc(a, b):
    return a[0] * b[0] + a[1] * b[1], a[0] * b[1] - a[1] * b[0]


def sine(x):
    y = x * x
    return x * (1.0 - y * (1 / 6) * (1.0 - y * (1 / 20) * (1.0 - y * (1 / 42) * (1.0 - y * (1 / 72)))))


def cosine(x):
    y = x * x
    return 1.0 - y * 0.5 * (1.0 - y * (1 / 12) * (1.0 - y * (1 / 30) * (1.0 - y * (1 / 56) * (1.0 - y * (1 / 90)))))


def transform(waves, right, left):
    size = waves[0][0].shape[0]
    pairs = [waves[first : first + 2] for first in range(0, len(waves), 2)]
    mids = []
    for pair in pairs:
        rows = jnp.concatenate(
            [jnp.concatenate([re.astype(jnp.bfloat16), im.astype(jnp.bfloat16)], 1) for re, im in pair], 0
        )
        mid = jnp.dot(rows, right, preferred_element_type=jnp.float32).astype(jnp.bfloat16)
        cut = [mid[i * size : (i + 1) * size] for i in range(len(pair))]
        mids.append(jnp.concatenate([jnp.concatenate([m[:, :size], m[:, size:]], 0) for m in cut], 1))
    out = []
    for pair, mid in zip(pairs, mids):
        done = jnp.dot(left, mid, preferred_element_type=jnp.float32)
        for i in range(len(pair)):
            out.append((done[:size, i * size : (i + 1) * size], done[size:, i * size : (i + 1) * size]))
    return out


def swap(values, half):
    return pltpu.roll(values, half, values.ndim - 1)


def low_lanes(shape):
    return lax.broadcasted_iota(jnp.int32, shape, len(shape) - 1) < shape[-1] // 2


def pack(pair):
    half = pair[0].shape[-1] // 2
    low = low_lanes(pair[0].shape)
    return jnp.where(low, pair[0], swap(pair[1], half)), jnp.where(low, swap(pair[0], half), pair[1])


def unpack(lows, highs):
    half = lows.shape[-1] // 2
    low = low_lanes(lows.shape)
    return jnp.where(low, lows, swap(highs, half)), jnp.where(low, swap(lows, half), highs)


def fetch(pairs, sems):
    copies = [pltpu.make_async_copy(source, target, sems.at[i]) for i, (source, target) in enumerate(pairs)]
    for copy in copies:
        copy.start()
    for copy in copies:
        copy.wait()


def pack_kernel(groups, slots, me_ref, rows_in, cols_in, count_in, potential_in, amps_in, earlier, *refs):
    rows_ref, cols_ref, count_ref, potential_ref, amps_ref, sems = refs[2 * len(groups) :]
    fetch(
        [
            (potential_in, potential_ref),
            (amps_in, amps_ref),
            (rows_in, rows_ref),
            (cols_in, cols_ref),
            (count_in, count_ref),
        ],
        sems,
    )
    even = lax.rem(me_ref[0], 2) == 0
    _, _, rows, size = potential_ref.shape
    for g, group in enumerate(groups):
        first, second = refs[2 * g : 2 * g + 2]
        for j, s in enumerate(group):
            lows, highs = pack((potential_ref[s, 0], potential_ref[s, 1]))
            first[j * rows : (j + 1) * rows] = jnp.where(even, highs, lows)
            second[j * rows : (j + 1) * rows] = jnp.where(even, lows, highs)
        top = len(group) * rows
        if g == 0:
            lane = lax.broadcasted_iota(jnp.int32, (8, size), 1)
            about = jnp.zeros((8, size), jnp.int32)
            for p in range(slots):
                about = jnp.where(lane == p, rows_ref[0, 0, p], jnp.where(lane == slots + p, cols_ref[0, 0, p], about))
            about = jnp.where(lane == 2 * slots, count_ref[0, 0], about).astype(jnp.float32)
            first[top:] = about
            second[top:] = about
        else:
            for p in range(slots):
                amps = amps_ref[0, 0, p].astype(jnp.float32)
                first[top + p * size : top + (p + 1) * size] = amps
                second[top + p * size : top + (p + 1) * size] = amps


def transmit(phase, absorption):
    magnitude = jnp.exp(-absorption)
    return magnitude * cosine(phase), magnitude * sine(phase)


def prepare_kernel(potential_in, tables_in, amps_in, trans_ref, tables_ref, amps_ref, potential_ref, sems):
    fetch([(potential_in, potential_ref), (tables_in, tables_ref), (amps_in, amps_ref)], sems)
    for s in range(potential_ref.shape[0]):
        trans_ref[s, 0], trans_ref[s, 1] = transmit(potential_ref[s, 0], potential_ref[s, 1])


class Names:
    def __init__(self, names, refs):
        self.__dict__.update(zip(names, refs))

    def get(self, name):
        return self.__dict__[name]


def stage_kernel(names, ahead, top, back, pieces, *refs):
    r = Names(names, refs)
    size = r.tables.shape[-1] // 2
    half = size // 2
    modes = r.modes_ref.shape[0]
    slots = (r.held.shape[0] - 8) // 10 if 0 not in ahead else r.rows.shape[-1]
    held = r.held if 0 not in ahead else r.held_out
    if 0 in ahead:
        me = r.me[0]
        last = me == pieces - 1
        even = lax.rem(me, 2) == 0
    else:
        even = held[1] == 1
    lanes = lax.broadcasted_iota(jnp.int32, (size, size), 1)

    def halves(i, start, count):
        one, two = r.across_even[start : start + count], r.across_odd[start : start + count]
        return jnp.where(even, one, two), jnp.where(even, two, one)

    if 0 in ahead:
        height = r.own.shape[-2]
        about = halves(0, len(ahead) * height, 8)[1][0:1].astype(jnp.int32)
        lane = lanes[0:1]
        number = jnp.int32(0)
        for k in range(2 * slots):
            p = k % slots
            if k < slots:
                row, col, count = r.rows[0, 0, p], r.cols[0, 0, p], r.count[0, 0]
                stays = (col < half) | last
                left, right = jnp.int32(0), jnp.where(last, 2, 1)
            else:
                row, col, count = [jnp.sum(jnp.where(lane == at, about, 0)) for at in (p, slots + p, 2 * slots)]
                stays = col >= half
                left, right = jnp.int32(1), jnp.int32(0)
            for j, value in enumerate((jnp.int32(k), row, col, left, right)):
                held[5 * number + 3 + j] = value
            number = number + ((p < count) & stays).astype(jnp.int32)
        held[0] = number
        held[1] = even.astype(jnp.int32)
        held[2] = r.count[0, 0]
        part = r.piece_0.shape[-2]
        for k in range(pieces):
            place = pl.multiple_of(lax.rem(me + k, pieces) * part, part)
            r.psi_0[:, pl.ds(place, part), :] = r.get("piece_%d" % k)[0]
    number = held[0]

    for i, s in enumerate(ahead):
        height = r.own.shape[-2]
        halo = transmit(*unpack(*halves(0, i * height, height)))
        for c in range(2):
            r.tiles[i, 0, c] = r.own[s, c]
            r.tiles[i, 1, c] = halo[c]
            r.tiles[i, 2, c] = jnp.full((height, size), 1.0 - c, jnp.float32)
    if top:
        begin = len(ahead) * r.own.shape[-2]
        for p in range(slots):
            r.amps_all[p] = r.amps[p].astype(jnp.float32)
            r.amps_all[slots + p] = halves(0, begin + p * size, size)[1]
    if back:
        r.grads[...] = jnp.zeros_like(r.grads)
    if 0 in back:
        r.total[...] = jnp.zeros_like(r.total)

    def load(ref, *lead):
        return [(ref[(*lead, m, slice(None), slice(0, size))], ref[(*lead, m, slice(None), slice(size, None))]) for m in range(modes)]

    def store(ref, waves, *lead):
        for m, (re, im) in enumerate(waves):
            ref[(*lead, m, slice(None), slice(0, size))] = re
            ref[(*lead, m, slice(None), slice(size, None))] = im

    def psi(s, at):
        return load(r.psi_0) if s == 0 else load(r.get("psi_%d" % s), at)

    def trans(s, at):
        ref = r.get("trans_%d" % s)
        return ref[at, 0], ref[at, 1]

    def slot_step(at, misfit):
        k, row, col, left, right = [held[5 * at + 3 + j] for j in range(5)]
        inside = lanes >= col
        turn = lax.rem(size - col, size)
        if ahead:
            waves = psi(ahead[0], at)
        for i, s in enumerate(ahead):
            for c in range(2):
                both = jnp.where(inside, r.tiles[i, left, c, pl.ds(row, size), :], r.tiles[i, right, c, pl.ds(row, size), :])
                r.get("trans_%d" % s)[at, c] = pltpu.roll(both, turn, 1)
            waves = [mul(trans(s, at), w) for w in waves]
            if top and s == ahead[-1]:
                waves = transform(waves, r.tables[0], r.tables[1])
            else:
                waves = transform(waves, r.tables[2], r.tables[3])
                store(r.get("psi_%d" % (s + 1)), waves, at)
        if top:
            inten = sum(re * re + im * im for re, im in waves)
            model = jnp.sqrt(inten + REG)
            observed = r.amps_all[k]
            diff = model - observed
            misfit = misfit + jnp.sum(diff * diff, axis=0, keepdims=True)
            ratio = 1.0 - observed / model
            waves = transform([(ratio * re, ratio * im) for re, im in waves], r.tables[1], r.tables[0])
        elif back:
            waves = load(r.wave_in, at)
        for i, s in enumerate(back):
            waves = [mulc(trans(s, at), w) for w in waves]
            quot = [mulc(a, w) for a, w in zip(psi(s, at), waves)]
            values = sum(im for _, im in quot), -sum(re for re, _ in quot)
            for c in range(2):
                turned = pltpu.roll(values[c], col, 1)
                r.grads[i, left, c, pl.ds(row, size), :] += jnp.where(inside, turned, 0.0)
                r.grads[i, right, c, pl.ds(row, size), :] += jnp.where(inside, 0.0, turned)
            if s > 0:
                waves = transform(waves, r.tables[4], r.tables[5])
        if 0 in back:
            for m, (re, im) in enumerate(waves):
                r.total[m, :, :size] += re
                r.total[m, :, size:] += im
        elif back or top:
            store(r.wave_out, waves, at)
        return misfit

    misfit = lax.fori_loop(0, number, slot_step, jnp.zeros((1, size), jnp.float32))
    if top:
        value = jnp.sum(misfit, axis=1, keepdims=True)
        lane = lax.broadcasted_iota(jnp.int32, (1, 1, size), 2)
        count = held[2].astype(jnp.float32)
        value = jnp.where(lane == 0, value[None], jnp.where(lane == 1, count, 0.0))
        r.sums[...] = jnp.broadcast_to(value[0], r.sums.shape)
    for i, s in enumerate(back):
        r.grad[i] = r.grads[i, 0]
        lows, highs = pack((r.grads[i, 1, 0], r.grads[i, 1, 1]))
        height = lows.shape[0]
        r.for_even[i * height : (i + 1) * height] = jnp.where(even, lows, highs)
        r.for_odd[i * height : (i + 1) * height] = jnp.where(even, highs, lows)


def arrived(even, across_even, across_odd):
    return unpack(jnp.where(even, across_odd, across_even), jnp.where(even, across_even, across_odd))


def assemble_kernel(pieces, parts, held_ref, total_ref, sums_ref, own_ref, even_in, odd_in, *refs):
    sides, (share_ref, done_ref, for_even, for_odd) = refs[: 2 * parts], refs[2 * parts :]
    parts_in = arrived(held_ref[1] == 1, even_in[...], odd_in[...])
    for c in range(2):
        done_ref[c] = own_ref[0, c] + parts_in[c]
    at = 0
    for i in range(parts):
        height = sides[2 * i].shape[0]
        for_even[at : at + height] = sides[2 * i][...]
        for_odd[at : at + height] = sides[2 * i + 1][...]
        at += height
    modes = total_ref.shape[0]
    part = total_ref.shape[1] // pieces
    for k in range(pieces):
        for m in range(modes):
            share_ref[k, m * part : (m + 1) * part] = total_ref[m, k * part : (k + 1) * part, :]
        share_ref[k, modes * part :] = jnp.concatenate([sums_ref[...], sums_ref[...]], 1)


def finish_kernel(back, modes, held_ref, early_ref, *refs):
    count = len(back)
    grads, (even_in, odd_in, share_in, grad_ref, share_ref) = refs[:count], refs[count:]
    even = held_ref[1] == 1
    rows, size = grad_ref.shape[2:]
    part = share_ref.shape[2]
    sums = jnp.sum(share_in[:, modes * part :, :], axis=0)[0:1]
    scale = lax.rsqrt(sums[:, 0:1] / (sums[:, 1:2] * (size * size)) + 1e-06)
    at = 0
    for g, group in enumerate(back):
        for i, s in enumerate(group):
            more = arrived(even, even_in[at : at + rows], odd_in[at : at + rows])
            at += rows
            for c in range(2):
                grad_ref[s, c] = (grads[g][i, c] + more[c]) * scale
    for c in range(2):
        grad_ref[grad_ref.shape[0] - 1, c] = early_ref[c] * scale
    for m in range(modes):
        share_ref[0, m] = jnp.sum(share_in[:, m * part : (m + 1) * part, :], axis=0) * scale


def total_over(value, axis):
    n = lax.axis_size(axis)
    if n & (n - 1):
        return lax.psum(value, axis)
    step = 1
    while step < n:
        value = value + lax.ppermute(value, axis, [(i, i ^ step) for i in range(n)])
        step *= 2
    return value


def body(potential, probe, amplitudes, row_offset, col_offset, counts):
    slices, _, rows, size = potential.shape
    modes = probe.shape[1]
    part = probe.shape[2]
    slots = row_offset.shape[-1]
    pieces = lax.axis_size("pos")
    cut = slices // 2
    groups = (tuple(range(cut)), tuple(range(cut, slices)))
    f32 = jnp.float32
    me = lax.axis_index("pos").astype(jnp.int32).reshape(1)
    here = [row_offset, col_offset, counts]
    anywhere = pl.BlockSpec(memory_space=pltpu.HBM)

    def exchange(value, first):
        edges = [(i, i + 1) for i in range(first, pieces - 1, 2)]
        return lax.ppermute(value, "pos", edges + [(j, i) for i, j in edges])

    def call(kernel, given, out, name, scratch=(), flops=0, places=None):
        return pl.pallas_call(
            kernel,
            out_shape=[x[0] if isinstance(x, tuple) else x for x in out],
            in_specs=places or [SMEM if jnp.issubdtype(x.dtype, jnp.integer) else VMEM for x in given],
            out_specs=[SMEM if jnp.issubdtype(x.dtype, jnp.integer) else VMEM for x in out],
            scratch_shapes=list(scratch),
            compiler_params=pltpu.CompilerParams(vmem_limit_bytes=24 * 2**20),
            cost_estimate=pl.CostEstimate(flops=flops, bytes_accessed=10**6, transcendentals=0),
            name=name,
        )(*given)

    def array(shape, dtype=f32):
        return jax.ShapeDtypeStruct(shape, dtype)

    def stage(given, made, scratch, ahead, top, back, name):
        given = dict(tables=tables_here, **given)
        scratch = dict(modes_ref=pltpu.SMEM((modes,), jnp.int32), **scratch)
        names = list(given) + list(made) + list(scratch)
        kernel = functools.partial(stage_kernel, names, ahead, top, back, pieces)
        flops = (len(ahead) + len(back) + 1) * 2 * 10**9
        return dict(zip(made, call(kernel, list(given.values()), list(made.values()), name, scratch.values(), flops)))

    gathered = {"piece_0": probe}
    for k in sorted(range(1, pieces), key=lambda k: -min(k, pieces - k)):
        gathered["piece_%d" % k] = lax.ppermute(probe, "pos", [((i + k) % pieces, i) for i in range(pieces)])
    heights = [len(groups[0]) * rows + 8, len(groups[1]) * rows + slots * size]
    packed = call(
        functools.partial(pack_kernel, groups, slots),
        [me, *here, potential, amplitudes, gathered["piece_%d" % (pieces // 2)]],
        [array((heights[i // 2], size)) for i in range(4)],
        "pack",
        scratch=[pltpu.SMEM(x.shape, jnp.int32) for x in here]
        + [pltpu.VMEM(potential.shape, f32), pltpu.VMEM(amplitudes.shape, amplitudes.dtype), pltpu.SemaphoreType.DMA((5,))],
        places=[SMEM] + [anywhere] * 6,
    )
    came = [exchange(packed[i], i % 2) for i in range(4)]
    trans_own, tables_here, amps = call(
        prepare_kernel,
        [potential, jnp.asarray(tables(size)), amplitudes],
        [array(potential.shape), array((6, 2 * size, 2 * size), jnp.bfloat16), array(amplitudes.shape, jnp.bfloat16)],
        "prepare",
        scratch=[pltpu.VMEM(potential.shape, f32), pltpu.SemaphoreType.DMA((3,))],
        flops=10**9,
        places=[anywhere] * 3,
    )
    amps = amps[0, 0]

    wave = (2 * slots, modes, size, 2 * size)
    trans = (2 * slots, 2, size, size)
    tiles = lambda n: pltpu.VMEM((n, 3, 2, rows, size), f32)
    sides = lambda n: dict(grad=array((n, 2, rows, size)), for_even=array((n * rows, size)), for_odd=array((n * rows, size)))

    first, second = groups
    a = stage(
        dict(me=me, rows=here[0], cols=here[1], count=here[2], own=trans_own, across_even=came[0], across_odd=came[1])
        | gathered,
        dict(held_out=array((10 * slots + 3 + 5,), jnp.int32), psi_0=array(wave[1:]))
        | {"psi_%d" % (s + 1): array(wave) for s in first}
        | {"trans_%d" % s: array(trans) for s in first},
        dict(tiles=tiles(len(first))),
        first,
        False,
        (),
        "ahead",
    )
    held = a["held_out"]
    b = stage(
        dict(own=trans_own, across_even=came[2], across_odd=came[3], amps=amps, held=held)
        | {"psi_%d" % second[0]: a["psi_%d" % second[0]]},
        dict(sums=array((8, size)), wave_out=array(wave))
        | {"psi_%d" % s: array(wave) for s in second[1:]}
        | {"trans_%d" % s: array(trans) for s in second},
        dict(tiles=tiles(len(second)), amps_all=pltpu.VMEM((2 * slots, size, size), f32)),
        second,
        True,
        (),
        "top",
    )
    sums = total_over(b["sums"], "group")
    state = a | b
    done = []
    back = [(slices - 1,), tuple(range(slices - 2, 0, -1)), (0,)]
    for group in back:
        end = 0 in group
        d = stage(
            dict(held=held, wave_in=state["wave_out"])
            | {"psi_%d" % s: state["psi_%d" % s] for s in group}
            | {"trans_%d" % s: state["trans_%d" % s] for s in group},
            (dict(total=array(wave[1:])) if end else dict(wave_out=array(wave))) | sides(len(group)),
            dict(grads=tiles(len(group))),
            (),
            False,
            group,
            "back",
        )
        state = state | d
        done.append(d)
    early, late = done[0], done[1:]
    rest = sum(len(group) for group in back[1:]) * rows
    shares, early_sum, for_even, for_odd = call(
        functools.partial(assemble_kernel, pieces, len(late)),
        [held, state["total"], sums, early["grad"], exchange(early["for_even"], 0), exchange(early["for_odd"], 1)]
        + [x[name] for x in late for name in ("for_even", "for_odd")],
        [
            array((pieces, modes * part + 8, 2 * size)),
            array((2, rows, size)),
            array((rest, size)),
            array((rest, size)),
        ],
        "assemble",
    )
    got = [exchange(for_even, 0), exchange(for_odd, 1)]
    shares = lax.all_to_all(shares, "pos", 0, 0)
    return call(
        functools.partial(finish_kernel, back[1:], modes),
        [held, early_sum, *[x["grad"] for x in late], *got, shares],
        [array(potential.shape), array(probe.shape)],
        "finish",
    )


def solution(mesh):
    placed = (
        P(None, None, "group", "pos"),
        P("group", None, "pos", None),
        P("group", "pos", None, None, None),
        P("group", "pos", None),
        P("group", "pos", None),
        P("group", "pos"),
    )
    return jax.shard_map(
        body,
        mesh=mesh,
        in_specs=placed,
        out_specs=(P(None, None, "group", "pos"), P("group", None, "pos", None)),
        check_vma=False,
    )
```

```python
import functools
import math

import jax
import jax.numpy as jnp
import ml_dtypes
import numpy as np
from jax import lax
from jax.experimental import pallas as pl
from jax.experimental.pallas import tpu as pltpu
from jax.sharding import PartitionSpec as P

PROP = 0.25
REG = 0.1
VMEM = pl.BlockSpec(memory_space=pltpu.VMEM)
SMEM = pl.BlockSpec(memory_space=pltpu.SMEM)


@functools.lru_cache(maxsize=None)
def tables(size):
    idx = np.arange(size)
    angle = np.float32(2.0 * math.pi / size) * (idx[:, None] * idx[None, :] % size).astype(np.float32)
    cosv = (np.cos(angle) / np.float32(math.sqrt(size))).astype(ml_dtypes.bfloat16).astype(np.float64)
    sinv = (np.sin(angle) / np.float32(math.sqrt(size))).astype(ml_dtypes.bfloat16).astype(np.float64)
    forward = np.block([[cosv, -sinv], [sinv, cosv]])
    inverse = np.block([[cosv, sinv], [-sinv, cosv]])
    freq = np.where(idx < size // 2, idx, idx - size).astype(np.float64)
    phase = -2.0 * math.pi * PROP / size * freq * freq
    real, imag = np.diag(np.cos(phase)), np.diag(np.sin(phase))
    ahead = forward @ np.block([[real, imag], [-imag, real]]) @ inverse
    behind = forward @ np.block([[real, -imag], [imag, real]]) @ inverse
    return np.stack([forward, inverse, ahead, ahead.T, behind, behind.T]).astype(ml_dtypes.bfloat16)


def mul(a, b):
    return a[0] * b[0] - a[1] * b[1], a[0] * b[1] + a[1] * b[0]


def mulc(a, b):
    return a[0] * b[0] + a[1] * b[1], a[0] * b[1] - a[1] * b[0]


def sine(x):
    y = x * x
    return x * (1.0 - y * (1 / 6) * (1.0 - y * (1 / 20) * (1.0 - y * (1 / 42) * (1.0 - y * (1 / 72)))))


def cosine(x):
    y = x * x
    return 1.0 - y * 0.5 * (1.0 - y * (1 / 12) * (1.0 - y * (1 / 30) * (1.0 - y * (1 / 56) * (1.0 - y * (1 / 90)))))


def transform(waves, right, left):
    size = waves[0][0].shape[0]
    pairs = [waves[first : first + 2] for first in range(0, len(waves), 2)]
    mids = []
    for pair in pairs:
        rows = jnp.concatenate(
            [jnp.concatenate([re.astype(jnp.bfloat16), im.astype(jnp.bfloat16)], 1) for re, im in pair], 0
        )
        mid = jnp.dot(rows, right, preferred_element_type=jnp.float32).astype(jnp.bfloat16)
        cut = [mid[i * size : (i + 1) * size] for i in range(len(pair))]
        mids.append(jnp.concatenate([jnp.concatenate([m[:, :size], m[:, size:]], 0) for m in cut], 1))
    out = []
    for pair, mid in zip(pairs, mids):
        done = jnp.dot(left, mid, preferred_element_type=jnp.float32)
        for i in range(len(pair)):
            out.append((done[:size, i * size : (i + 1) * size], done[size:, i * size : (i + 1) * size]))
    return out


def swap(values, half):
    return pltpu.roll(values, half, values.ndim - 1)


def low_lanes(shape):
    return lax.broadcasted_iota(jnp.int32, shape, len(shape) - 1) < shape[-1] // 2


def pack(pair):
    half = pair[0].shape[-1] // 2
    low = low_lanes(pair[0].shape)
    return jnp.where(low, pair[0], swap(pair[1], half)), jnp.where(low, swap(pair[0], half), pair[1])


def unpack(lows, highs):
    half = lows.shape[-1] // 2
    low = low_lanes(lows.shape)
    return jnp.where(low, lows, swap(highs, half)), jnp.where(low, swap(lows, half), highs)


def fetch(pairs, sems):
    copies = [pltpu.make_async_copy(source, target, sems.at[i]) for i, (source, target) in enumerate(pairs)]
    for copy in copies:
        copy.start()
    for copy in copies:
        copy.wait()


def pack_kernel(groups, slots, me_ref, rows_in, cols_in, count_in, potential_in, amps_in, *refs):
    rows_ref, cols_ref, count_ref, potential_ref, amps_ref, sems = refs[2 * len(groups) :]
    fetch(
        [
            (potential_in, potential_ref),
            (amps_in, amps_ref),
            (rows_in, rows_ref),
            (cols_in, cols_ref),
            (count_in, count_ref),
        ],
        sems,
    )
    even = lax.rem(me_ref[0], 2) == 0
    _, _, rows, size = potential_ref.shape
    for g, group in enumerate(groups):
        first, second = refs[2 * g : 2 * g + 2]
        for j, s in enumerate(group):
            lows, highs = pack((potential_ref[s, 0], potential_ref[s, 1]))
            first[j * rows : (j + 1) * rows] = jnp.where(even, highs, lows)
            second[j * rows : (j + 1) * rows] = jnp.where(even, lows, highs)
        top = len(group) * rows
        if g == 0:
            lane = lax.broadcasted_iota(jnp.int32, (8, size), 1)
            about = jnp.zeros((8, size), jnp.int32)
            for p in range(slots):
                about = jnp.where(lane == p, rows_ref[0, 0, p], jnp.where(lane == slots + p, cols_ref[0, 0, p], about))
            about = jnp.where(lane == 2 * slots, count_ref[0, 0], about).astype(jnp.float32)
            first[top:] = about
            second[top:] = about
        else:
            for p in range(slots):
                amps = amps_ref[0, 0, p].astype(jnp.float32)
                first[top + p * size : top + (p + 1) * size] = amps
                second[top + p * size : top + (p + 1) * size] = amps


def transmit(phase, absorption):
    magnitude = jnp.exp(-absorption)
    return magnitude * cosine(phase), magnitude * sine(phase)


def gate_kernel(*refs):
    pass


def prepare_kernel(potential_in, tables_in, amps_in, trans_ref, tables_ref, amps_ref, potential_ref, sems):
    fetch([(potential_in, potential_ref), (tables_in, tables_ref), (amps_in, amps_ref)], sems)
    for s in range(potential_ref.shape[0]):
        trans_ref[s, 0], trans_ref[s, 1] = transmit(potential_ref[s, 0], potential_ref[s, 1])


def whose(me, hops, odd):
    return jnp.where(lax.rem(me, 2) == odd, me + hops, me - hops)


class Names:
    def __init__(self, names, refs):
        self.__dict__.update(zip(names, refs))

    def get(self, name):
        return self.__dict__[name]


def stage_kernel(names, ahead, top, back, pieces, *refs):
    r = Names(names, refs)
    size = r.tables.shape[-1] // 2
    half = size // 2
    modes = r.modes_ref.shape[0]
    slots = (r.held.shape[0] - 8) // 10 if 0 not in ahead else r.rows.shape[-1]
    held = r.held if 0 not in ahead else r.held_out
    if 0 in ahead:
        me = r.me[0]
        last = me == pieces - 1
        even = lax.rem(me, 2) == 0
    else:
        even = held[1] == 1
    lanes = lax.broadcasted_iota(jnp.int32, (size, size), 1)

    def halves(i, start, count):
        one, two = r.across_even[start : start + count], r.across_odd[start : start + count]
        return jnp.where(even, one, two), jnp.where(even, two, one)

    if 0 in ahead:
        height = r.own.shape[-2]
        about = halves(0, len(ahead) * height, 8)[1][0:1].astype(jnp.int32)
        lane = lanes[0:1]
        number = jnp.int32(0)
        for k in range(2 * slots):
            p = k % slots
            if k < slots:
                row, col, count = r.rows[0, 0, p], r.cols[0, 0, p], r.count[0, 0]
                stays = (col < half) | last
                left, right = jnp.int32(0), jnp.where(last, 2, 1)
            else:
                row, col, count = [jnp.sum(jnp.where(lane == at, about, 0)) for at in (p, slots + p, 2 * slots)]
                stays = col >= half
                left, right = jnp.int32(1), jnp.int32(0)
            for j, value in enumerate((jnp.int32(k), row, col, left, right)):
                held[5 * number + 3 + j] = value
            number = number + ((p < count) & stays).astype(jnp.int32)
        held[0] = number
        held[1] = even.astype(jnp.int32)
        held[2] = r.count[0, 0]
        part = r.piece_own.shape[-2]

        def put(name, at):
            @pl.when((at >= 0) & (at < pieces))
            def _():
                r.psi_0[:, pl.ds(pl.multiple_of(at * part, part), part), :] = r.get(name)[0]

        put("piece_own", me)
        for name in names:
            if name.startswith("piece_") and name != "piece_own":
                put(name, whose(me, int(name[7:]), int(name[6])))
    number = held[0]

    for i, s in enumerate(ahead):
        height = r.own.shape[-2]
        halo = transmit(*unpack(*halves(0, i * height, height)))
        for c in range(2):
            r.tiles[i, 0, c] = r.own[s, c]
            r.tiles[i, 1, c] = halo[c]
            r.tiles[i, 2, c] = jnp.full((height, size), 1.0 - c, jnp.float32)
    if top:
        begin = len(ahead) * r.own.shape[-2]
        for p in range(slots):
            r.amps_all[p] = r.amps[p].astype(jnp.float32)
            r.amps_all[slots + p] = halves(0, begin + p * size, size)[1]
    if back:
        r.grads[...] = jnp.zeros_like(r.grads)
    if 0 in back:
        r.total[...] = jnp.zeros_like(r.total)

    def load(ref, *lead):
        return [(ref[(*lead, m, slice(None), slice(0, size))], ref[(*lead, m, slice(None), slice(size, None))]) for m in range(modes)]

    def store(ref, waves, *lead):
        for m, (re, im) in enumerate(waves):
            ref[(*lead, m, slice(None), slice(0, size))] = re
            ref[(*lead, m, slice(None), slice(size, None))] = im

    def psi(s, at):
        return load(r.psi_0) if s == 0 else load(r.get("psi_%d" % s), at)

    def trans(s, at):
        ref = r.get("trans_%d" % s)
        return ref[at, 0], ref[at, 1]

    def slot_step(at, misfit):
        k, row, col, left, right = [held[5 * at + 3 + j] for j in range(5)]
        inside = lanes >= col
        turn = lax.rem(size - col, size)
        if ahead:
            waves = psi(ahead[0], at)
        for i, s in enumerate(ahead):
            for c in range(2):
                both = jnp.where(inside, r.tiles[i, left, c, pl.ds(row, size), :], r.tiles[i, right, c, pl.ds(row, size), :])
                r.get("trans_%d" % s)[at, c] = pltpu.roll(both, turn, 1)
            waves = [mul(trans(s, at), w) for w in waves]
            if top and s == ahead[-1]:
                waves = transform(waves, r.tables[0], r.tables[1])
            else:
                waves = transform(waves, r.tables[2], r.tables[3])
                store(r.get("psi_%d" % (s + 1)), waves, at)
        if top:
            inten = sum(re * re + im * im for re, im in waves)
            model = jnp.sqrt(inten + REG)
            observed = r.amps_all[k]
            diff = model - observed
            misfit = misfit + jnp.sum(diff * diff, axis=0, keepdims=True)
            ratio = 1.0 - observed / model
            waves = transform([(ratio * re, ratio * im) for re, im in waves], r.tables[1], r.tables[0])
        elif back:
            waves = load(r.wave_in, at)
        for i, s in enumerate(back):
            waves = [mulc(trans(s, at), w) for w in waves]
            quot = [mulc(a, w) for a, w in zip(psi(s, at), waves)]
            values = sum(im for _, im in quot), -sum(re for re, _ in quot)
            for c in range(2):
                turned = pltpu.roll(values[c], col, 1)
                r.grads[i, left, c, pl.ds(row, size), :] += jnp.where(inside, turned, 0.0)
                r.grads[i, right, c, pl.ds(row, size), :] += jnp.where(inside, 0.0, turned)
            if s > 0:
                waves = transform(waves, r.tables[4], r.tables[5])
        if 0 in back:
            for m, (re, im) in enumerate(waves):
                r.total[m, :, :size] += re
                r.total[m, :, size:] += im
        elif back or top:
            store(r.wave_out, waves, at)
        return misfit

    misfit = lax.fori_loop(0, number, slot_step, jnp.zeros((1, size), jnp.float32))
    if top:
        value = jnp.sum(misfit, axis=1, keepdims=True)
        lane = lax.broadcasted_iota(jnp.int32, (1, 1, size), 2)
        count = held[2].astype(jnp.float32)
        value = jnp.where(lane == 0, value[None], jnp.where(lane == 1, count, 0.0))
        r.sums[...] = jnp.broadcast_to(value[0], r.sums.shape)
    for i, s in enumerate(back):
        r.grad[i] = r.grads[i, 0]
        lows, highs = pack((r.grads[i, 1, 0], r.grads[i, 1, 1]))
        height = lows.shape[0]
        r.for_even[i * height : (i + 1) * height] = jnp.where(even, lows, highs)
        r.for_odd[i * height : (i + 1) * height] = jnp.where(even, highs, lows)


def arrived(even, across_even, across_odd):
    return unpack(jnp.where(even, across_odd, across_even), jnp.where(even, across_even, across_odd))


def assemble_kernel(pieces, parts, flows, held_ref, me_ref, total_ref, sums_ref, own_ref, even_in, odd_in, *refs):
    sides, (done_ref, for_even, for_odd, *shares) = refs[: 2 * parts], refs[2 * parts :]
    parts_in = arrived(held_ref[1] == 1, even_in[...], odd_in[...])
    for c in range(2):
        done_ref[c] = own_ref[0, c] + parts_in[c]
    at = 0
    for i in range(parts):
        height = sides[2 * i].shape[0]
        for_even[at : at + height] = sides[2 * i][...]
        for_odd[at : at + height] = sides[2 * i + 1][...]
        at += height
    modes = total_ref.shape[0]
    part = total_ref.shape[1] // pieces
    me = me_ref[0]
    for (hops, odd), share_ref in zip([(0, 0)] + flows, shares):
        at = pl.multiple_of(jnp.clip(whose(me, hops, odd), 0, pieces - 1) * part, part)
        for m in range(modes):
            share_ref[m * part : (m + 1) * part] = total_ref[m, pl.ds(at, part), :]
        share_ref[modes * part :] = jnp.concatenate([sums_ref[...], sums_ref[...]], 1)


def finish_kernel(back, modes, held_ref, early_ref, *refs):
    count = len(back)
    grads, (even_in, odd_in, *share_in, grad_ref, share_ref) = refs[:count], refs[count:]
    even = held_ref[1] == 1
    rows, size = grad_ref.shape[2:]
    part = share_ref.shape[2]
    share = sum(ref[...] for ref in share_in)
    sums = share[modes * part : modes * part + 1]
    scale = lax.rsqrt(sums[:, 0:1] / (sums[:, 1:2] * (size * size)) + 1e-06)
    at = 0
    for g, group in enumerate(back):
        for i, s in enumerate(group):
            more = arrived(even, even_in[at : at + rows], odd_in[at : at + rows])
            at += rows
            for c in range(2):
                grad_ref[s, c] = (grads[g][i, c] + more[c]) * scale
    for c in range(2):
        grad_ref[grad_ref.shape[0] - 1, c] = early_ref[c] * scale
    for m in range(modes):
        share_ref[0, m] = share[m * part : (m + 1) * part] * scale


def total_over(value, axis):
    n = lax.axis_size(axis)
    if n & (n - 1):
        return lax.psum(value, axis)
    step = 1
    while step < n:
        value = value + lax.ppermute(value, axis, [(i, i ^ step) for i in range(n)])
        step *= 2
    return value


def body(potential, probe, amplitudes, row_offset, col_offset, counts):
    slices, _, rows, size = potential.shape
    modes = probe.shape[1]
    part = probe.shape[2]
    slots = row_offset.shape[-1]
    pieces = lax.axis_size("pos")
    cut = slices // 2
    groups = (tuple(range(cut)), tuple(range(cut, slices)))
    f32 = jnp.float32
    me = lax.axis_index("pos").astype(jnp.int32).reshape(1)
    here = [row_offset, col_offset, counts]
    anywhere = pl.BlockSpec(memory_space=pltpu.HBM)

    def swaps(odd, hops):
        edges = [(i, i + 1) for i in range(odd, pieces - 1, 2)]
        return [(j, i) for i, j in edges if i + hops < pieces] + [(i, j) for i, j in edges if j - hops >= 0]

    def exchange(value, odd):
        return lax.ppermute(value, "pos", swaps(odd, 1))

    def call(kernel, given, out, name, scratch=(), flops=0, places=None):
        return pl.pallas_call(
            kernel,
            out_shape=[x[0] if isinstance(x, tuple) else x for x in out],
            in_specs=places or [SMEM if jnp.issubdtype(x.dtype, jnp.integer) else VMEM for x in given],
            out_specs=[SMEM if jnp.issubdtype(x.dtype, jnp.integer) else VMEM for x in out],
            scratch_shapes=list(scratch),
            compiler_params=pltpu.CompilerParams(vmem_limit_bytes=24 * 2**20),
            cost_estimate=pl.CostEstimate(flops=flops, bytes_accessed=10**6, transcendentals=0),
            name=name,
        )(*given)

    def array(shape, dtype=f32):
        return jax.ShapeDtypeStruct(shape, dtype)

    def stage(given, made, scratch, ahead, top, back, name):
        given = dict(tables=tables_here, **given)
        scratch = dict(modes_ref=pltpu.SMEM((modes,), jnp.int32), **scratch)
        names = list(given) + list(made) + list(scratch)
        kernel = functools.partial(stage_kernel, names, ahead, top, back, pieces)
        flops = (len(ahead) + len(back) + 1) * 2 * 10**9
        return dict(zip(made, call(kernel, list(given.values()), list(made.values()), name, scratch.values(), flops)))

    flows = [(hops, odd) for hops in range(1, pieces) for odd in range(2) if swaps(odd, hops)]
    def gate(values, after, name="gate"):
        return pl.pallas_call(
            gate_kernel,
            out_shape=[array(x.shape) for x in values],
            in_specs=[VMEM] * (len(values) + len(after)),
            out_specs=[VMEM] * len(values),
            input_output_aliases={i: i for i in range(len(values))},
            compiler_params=pltpu.CompilerParams(vmem_limit_bytes=24 * 2**20),
            name=name,
        )(*values, *after)

    gathered = {}
    for hops in range(1, pieces):
        now = [odd for hop, odd in flows if hop == hops]
        sources = [gathered["piece_%d%d" % (1 - odd, hops - 1)] if hops > 1 else probe for odd in now]
        if hops == 2:
            sources = gate(sources, [], "round")
            gathered |= {"piece_%d1" % (1 - odd): source for odd, source in zip(now, sources)}
        for odd, source in zip(now, sources):
            gathered["piece_%d%d" % (odd, hops)] = lax.ppermute(source, "pos", swaps(odd, hops))
    heights = [len(groups[0]) * rows + 8, len(groups[1]) * rows + slots * size]
    packed = call(
        functools.partial(pack_kernel, groups, slots),
        [me, *here, potential, amplitudes],
        [array((heights[i // 2], size)) for i in range(4)],
        "pack",
        scratch=[pltpu.SMEM(x.shape, jnp.int32) for x in here]
        + [pltpu.VMEM(potential.shape, f32), pltpu.VMEM(amplitudes.shape, amplitudes.dtype), pltpu.SemaphoreType.DMA((5,))],
        places=[SMEM] + [anywhere] * 5,
    )
    packed = gate(packed, [gathered["piece_%d%d" % f[::-1]] for f in flows if f[0] >= pieces - 2])
    came = [exchange(packed[i], i % 2) for i in range(4)]
    trans_own, tables_here, amps = call(
        prepare_kernel,
        [potential, jnp.asarray(tables(size)), amplitudes],
        [array(potential.shape), array((6, 2 * size, 2 * size), jnp.bfloat16), array(amplitudes.shape, jnp.bfloat16)],
        "prepare",
        scratch=[pltpu.VMEM(potential.shape, f32), pltpu.SemaphoreType.DMA((3,))],
        flops=10**9,
        places=[anywhere] * 3,
    )
    amps = amps[0, 0]

    wave = (2 * slots, modes, size, 2 * size)
    trans = (2 * slots, 2, size, size)
    tiles = lambda n: pltpu.VMEM((n, 3, 2, rows, size), f32)
    sides = lambda n: dict(grad=array((n, 2, rows, size)), for_even=array((n * rows, size)), for_odd=array((n * rows, size)))

    first, second = groups
    a = stage(
        dict(me=me, rows=here[0], cols=here[1], count=here[2], own=trans_own, across_even=came[0], across_odd=came[1])
        | {"piece_own": probe}
        | gathered,
        dict(held_out=array((10 * slots + 3 + 5,), jnp.int32), psi_0=array(wave[1:]))
        | {"psi_%d" % (s + 1): array(wave) for s in first}
        | {"trans_%d" % s: array(trans) for s in first},
        dict(tiles=tiles(len(first))),
        first,
        False,
        (),
        "ahead",
    )
    held = a["held_out"]
    b = stage(
        dict(own=trans_own, across_even=came[2], across_odd=came[3], amps=amps, held=held)
        | {"psi_%d" % second[0]: a["psi_%d" % second[0]]},
        dict(sums=array((8, size)), wave_out=array(wave))
        | {"psi_%d" % s: array(wave) for s in second[1:]}
        | {"trans_%d" % s: array(trans) for s in second},
        dict(tiles=tiles(len(second)), amps_all=pltpu.VMEM((2 * slots, size, size), f32)),
        second,
        True,
        (),
        "top",
    )
    sums = total_over(b["sums"], "group")
    state = a | b
    done = []
    back = [(slices - 1,), tuple(range(slices - 2, 0, -1)), (0,)]
    for group in back:
        end = 0 in group
        d = stage(
            dict(held=held, wave_in=state["wave_out"])
            | {"psi_%d" % s: state["psi_%d" % s] for s in group}
            | {"trans_%d" % s: state["trans_%d" % s] for s in group},
            (dict(total=array(wave[1:])) if end else dict(wave_out=array(wave))) | sides(len(group)),
            dict(grads=tiles(len(group))),
            (),
            False,
            group,
            "back",
        )
        state = state | d
        done.append(d)
    early, late = done[0], done[1:]
    rest = sum(len(group) for group in back[1:]) * rows
    early_sum, for_even, for_odd, *shares = call(
        functools.partial(assemble_kernel, pieces, len(late), flows),
        [held, me, state["total"], sums, early["grad"], exchange(early["for_even"], 0), exchange(early["for_odd"], 1)]
        + [x[name] for x in late for name in ("for_even", "for_odd")],
        [array((2, rows, size)), array((rest, size)), array((rest, size))]
        + [array((modes * part + 8, 2 * size))] * (1 + len(flows)),
        "assemble",
    )
    own_share, flow = shares[0], dict(zip(flows, shares[1:]))
    ends = [own_share]
    for hops, odd in sorted(flows, key=lambda f: -f[0]):
        came_back = lax.ppermute(flow[hops, odd], "pos", [(j, i) for i, j in swaps(odd, hops)])
        if hops >= pieces - 2 and odd == 0:
            (for_even,) = gate([for_even], [came_back])
        if hops > 1:
            flow[hops - 1, 1 - odd] = flow[hops - 1, 1 - odd] + came_back
        else:
            ends.append(came_back)
    got = [exchange(for_even, 0), exchange(for_odd, 1)]
    return call(
        functools.partial(finish_kernel, back[1:], modes),
        [held, early_sum, *[x["grad"] for x in late], *got, *ends],
        [array(potential.shape), array(probe.shape)],
        "finish",
    )


def solution(mesh):
    placed = (
        P(None, None, "group", "pos"),
        P("group", None, "pos", None),
        P("group", "pos", None, None, None),
        P("group", "pos", None),
        P("group", "pos", None),
        P("group", "pos"),
    )
    return jax.shard_map(
        body,
        mesh=mesh,
        in_specs=placed,
        out_specs=(P(None, None, "group", "pos"), P("group", None, "pos", None)),
        check_vma=False,
    )
```

```python
import functools
import math

import jax
import jax.numpy as jnp
import ml_dtypes
import numpy as np
from jax import lax
from jax.experimental import pallas as pl
from jax.experimental.pallas import tpu as pltpu
from jax.sharding import PartitionSpec as P

PROP = 0.25
REG = 0.1
VMEM = pl.BlockSpec(memory_space=pltpu.VMEM)
SMEM = pl.BlockSpec(memory_space=pltpu.SMEM)


@functools.lru_cache(maxsize=None)
def tables(size):
    idx = np.arange(size)
    angle = np.float32(2.0 * math.pi / size) * (idx[:, None] * idx[None, :] % size).astype(np.float32)
    cosv = (np.cos(angle) / np.float32(math.sqrt(size))).astype(ml_dtypes.bfloat16).astype(np.float64)
    sinv = (np.sin(angle) / np.float32(math.sqrt(size))).astype(ml_dtypes.bfloat16).astype(np.float64)
    forward = np.block([[cosv, -sinv], [sinv, cosv]])
    inverse = np.block([[cosv, sinv], [-sinv, cosv]])
    freq = np.where(idx < size // 2, idx, idx - size).astype(np.float64)
    phase = -2.0 * math.pi * PROP / size * freq * freq
    real, imag = np.diag(np.cos(phase)), np.diag(np.sin(phase))
    ahead = forward @ np.block([[real, imag], [-imag, real]]) @ inverse
    behind = forward @ np.block([[real, -imag], [imag, real]]) @ inverse
    rows = np.arange(2 * size).reshape(2, size // 8, 8).swapaxes(0, 1).reshape(-1)
    left = [t.T[rows] for t in (forward, inverse, ahead, behind)]
    return np.stack([forward, inverse, ahead, behind, *left]).astype(ml_dtypes.bfloat16)


def mul(a, b):
    return a[0] * b[0] - a[1] * b[1], a[0] * b[1] + a[1] * b[0]


def mulc(a, b):
    return a[0] * b[0] + a[1] * b[1], a[0] * b[1] - a[1] * b[0]


def sine(x):
    y = x * x
    return x * (1.0 - y * (1 / 6) * (1.0 - y * (1 / 20) * (1.0 - y * (1 / 42) * (1.0 - y * (1 / 72)))))


def cosine(x):
    y = x * x
    return 1.0 - y * 0.5 * (1.0 - y * (1 / 12) * (1.0 - y * (1 / 30) * (1.0 - y * (1 / 56) * (1.0 - y * (1 / 90)))))


def transform(waves, right, left):
    size = waves[0][0].shape[0]
    pairs = [waves[first : first + 2] for first in range(0, len(waves), 2)]
    mids = []
    for pair in pairs:
        rows = jnp.concatenate(
            [jnp.concatenate([re.astype(jnp.bfloat16), im.astype(jnp.bfloat16)], 1) for re, im in pair], 0
        )
        mid = jnp.dot(rows, right, preferred_element_type=jnp.float32).astype(jnp.bfloat16)
        cut = [mid[i * size : (i + 1) * size] for i in range(len(pair))]
        mids.append(jnp.concatenate([jnp.concatenate([m[:, :size], m[:, size:]], 0) for m in cut], 1))
    out = []
    for pair, mid in zip(pairs, mids):
        done = jnp.dot(left, mid, preferred_element_type=jnp.float32)
        done = done.reshape(size // 8, 2, 8, -1)
        parts = [done[:, c].reshape(size, -1) for c in range(2)]
        for i in range(len(pair)):
            out.append(tuple(x[:, i * size : (i + 1) * size] for x in parts))
    return out


def swap(values, half):
    return pltpu.roll(values, half, values.ndim - 1)


def low_lanes(shape):
    return lax.broadcasted_iota(jnp.int32, shape, len(shape) - 1) < shape[-1] // 2


def pack(pair):
    half = pair[0].shape[-1] // 2
    low = low_lanes(pair[0].shape)
    return jnp.where(low, pair[0], swap(pair[1], half)), jnp.where(low, swap(pair[0], half), pair[1])


def unpack(lows, highs):
    half = lows.shape[-1] // 2
    low = low_lanes(lows.shape)
    return jnp.where(low, lows, swap(highs, half)), jnp.where(low, swap(lows, half), highs)


def pack_kernel(groups, me_ref, row_ref, col_ref, count_ref, potential_ref, amps_ref, *refs):
    slots = row_ref.shape[0]
    even = lax.rem(me_ref[0], 2) == 0
    _, _, rows, size = potential_ref.shape
    for g, group in enumerate(groups):
        first, second = refs[2 * g : 2 * g + 2]
        for j, s in enumerate(group):
            lows, highs = pack((potential_ref[s, 0], potential_ref[s, 1]))
            first[j * rows : (j + 1) * rows] = jnp.where(even, highs, lows)
            second[j * rows : (j + 1) * rows] = jnp.where(even, lows, highs)
        top = len(group) * rows
        if g == 0:
            lane = lax.broadcasted_iota(jnp.int32, (8, size), 1)
            about = jnp.zeros((8, size), jnp.int32)
            for p in range(slots):
                about = jnp.where(lane == p, row_ref[p], jnp.where(lane == slots + p, col_ref[p], about))
            about = jnp.where(lane == 2 * slots, count_ref[0], about).astype(jnp.float32)
            first[top:] = about
            second[top:] = about
        else:
            for p in range(slots):
                amps = amps_ref[p].astype(jnp.float32)
                first[top + p * size : top + (p + 1) * size] = amps
                second[top + p * size : top + (p + 1) * size] = amps


def transmit(phase, absorption):
    magnitude = jnp.exp(-absorption)
    return magnitude * cosine(phase), magnitude * sine(phase)


def gate_kernel(*refs):
    pass


def prepare_kernel(potential_ref, tables_ref, amps_ref, pieces_ref, trans_ref, tables_out, amps_out, probe_ref):
    part = pieces_ref.shape[2]
    for k in range(pieces_ref.shape[0]):
        probe_ref[:, k * part : (k + 1) * part, :] = pieces_ref[k]
    for s in range(potential_ref.shape[0]):
        trans_ref[s, 0], trans_ref[s, 1] = transmit(potential_ref[s, 0], potential_ref[s, 1])
    tables_out[...] = tables_ref[...]
    amps_out[...] = amps_ref[...]


class Names:
    def __init__(self, names, refs):
        self.__dict__.update(zip(names, refs))

    def get(self, name):
        return self.__dict__[name]


def stage_kernel(names, ahead, top, back, pieces, *refs):
    r = Names(names, refs)
    size = r.tables.shape[-1] // 2
    half = size // 2
    modes = r.modes_ref.shape[0]
    slots = r.rows.shape[0]
    me = r.me[0]
    last = me == pieces - 1
    even = lax.rem(me, 2) == 0
    lanes = lax.broadcasted_iota(jnp.int32, (size, size), 1)

    def halves(i, start, count):
        one, two = r.across_even[start : start + count], r.across_odd[start : start + count]
        return jnp.where(even, one, two), jnp.where(even, two, one)

    if 0 in ahead:
        height = r.own.shape[-2]
        about = halves(0, len(ahead) * height, 8)[1][0:1].astype(jnp.int32)
        lane = lanes[0:1]
        number = jnp.int32(0)
        for k in range(2 * slots):
            p = k % slots
            if k < slots:
                row, col, count = r.rows[p], r.cols[p], r.count[0]
                stays = (col < half) | last
            else:
                row, col, count = [jnp.sum(jnp.where(lane == at, about, 0)) for at in (p, slots + p, 2 * slots)]
                stays = col >= half
            r.held_out[3 * number + 1] = jnp.int32(k)
            r.held_out[3 * number + 2] = row
            r.held_out[3 * number + 3] = col
            number = number + ((p < count) & stays).astype(jnp.int32)
        r.held_out[0] = number
        held = r.held_out
    else:
        held = r.held
    number = held[0]

    for i, s in enumerate(ahead):
        height = r.own.shape[-2]
        halo = transmit(*unpack(*halves(0, i * height, height)))
        for c in range(2):
            r.tiles[i, 0, c] = r.own[s, c]
            r.tiles[i, 1, c] = halo[c]
            r.tiles[i, 2, c] = jnp.full((height, size), 1.0 - c, jnp.float32)
    if top:
        begin = len(ahead) * r.own.shape[-2]
        for p in range(slots):
            r.amps_all[p] = r.amps[p].astype(jnp.float32)
            r.amps_all[slots + p] = halves(0, begin + p * size, size)[1]
    if back:
        r.grads[...] = jnp.zeros_like(r.grads)
    if 0 in back:
        r.total[...] = jnp.zeros_like(r.total)

    def load(ref, *lead):
        return [(ref[(*lead, m, slice(None), slice(0, size))], ref[(*lead, m, slice(None), slice(size, None))]) for m in range(modes)]

    def store(ref, waves, *lead):
        for m, (re, im) in enumerate(waves):
            ref[(*lead, m, slice(None), slice(0, size))] = re
            ref[(*lead, m, slice(None), slice(size, None))] = im

    def psi(s, at):
        return load(r.psi_0) if s == 0 else load(r.get("psi_%d" % s), at)

    def trans(s, at):
        ref = r.get("trans_%d" % s)
        return ref[at, 0], ref[at, 1]

    def slot_step(at, misfit):
        k = held[3 * at + 1]
        row = held[3 * at + 2]
        col = held[3 * at + 3]
        own = k < slots
        left = jnp.where(own, 0, 1)
        right = jnp.where(own, jnp.where(last, 2, 1), 0)
        turn = lax.rem(size - col, size)
        inside = lanes >= col
        for i, s in enumerate(ahead):
            for c in range(2):
                both = jnp.where(inside, r.tiles[i, left, c, pl.ds(row, size), :], r.tiles[i, right, c, pl.ds(row, size), :])
                r.get("trans_%d" % s)[at, c] = pltpu.roll(both, turn, 1)
            waves = [mul(trans(s, at), w) for w in psi(s, at)]
            if top and s == ahead[-1]:
                waves = transform(waves, r.tables[0], r.tables[4])
            else:
                waves = transform(waves, r.tables[2], r.tables[6])
                store(r.get("psi_%d" % (s + 1)), waves, at)
        if top:
            inten = sum(re * re + im * im for re, im in waves)
            model = jnp.sqrt(inten + REG)
            observed = r.amps_all[k]
            diff = model - observed
            misfit = misfit + jnp.sum(diff * diff, axis=0, keepdims=True)
            ratio = 1.0 - observed / model
            waves = transform([(ratio * re, ratio * im) for re, im in waves], r.tables[1], r.tables[5])
        elif back:
            waves = load(r.wave_in, at)
        for i, s in enumerate(back):
            waves = [mulc(trans(s, at), w) for w in waves]
            quot = [mulc(a, w) for a, w in zip(psi(s, at), waves)]
            values = sum(im for _, im in quot), -sum(re for re, _ in quot)
            for c in range(2):
                turned = pltpu.roll(values[c], col, 1)
                r.grads[i, left, c, pl.ds(row, size), :] += jnp.where(inside, turned, 0.0)
                r.grads[i, right, c, pl.ds(row, size), :] += jnp.where(inside, 0.0, turned)
            if s > 0:
                waves = transform(waves, r.tables[3], r.tables[7])
        if 0 in back:
            for m, (re, im) in enumerate(waves):
                r.total[m, :, :size] += re
                r.total[m, :, size:] += im
        elif back or top:
            store(r.wave_out, waves, at)
        return misfit

    misfit = lax.fori_loop(0, number, slot_step, jnp.zeros((1, size), jnp.float32))
    if top:
        value = jnp.sum(misfit, axis=1, keepdims=True)
        lane = lax.broadcasted_iota(jnp.int32, (1, 1, size), 2)
        count = r.count[0].astype(jnp.float32)
        value = jnp.where(lane == 0, value[None], jnp.where(lane == 1, count, 0.0))
        r.sums[...] = jnp.broadcast_to(value[0], r.sums.shape)
    for i, s in enumerate(back):
        r.grad[i] = r.grads[i, 0]
        lows, highs = pack((r.grads[i, 1, 0], r.grads[i, 1, 1]))
        height = lows.shape[0]
        r.for_even[i * height : (i + 1) * height] = jnp.where(even, lows, highs)
        r.for_odd[i * height : (i + 1) * height] = jnp.where(even, highs, lows)
    if 0 in back:
        part = r.total.shape[1] // pieces
        sums = r.sums_in[...]
        for k in range(pieces):
            for m in range(modes):
                r.share[k, m * part : (m + 1) * part] = r.total[m, k * part : (k + 1) * part, :]
            r.share[k, modes * part :] = jnp.concatenate([sums, sums], 1)


def stage(given, made, scratch, ahead, top, back, pieces, name):
    names = [n for n, _, _ in given] + [n for n, _ in made] + [n for n, _ in scratch]
    out = pl.pallas_call(
        functools.partial(stage_kernel, names, ahead, top, back, pieces),
        out_shape=[jax.ShapeDtypeStruct(shape, jnp.float32) for _, shape in made],
        in_specs=[SMEM if small else VMEM for _, _, small in given],
        out_specs=[VMEM] * len(made),
        scratch_shapes=[x for _, x in scratch],
        compiler_params=pltpu.CompilerParams(vmem_limit_bytes=24 * 2**20),
        cost_estimate=pl.CostEstimate(flops=(len(ahead) + len(back) + 1) * 10**9, bytes_accessed=10**7, transcendentals=0),
        name=name,
    )(*[x for _, x, _ in given])
    return dict(zip([n for n, _ in made], out))


def finish_kernel(back, modes, me_ref, *refs):
    count = len(back)
    grads, evens, odds = refs[:count], refs[count : 2 * count], refs[2 * count : 3 * count]
    share_in, grad_ref, share_ref = refs[3 * count :]
    even = lax.rem(me_ref[0], 2) == 0
    rows, size = grad_ref.shape[2:]
    part = share_ref.shape[2]
    sums = jnp.sum(share_in[:, modes * part :, :], axis=0)[0:1]
    scale = lax.rsqrt(sums[:, 0:1] / (sums[:, 1:2] * (size * size)) + 1e-06)
    for g, group in enumerate(back):
        for i, s in enumerate(group):
            one, two = evens[g][i * rows : (i + 1) * rows], odds[g][i * rows : (i + 1) * rows]
            arrived = unpack(jnp.where(even, two, one), jnp.where(even, one, two))
            for c in range(2):
                grad_ref[s, c] = (grads[g][i, c] + arrived[c]) * scale
    for m in range(modes):
        share_ref[0, m] = jnp.sum(share_in[:, m * part : (m + 1) * part, :], axis=0) * scale


def total_over(value, axis):
    n = lax.axis_size(axis)
    if n & (n - 1):
        return lax.psum(value, axis)
    step = 1
    while step < n:
        value = value + lax.ppermute(value, axis, [(i, i ^ step) for i in range(n)])
        step *= 2
    return value


def body(potential, probe, amplitudes, row_offset, col_offset, counts):
    slices, _, rows, size = potential.shape
    modes = probe.shape[1]
    part = probe.shape[2]
    slots = row_offset.shape[-1]
    pieces = lax.axis_size("pos")
    cut = slices // 2
    groups = (tuple(range(cut)), tuple(range(cut, slices)))
    f32 = jnp.float32
    me = lax.axis_index("pos").astype(jnp.int32).reshape(1)
    here = [row_offset[0, 0], col_offset[0, 0], counts[0]]

    def exchange(value, first):
        edges = [(i, i + 1) for i in range(first, pieces - 1, 2)]
        return lax.ppermute(value, "pos", edges + [(j, i) for i, j in edges])

    def call(kernel, given, out, name, scratch=(), flops=0):
        return pl.pallas_call(
            kernel,
            out_shape=[x[0] if isinstance(x, tuple) else x for x in out],
            in_specs=[SMEM if jnp.issubdtype(x.dtype, jnp.integer) else VMEM for x in given],
            out_specs=[SMEM if jnp.issubdtype(x.dtype, jnp.integer) else VMEM for x in out],
            scratch_shapes=list(scratch),
            compiler_params=pltpu.CompilerParams(vmem_limit_bytes=24 * 2**20),
            cost_estimate=pl.CostEstimate(flops=flops, bytes_accessed=10**6, transcendentals=0),
            name=name,
        )(*given)

    def array(shape, dtype=f32):
        return jax.ShapeDtypeStruct(shape, dtype)

    def stage(given, made, scratch, ahead, top, back, name):
        given = dict(me=me, rows=here[0], cols=here[1], count=here[2], tables=tables_here, **given)
        scratch = dict(modes_ref=pltpu.SMEM((modes,), jnp.int32), **scratch)
        names = list(given) + list(made) + list(scratch)
        kernel = functools.partial(stage_kernel, names, ahead, top, back, pieces)
        flops = (len(ahead) + len(back) + 1) * 2 * 10**9
        return dict(zip(made, call(kernel, list(given.values()), list(made.values()), name, scratch.values(), flops)))

    gathered = lax.all_to_all(jnp.broadcast_to(probe, (pieces,) + probe.shape[1:]), "pos", 0, 0)
    heights = [len(groups[0]) * rows + 8, len(groups[1]) * rows + slots * size]
    packed = call(
        functools.partial(pack_kernel, groups),
        [me, *here, potential, amplitudes[0, 0]],
        [array((heights[i // 2], size)) for i in range(4)],
        "pack",
    )
    came = [exchange(packed[i], i % 2) for i in range(2)]
    held_back = pl.pallas_call(
        gate_kernel,
        out_shape=[array(x.shape) for x in packed[2:]],
        in_specs=[VMEM] * 4,
        out_specs=[VMEM] * 2,
        input_output_aliases={0: 0, 1: 1},
        compiler_params=pltpu.CompilerParams(vmem_limit_bytes=24 * 2**20),
        name="gate",
    )(*packed[2:], *came)
    came += [exchange(held_back[i], i) for i in range(2)]
    trans_own, tables_here, amps, probe_all = call(
        prepare_kernel,
        [potential, jnp.asarray(tables(size)), amplitudes[0, 0], gathered],
        [
            array(potential.shape),
            array((8, 2 * size, 2 * size), jnp.bfloat16),
            array((slots, size, size), jnp.bfloat16),
            array((modes, size, 2 * size)),
        ],
        "prepare",
        flops=10**9,
    )

    wave = (2 * slots, modes, size, 2 * size)
    trans = (2 * slots, 2, size, size)
    tiles = lambda n: pltpu.VMEM((n, 3, 2, rows, size), f32)
    sides = lambda n: dict(grad=array((n, 2, rows, size)), for_even=array((n * rows, size)), for_odd=array((n * rows, size)))

    first, second = groups
    a = stage(
        dict(own=trans_own, across_even=came[0], across_odd=came[1], psi_0=probe_all),
        dict(held_out=array((6 * slots + 4,), jnp.int32))
        | {"psi_%d" % (s + 1): array(wave) for s in first}
        | {"trans_%d" % s: array(trans) for s in first},
        dict(tiles=tiles(len(first))),
        first,
        False,
        (),
        "ahead",
    )
    held = a["held_out"]
    b = stage(
        dict(own=trans_own, across_even=came[2], across_odd=came[3], amps=amps, held=held)
        | {"psi_%d" % second[0]: a["psi_%d" % second[0]]},
        dict(sums=array((8, size)), wave_out=array(wave))
        | {"psi_%d" % s: array(wave) for s in second[1:]}
        | {"trans_%d" % s: array(trans) for s in second},
        dict(tiles=tiles(len(second)), amps_all=pltpu.VMEM((2 * slots, size, size), f32)),
        second,
        True,
        (),
        "top",
    )
    sums = total_over(b["sums"], "group")
    state = a | b | dict(psi_0=probe_all)
    done = []
    back = [(slices - 1,), tuple(range(slices - 2, 0, -1)), (0,)]
    for group in back:
        end = 0 in group
        made = dict(share=array((pieces, modes * part + 8, 2 * size))) if end else dict(wave_out=array(wave))
        scratch = dict(total=pltpu.VMEM(wave[1:], f32)) if end else {}
        d = stage(
            dict(held=held, wave_in=state["wave_out"])
            | {"psi_%d" % s: state["psi_%d" % s] for s in group}
            | {"trans_%d" % s: state["trans_%d" % s] for s in group}
            | (dict(sums_in=sums) if end else {}),
            made | sides(len(group)),
            dict(grads=tiles(len(group))) | scratch,
            (),
            False,
            group,
            "back",
        )
        state = state | d
        done.append(d)
    join = lambda name: jnp.concatenate([x[name] for x in done], 0)
    got = [exchange(join("for_even"), 0), exchange(join("for_odd"), 1)]
    shares = lax.all_to_all(d["share"], "pos", 0, 0)
    return call(
        functools.partial(finish_kernel, (sum(back, ()),), modes),
        [me, join("grad"), *got, shares],
        [array(potential.shape), array(probe.shape)],
        "finish",
    )


def solution(mesh):
    placed = (
        P(None, None, "group", "pos"),
        P("group", None, "pos", None),
        P("group", "pos", None, None, None),
        P("group", "pos", None),
        P("group", "pos", None),
        P("group", "pos"),
    )
    return jax.shard_map(
        body,
        mesh=mesh,
        in_specs=placed,
        out_specs=(P(None, None, "group", "pos"), P("group", None, "pos", None)),
        check_vma=False,
    )
```

```python
import functools
import math

import jax
import jax.numpy as jnp
import ml_dtypes
import numpy as np
from jax import lax
from jax.experimental import pallas as pl
from jax.experimental.pallas import tpu as pltpu
from jax.sharding import PartitionSpec as P

PROP = 0.25
REG = 0.1
VMEM = pl.BlockSpec(memory_space=pltpu.VMEM)
SMEM = pl.BlockSpec(memory_space=pltpu.SMEM)


@functools.lru_cache(maxsize=None)
def tables(size):
    idx = np.arange(size)
    angle = np.float32(2.0 * math.pi / size) * (idx[:, None] * idx[None, :] % size).astype(np.float32)
    cosv = (np.cos(angle) / np.float32(math.sqrt(size))).astype(ml_dtypes.bfloat16).astype(np.float64)
    sinv = (np.sin(angle) / np.float32(math.sqrt(size))).astype(ml_dtypes.bfloat16).astype(np.float64)
    forward = np.block([[cosv, -sinv], [sinv, cosv]])
    inverse = np.block([[cosv, sinv], [-sinv, cosv]])
    freq = np.where(idx < size // 2, idx, idx - size).astype(np.float64)
    phase = -2.0 * math.pi * PROP / size * freq * freq
    real, imag = np.diag(np.cos(phase)), np.diag(np.sin(phase))
    ahead = forward @ np.block([[real, imag], [-imag, real]]) @ inverse
    behind = forward @ np.block([[real, -imag], [imag, real]]) @ inverse
    rows = np.arange(2 * size).reshape(2, size // 8, 8).swapaxes(0, 1).reshape(-1)
    left = [t.T[rows] for t in (forward, inverse, ahead, behind)]
    return np.stack([forward, inverse, ahead, behind, *left]).astype(ml_dtypes.bfloat16)


def mul(a, b):
    return a[0] * b[0] - a[1] * b[1], a[0] * b[1] + a[1] * b[0]


def mulc(a, b):
    return a[0] * b[0] + a[1] * b[1], a[0] * b[1] - a[1] * b[0]


def sine(x):
    y = x * x
    return x * (1.0 - y * (1 / 6) * (1.0 - y * (1 / 20) * (1.0 - y * (1 / 42) * (1.0 - y * (1 / 72)))))


def cosine(x):
    y = x * x
    return 1.0 - y * 0.5 * (1.0 - y * (1 / 12) * (1.0 - y * (1 / 30) * (1.0 - y * (1 / 56) * (1.0 - y * (1 / 90)))))


def transform(waves, right, left):
    size = waves[0][0].shape[0]
    pairs = [waves[first : first + 2] for first in range(0, len(waves), 2)]
    mids = []
    for pair in pairs:
        rows = jnp.concatenate(
            [jnp.concatenate([re.astype(jnp.bfloat16), im.astype(jnp.bfloat16)], 1) for re, im in pair], 0
        )
        mid = jnp.dot(rows, right, preferred_element_type=jnp.float32).astype(jnp.bfloat16)
        cut = [mid[i * size : (i + 1) * size] for i in range(len(pair))]
        mids.append(jnp.concatenate([jnp.concatenate([m[:, :size], m[:, size:]], 0) for m in cut], 1))
    out = []
    for pair, mid in zip(pairs, mids):
        done = jnp.dot(left, mid, preferred_element_type=jnp.float32)
        done = done.reshape(size // 8, 2, 8, -1)
        parts = [done[:, c].reshape(size, -1) for c in range(2)]
        for i in range(len(pair)):
            out.append(tuple(x[:, i * size : (i + 1) * size] for x in parts))
    return out


def swap(values, half):
    return pltpu.roll(values, half, values.ndim - 1)


def low_lanes(shape):
    return lax.broadcasted_iota(jnp.int32, shape, len(shape) - 1) < shape[-1] // 2


def pack(pair):
    half = pair[0].shape[-1] // 2
    low = low_lanes(pair[0].shape)
    return jnp.where(low, pair[0], swap(pair[1], half)), jnp.where(low, swap(pair[0], half), pair[1])


def unpack(lows, highs):
    half = lows.shape[-1] // 2
    low = low_lanes(lows.shape)
    return jnp.where(low, lows, swap(highs, half)), jnp.where(low, swap(lows, half), highs)


def pack_kernel(groups, me_ref, row_ref, col_ref, count_ref, potential_ref, amps_ref, *refs):
    slots = row_ref.shape[0]
    even = lax.rem(me_ref[0], 2) == 0
    _, _, rows, size = potential_ref.shape
    for g, group in enumerate(groups):
        first, second = refs[2 * g : 2 * g + 2]
        for j, s in enumerate(group):
            lows, highs = pack((potential_ref[s, 0], potential_ref[s, 1]))
            first[j * rows : (j + 1) * rows] = jnp.where(even, highs, lows)
            second[j * rows : (j + 1) * rows] = jnp.where(even, lows, highs)
        top = len(group) * rows
        if g == 0:
            lane = lax.broadcasted_iota(jnp.int32, (8, size), 1)
            about = jnp.zeros((8, size), jnp.int32)
            for p in range(slots):
                about = jnp.where(lane == p, row_ref[p], jnp.where(lane == slots + p, col_ref[p], about))
            about = jnp.where(lane == 2 * slots, count_ref[0], about).astype(jnp.float32)
            first[top:] = about
            second[top:] = about
        else:
            for p in range(slots):
                amps = amps_ref[p].astype(jnp.float32)
                first[top + p * size : top + (p + 1) * size] = amps
                second[top + p * size : top + (p + 1) * size] = amps


def transmit(phase, absorption):
    magnitude = jnp.exp(-absorption)
    return magnitude * cosine(phase), magnitude * sine(phase)


def gate_kernel(*refs):
    pass


def prepare_kernel(potential_ref, tables_ref, amps_ref, pieces_ref, trans_ref, tables_out, amps_out, probe_ref):
    part = pieces_ref.shape[2]
    for k in range(pieces_ref.shape[0]):
        probe_ref[:, k * part : (k + 1) * part, :] = pieces_ref[k]
    for s in range(potential_ref.shape[0]):
        trans_ref[s, 0], trans_ref[s, 1] = transmit(potential_ref[s, 0], potential_ref[s, 1])
    tables_out[...] = tables_ref[...]
    amps_out[...] = amps_ref[...]


class Names:
    def __init__(self, names, refs):
        self.__dict__.update(zip(names, refs))

    def get(self, name):
        return self.__dict__[name]


def stage_kernel(names, ahead, top, back, pieces, *refs):
    r = Names(names, refs)
    size = r.tables.shape[-1] // 2
    half = size // 2
    modes = r.modes_ref.shape[0]
    slots = r.rows.shape[0]
    me = r.me[0]
    last = me == pieces - 1
    even = lax.rem(me, 2) == 0
    lanes = lax.broadcasted_iota(jnp.int32, (size, size), 1)

    def halves(i, start, count):
        one, two = r.across_even[start : start + count], r.across_odd[start : start + count]
        return jnp.where(even, one, two), jnp.where(even, two, one)

    if 0 in ahead:
        height = r.own.shape[-2]
        about = halves(0, len(ahead) * height, 8)[1][0:1].astype(jnp.int32)
        lane = lanes[0:1]
        number = jnp.int32(0)
        for k in range(2 * slots):
            p = k % slots
            if k < slots:
                row, col, count = r.rows[p], r.cols[p], r.count[0]
                stays = (col < half) | last
            else:
                row, col, count = [jnp.sum(jnp.where(lane == at, about, 0)) for at in (p, slots + p, 2 * slots)]
                stays = col >= half
            r.held_out[3 * number + 1] = jnp.int32(k)
            r.held_out[3 * number + 2] = row
            r.held_out[3 * number + 3] = col
            number = number + ((p < count) & stays).astype(jnp.int32)
        r.held_out[0] = number
        held = r.held_out
    else:
        held = r.held
    number = held[0]

    for i, s in enumerate(ahead):
        height = r.own.shape[-2]
        halo = transmit(*unpack(*halves(0, i * height, height)))
        for c in range(2):
            r.tiles[i, 0, c] = r.own[s, c]
            r.tiles[i, 1, c] = halo[c]
            r.tiles[i, 2, c] = jnp.full((height, size), 1.0 - c, jnp.float32)
    if top:
        begin = len(ahead) * r.own.shape[-2]
        for p in range(slots):
            r.amps_all[p] = r.amps[p].astype(jnp.float32)
            r.amps_all[slots + p] = halves(0, begin + p * size, size)[1]
    if back:
        r.grads[...] = jnp.zeros_like(r.grads)
    if 0 in back:
        r.total[...] = jnp.zeros_like(r.total)

    def load(ref, *lead):
        return [(ref[(*lead, m, slice(None), slice(0, size))], ref[(*lead, m, slice(None), slice(size, None))]) for m in range(modes)]

    def store(ref, waves, *lead):
        for m, (re, im) in enumerate(waves):
            ref[(*lead, m, slice(None), slice(0, size))] = re
            ref[(*lead, m, slice(None), slice(size, None))] = im

    def psi(s, at):
        return load(r.psi_0) if s == 0 else load(r.get("psi_%d" % s), at)

    def trans(s, at):
        ref = r.get("trans_%d" % s)
        return ref[at, 0], ref[at, 1]

    def slot_step(at, misfit):
        k = held[3 * at + 1]
        row = held[3 * at + 2]
        col = held[3 * at + 3]
        own = k < slots
        left = jnp.where(own, 0, 1)
        right = jnp.where(own, jnp.where(last, 2, 1), 0)
        turn = lax.rem(size - col, size)
        inside = lanes >= col
        for i, s in enumerate(ahead):
            for c in range(2):
                both = jnp.where(inside, r.tiles[i, left, c, pl.ds(row, size), :], r.tiles[i, right, c, pl.ds(row, size), :])
                r.get("trans_%d" % s)[at, c] = pltpu.roll(both, turn, 1)
            waves = [mul(trans(s, at), w) for w in psi(s, at)]
            if top and s == ahead[-1]:
                waves = transform(waves, r.tables[0], r.tables[4])
            else:
                waves = transform(waves, r.tables[2], r.tables[6])
                store(r.get("psi_%d" % (s + 1)), waves, at)
        if top:
            inten = sum(re * re + im * im for re, im in waves)
            model = jnp.sqrt(inten + REG)
            observed = r.amps_all[k]
            diff = model - observed
            misfit = misfit + jnp.sum(diff * diff, axis=0, keepdims=True)
            ratio = 1.0 - observed / model
            waves = transform([(ratio * re, ratio * im) for re, im in waves], r.tables[1], r.tables[5])
        elif back:
            waves = load(r.wave_in, at)
        for i, s in enumerate(back):
            waves = [mulc(trans(s, at), w) for w in waves]
            quot = [mulc(a, w) for a, w in zip(psi(s, at), waves)]
            values = sum(im for _, im in quot), -sum(re for re, _ in quot)
            for c in range(2):
                turned = pltpu.roll(values[c], col, 1)
                r.grads[i, left, c, pl.ds(row, size), :] += jnp.where(inside, turned, 0.0)
                r.grads[i, right, c, pl.ds(row, size), :] += jnp.where(inside, 0.0, turned)
            if s > 0:
                waves = transform(waves, r.tables[3], r.tables[7])
        if 0 in back:
            for m, (re, im) in enumerate(waves):
                r.total[m, :, :size] += re
                r.total[m, :, size:] += im
        elif back or top:
            store(r.wave_out, waves, at)
        return misfit

    misfit = lax.fori_loop(0, number, slot_step, jnp.zeros((1, size), jnp.float32))
    if top:
        value = jnp.sum(misfit, axis=1, keepdims=True)
        lane = lax.broadcasted_iota(jnp.int32, (1, 1, size), 2)
        count = r.count[0].astype(jnp.float32)
        value = jnp.where(lane == 0, value[None], jnp.where(lane == 1, count, 0.0))
        r.sums[...] = jnp.broadcast_to(value[0], r.sums.shape)
    for i, s in enumerate(back):
        r.grad[i] = r.grads[i, 0]
        lows, highs = pack((r.grads[i, 1, 0], r.grads[i, 1, 1]))
        height = lows.shape[0]
        r.for_even[i * height : (i + 1) * height] = jnp.where(even, lows, highs)
        r.for_odd[i * height : (i + 1) * height] = jnp.where(even, highs, lows)
    if 0 in back:
        part = r.total.shape[1] // pieces
        sums = r.sums_in[...]
        for k in range(pieces):
            for m in range(modes):
                r.share[k, m * part : (m + 1) * part] = r.total[m, k * part : (k + 1) * part, :]
            r.share[k, modes * part :] = jnp.concatenate([sums, sums], 1)


def stage(given, made, scratch, ahead, top, back, pieces, name):
    names = [n for n, _, _ in given] + [n for n, _ in made] + [n for n, _ in scratch]
    out = pl.pallas_call(
        functools.partial(stage_kernel, names, ahead, top, back, pieces),
        out_shape=[jax.ShapeDtypeStruct(shape, jnp.float32) for _, shape in made],
        in_specs=[SMEM if small else VMEM for _, _, small in given],
        out_specs=[VMEM] * len(made),
        scratch_shapes=[x for _, x in scratch],
        compiler_params=pltpu.CompilerParams(vmem_limit_bytes=24 * 2**20),
        cost_estimate=pl.CostEstimate(flops=(len(ahead) + len(back) + 1) * 10**9, bytes_accessed=10**7, transcendentals=0),
        name=name,
    )(*[x for _, x, _ in given])
    return dict(zip([n for n, _ in made], out))


def finish_kernel(back, modes, me_ref, *refs):
    count = len(back)
    grads, evens, odds = refs[:count], refs[count : 2 * count], refs[2 * count : 3 * count]
    share_in, grad_ref, share_ref = refs[3 * count :]
    even = lax.rem(me_ref[0], 2) == 0
    rows, size = grad_ref.shape[2:]
    part = share_ref.shape[2]
    sums = jnp.sum(share_in[:, modes * part :, :], axis=0)[0:1]
    scale = lax.rsqrt(sums[:, 0:1] / (sums[:, 1:2] * (size * size)) + 1e-06)
    for g, group in enumerate(back):
        for i, s in enumerate(group):
            one, two = evens[g][i * rows : (i + 1) * rows], odds[g][i * rows : (i + 1) * rows]
            arrived = unpack(jnp.where(even, two, one), jnp.where(even, one, two))
            for c in range(2):
                grad_ref[s, c] = (grads[g][i, c] + arrived[c]) * scale
    for m in range(modes):
        share_ref[0, m] = jnp.sum(share_in[:, m * part : (m + 1) * part, :], axis=0) * scale


def total_over(value, axis):
    n = lax.axis_size(axis)
    if n & (n - 1):
        return lax.psum(value, axis)
    step = 1
    while step < n:
        ways = 4 if n // step % 4 == 0 else 2
        value = value + sum(
            lax.ppermute(value, axis, [(i, i ^ (step * k)) for i in range(n)]) for k in range(1, ways)
        )
        step *= ways
    return value


def body(potential, probe, amplitudes, row_offset, col_offset, counts):
    slices, _, rows, size = potential.shape
    modes = probe.shape[1]
    part = probe.shape[2]
    slots = row_offset.shape[-1]
    pieces = lax.axis_size("pos")
    cut = slices // 2
    groups = (tuple(range(cut)), tuple(range(cut, slices)))
    f32 = jnp.float32
    me = lax.axis_index("pos").astype(jnp.int32).reshape(1)
    here = [row_offset[0, 0], col_offset[0, 0], counts[0]]

    def exchange(value, first):
        edges = [(i, i + 1) for i in range(first, pieces - 1, 2)]
        return lax.ppermute(value, "pos", edges + [(j, i) for i, j in edges])

    def call(kernel, given, out, name, scratch=(), flops=0):
        return pl.pallas_call(
            kernel,
            out_shape=[x[0] if isinstance(x, tuple) else x for x in out],
            in_specs=[SMEM if jnp.issubdtype(x.dtype, jnp.integer) else VMEM for x in given],
            out_specs=[SMEM if jnp.issubdtype(x.dtype, jnp.integer) else VMEM for x in out],
            scratch_shapes=list(scratch),
            compiler_params=pltpu.CompilerParams(vmem_limit_bytes=24 * 2**20),
            cost_estimate=pl.CostEstimate(flops=flops, bytes_accessed=10**6, transcendentals=0),
            name=name,
        )(*given)

    def array(shape, dtype=f32):
        return jax.ShapeDtypeStruct(shape, dtype)

    def stage(given, made, scratch, ahead, top, back, name):
        given = dict(me=me, rows=here[0], cols=here[1], count=here[2], tables=tables_here, **given)
        scratch = dict(modes_ref=pltpu.SMEM((modes,), jnp.int32), **scratch)
        names = list(given) + list(made) + list(scratch)
        kernel = functools.partial(stage_kernel, names, ahead, top, back, pieces)
        flops = (len(ahead) + len(back) + 1) * 2 * 10**9
        return dict(zip(made, call(kernel, list(given.values()), list(made.values()), name, scratch.values(), flops)))

    gathered = lax.all_to_all(jnp.broadcast_to(probe, (pieces,) + probe.shape[1:]), "pos", 0, 0)
    heights = [len(groups[0]) * rows + 8, len(groups[1]) * rows + slots * size]
    packed = call(
        functools.partial(pack_kernel, groups),
        [me, *here, potential, amplitudes[0, 0]],
        [array((heights[i // 2], size)) for i in range(4)],
        "pack",
    )
    came = [exchange(packed[i], i % 2) for i in range(4)]
    trans_own, tables_here, amps, probe_all = call(
        prepare_kernel,
        [potential, jnp.asarray(tables(size)), amplitudes[0, 0], gathered],
        [
            array(potential.shape),
            array((8, 2 * size, 2 * size), jnp.bfloat16),
            array((slots, size, size), jnp.bfloat16),
            array((modes, size, 2 * size)),
        ],
        "prepare",
        flops=10**9,
    )

    wave = (2 * slots, modes, size, 2 * size)
    trans = (2 * slots, 2, size, size)
    tiles = lambda n: pltpu.VMEM((n, 3, 2, rows, size), f32)
    sides = lambda n: dict(grad=array((n, 2, rows, size)), for_even=array((n * rows, size)), for_odd=array((n * rows, size)))

    first, second = groups
    a = stage(
        dict(own=trans_own, across_even=came[0], across_odd=came[1], psi_0=probe_all),
        dict(held_out=array((6 * slots + 4,), jnp.int32))
        | {"psi_%d" % (s + 1): array(wave) for s in first}
        | {"trans_%d" % s: array(trans) for s in first},
        dict(tiles=tiles(len(first))),
        first,
        False,
        (),
        "ahead",
    )
    held = a["held_out"]
    b = stage(
        dict(own=trans_own, across_even=came[2], across_odd=came[3], amps=amps, held=held)
        | {"psi_%d" % second[0]: a["psi_%d" % second[0]]},
        dict(sums=array((8, size)), wave_out=array(wave))
        | {"psi_%d" % s: array(wave) for s in second[1:]}
        | {"trans_%d" % s: array(trans) for s in second},
        dict(tiles=tiles(len(second)), amps_all=pltpu.VMEM((2 * slots, size, size), f32)),
        second,
        True,
        (),
        "top",
    )
    sums = total_over(b["sums"], "group")
    state = a | b | dict(psi_0=probe_all)
    done = []
    back = [(s,) for s in second[::-1]] + [first[::-1]]
    for group in back:
        end = 0 in group
        made = dict(share=array((pieces, modes * part + 8, 2 * size))) if end else dict(wave_out=array(wave))
        scratch = dict(total=pltpu.VMEM(wave[1:], f32)) if end else {}
        d = stage(
            dict(held=held, wave_in=state["wave_out"])
            | {"psi_%d" % s: state["psi_%d" % s] for s in group}
            | {"trans_%d" % s: state["trans_%d" % s] for s in group}
            | (dict(sums_in=sums) if end else {}),
            made | sides(len(group)),
            dict(grads=tiles(len(group))) | scratch,
            (),
            False,
            group,
            "back",
        )
        state = state | d
        done.append(d)
    got = [[exchange(d[name], odd) for d in done] for odd, name in enumerate(("for_even", "for_odd"))]
    (share,) = pl.pallas_call(
        gate_kernel,
        out_shape=[array(state["share"].shape)],
        in_specs=[pl.BlockSpec(memory_space=pl.ANY)] * 3,
        out_specs=[pl.BlockSpec(memory_space=pl.ANY)],
        input_output_aliases={0: 0},
        compiler_params=pltpu.CompilerParams(vmem_limit_bytes=24 * 2**20),
        name="gate",
    )(state["share"], got[0][-2], got[1][-2])
    shares = lax.all_to_all(share, "pos", 0, 0)
    return call(
        functools.partial(finish_kernel, back, modes),
        [me, *[d["grad"] for d in done], *got[0], *got[1], shares],
        [array(potential.shape), array(probe.shape)],
        "finish",
    )


def solution(mesh):
    placed = (
        P(None, None, "group", "pos"),
        P("group", None, "pos", None),
        P("group", "pos", None, None, None),
        P("group", "pos", None),
        P("group", "pos", None),
        P("group", "pos"),
    )
    return jax.shard_map(
        body,
        mesh=mesh,
        in_specs=placed,
        out_specs=(P(None, None, "group", "pos"), P("group", None, "pos", None)),
        check_vma=False,
    )
```

```python
import functools
import math

import jax
import jax.numpy as jnp
import ml_dtypes
import numpy as np
from jax import lax
from jax.experimental import pallas as pl
from jax.experimental.pallas import tpu as pltpu
from jax.sharding import PartitionSpec as P

PROP = 0.25
REG = 0.1
VMEM = pl.BlockSpec(memory_space=pltpu.VMEM)
SMEM = pl.BlockSpec(memory_space=pltpu.SMEM)


@functools.lru_cache(maxsize=None)
def tables(size):
    idx = np.arange(size)
    angle = np.float32(2.0 * math.pi / size) * (idx[:, None] * idx[None, :] % size).astype(np.float32)
    cosv = (np.cos(angle) / np.float32(math.sqrt(size))).astype(ml_dtypes.bfloat16).astype(np.float64)
    sinv = (np.sin(angle) / np.float32(math.sqrt(size))).astype(ml_dtypes.bfloat16).astype(np.float64)
    forward = np.block([[cosv, -sinv], [sinv, cosv]])
    inverse = np.block([[cosv, sinv], [-sinv, cosv]])
    freq = np.where(idx < size // 2, idx, idx - size).astype(np.float64)
    phase = -2.0 * math.pi * PROP / size * freq * freq
    real, imag = np.diag(np.cos(phase)), np.diag(np.sin(phase))
    ahead = forward @ np.block([[real, imag], [-imag, real]]) @ inverse
    behind = forward @ np.block([[real, -imag], [imag, real]]) @ inverse
    rows = np.arange(2 * size).reshape(2, size // 8, 8).swapaxes(0, 1).reshape(-1)
    left = [t.T[rows] for t in (forward, inverse, ahead, behind)]
    return np.stack([forward, inverse, ahead, behind, *left]).astype(ml_dtypes.bfloat16)


def mul(a, b):
    return a[0] * b[0] - a[1] * b[1], a[0] * b[1] + a[1] * b[0]


def mulc(a, b):
    return a[0] * b[0] + a[1] * b[1], a[0] * b[1] - a[1] * b[0]


def sine(x):
    y = x * x
    return x * (1.0 - y * (1 / 6) * (1.0 - y * (1 / 20) * (1.0 - y * (1 / 42) * (1.0 - y * (1 / 72)))))


def cosine(x):
    y = x * x
    return 1.0 - y * 0.5 * (1.0 - y * (1 / 12) * (1.0 - y * (1 / 30) * (1.0 - y * (1 / 56) * (1.0 - y * (1 / 90)))))


def transform(waves, right, left):
    size = waves[0][0].shape[0]
    pairs = [waves[first : first + 2] for first in range(0, len(waves), 2)]
    mids = []
    for pair in pairs:
        rows = jnp.concatenate(
            [jnp.concatenate([re.astype(jnp.bfloat16), im.astype(jnp.bfloat16)], 1) for re, im in pair], 0
        )
        mid = jnp.dot(rows, right, preferred_element_type=jnp.float32).astype(jnp.bfloat16)
        cut = [mid[i * size : (i + 1) * size] for i in range(len(pair))]
        mids.append(jnp.concatenate([jnp.concatenate([m[:, :size], m[:, size:]], 0) for m in cut], 1))
    out = []
    for pair, mid in zip(pairs, mids):
        done = jnp.dot(left, mid, preferred_element_type=jnp.float32)
        done = done.reshape(size // 8, 2, 8, -1)
        parts = [done[:, c].reshape(size, -1) for c in range(2)]
        for i in range(len(pair)):
            out.append(tuple(x[:, i * size : (i + 1) * size] for x in parts))
    return out


def split_kernel(potential_ref, *refs):
    at = 0
    for ref in refs:
        ref[...] = potential_ref[at : at + ref.shape[0]]
        at += ref.shape[0]


def transmit(phase, absorption):
    magnitude = jnp.exp(-absorption)
    return magnitude * cosine(phase), magnitude * sine(phase)


def gate_kernel(*refs):
    pass


def prepare_kernel(potential_ref, tables_ref, amps_ref, pieces_ref, trans_ref, tables_out, amps_out, probe_ref):
    part = pieces_ref.shape[2]
    for k in range(pieces_ref.shape[0]):
        probe_ref[:, k * part : (k + 1) * part, :] = pieces_ref[k]
    for s in range(potential_ref.shape[0]):
        trans_ref[s, 0], trans_ref[s, 1] = transmit(potential_ref[s, 0], potential_ref[s, 1])
    tables_out[...] = tables_ref[...]
    amps_out[...] = amps_ref[...]


class Names:
    def __init__(self, names, refs):
        self.__dict__.update(zip(names, refs))

    def get(self, name):
        return self.__dict__[name]


def stage_kernel(names, ahead, top, back, pieces, *refs):
    r = Names(names, refs)
    size = r.tables.shape[-1] // 2
    modes = r.modes_ref.shape[0]
    lanes = lax.broadcasted_iota(jnp.int32, (size, size), 1)
    for i, s in enumerate(ahead):
        r.tiles[i, 0, 0], r.tiles[i, 0, 1] = r.own[s, 0], r.own[s, 1]
        r.tiles[i, 1, 0], r.tiles[i, 1, 1] = transmit(r.beyond[i, 0], r.beyond[i, 1])
    if back:
        r.grads[...] = jnp.zeros_like(r.grads)
    if 0 in back:
        r.total[...] = jnp.zeros_like(r.total)

    def load(ref, *lead):
        return [(ref[(*lead, m, slice(None), slice(0, size))], ref[(*lead, m, slice(None), slice(size, None))]) for m in range(modes)]

    def store(ref, waves, *lead):
        for m, (re, im) in enumerate(waves):
            ref[(*lead, m, slice(None), slice(0, size))] = re
            ref[(*lead, m, slice(None), slice(size, None))] = im

    def psi(s, at):
        return load(r.psi_0) if s == 0 else load(r.get("psi_%d" % s), at)

    def trans(s, at):
        ref = r.get("trans_%d" % s)
        return ref[at, 0], ref[at, 1]

    def slot_step(at, misfit):
        row, col = r.rows[at], r.cols[at]
        turn = lax.rem(size - col, size)
        inside = lanes >= col
        for i, s in enumerate(ahead):
            for c in range(2):
                both = jnp.where(inside, r.tiles[i, 0, c, pl.ds(row, size), :], r.tiles[i, 1, c, pl.ds(row, size), :])
                r.get("trans_%d" % s)[at, c] = pltpu.roll(both, turn, 1)
            waves = [mul(trans(s, at), w) for w in psi(s, at)]
            if top and s == ahead[-1]:
                waves = transform(waves, r.tables[0], r.tables[4])
            else:
                waves = transform(waves, r.tables[2], r.tables[6])
                store(r.get("psi_%d" % (s + 1)), waves, at)
        if top:
            inten = sum(re * re + im * im for re, im in waves)
            model = jnp.sqrt(inten + REG)
            observed = r.amps[at].astype(jnp.float32)
            diff = model - observed
            misfit = misfit + jnp.sum(diff * diff, axis=0, keepdims=True)
            ratio = 1.0 - observed / model
            waves = transform([(ratio * re, ratio * im) for re, im in waves], r.tables[1], r.tables[5])
        elif back:
            waves = load(r.wave_in, at)
        for i, s in enumerate(back):
            waves = [mulc(trans(s, at), w) for w in waves]
            quot = [mulc(a, w) for a, w in zip(psi(s, at), waves)]
            values = sum(im for _, im in quot), -sum(re for re, _ in quot)
            for c in range(2):
                turned = pltpu.roll(values[c], col, 1)
                r.grads[i, 0, c, pl.ds(row, size), :] += jnp.where(inside, turned, 0.0)
                r.grads[i, 1, c, pl.ds(row, size), :] += jnp.where(inside, 0.0, turned)
            if s > 0:
                waves = transform(waves, r.tables[3], r.tables[7])
        if 0 in back:
            for m, (re, im) in enumerate(waves):
                r.total[m, :, :size] += re
                r.total[m, :, size:] += im
        elif back or top:
            store(r.wave_out, waves, at)
        return misfit

    misfit = lax.fori_loop(0, r.count[0], slot_step, jnp.zeros((1, size), jnp.float32))
    if top:
        value = jnp.sum(misfit, axis=1, keepdims=True)
        lane = lax.broadcasted_iota(jnp.int32, (1, 1, size), 2)
        count = r.count[0].astype(jnp.float32)
        value = jnp.where(lane == 0, value[None], jnp.where(lane == 1, count, 0.0))
        r.sums[...] = jnp.broadcast_to(value[0], r.sums.shape)
    for i, s in enumerate(back):
        r.grad[i] = r.grads[i, 0]
        r.spill[i] = r.grads[i, 1]
    if 0 in back:
        r.early[...] = r.early_own[...] + r.early_in[...]
        part = r.total.shape[1] // pieces
        for k in range(pieces):
            at = pl.multiple_of(lax.rem(r.me[0] + k, pieces) * part, part)
            share = r.get("share_%d" % k)
            for m in range(modes):
                share[m * part : (m + 1) * part] = r.total[m, pl.ds(at, part), :]
            share[modes * part :] = jnp.concatenate([r.sums_in[...], r.sums_in[...]], 1)


def finish_kernel(back, modes, early_ref, *refs):
    count = len(back)
    grads, spills, (*shares, grad_ref, share_ref) = refs[:count], refs[count : 2 * count], refs[2 * count :]
    size = grad_ref.shape[-1]
    part = share_ref.shape[2]
    share = sum(ref[...] for ref in shares)
    sums = share[modes * part : modes * part + 1]
    scale = lax.rsqrt(sums[:, 0:1] / (sums[:, 1:2] * (size * size)) + 1e-06)
    for c in range(2):
        grad_ref[grad_ref.shape[0] - 1, c] = early_ref[0, c] * scale
    for g, group in enumerate(back):
        for i, s in enumerate(group):
            for c in range(2):
                grad_ref[s, c] = (grads[g][i, c] + spills[g][i, c]) * scale
    for m in range(modes):
        share_ref[0, m] = share[m * part : (m + 1) * part] * scale


def total_over(value, axis):
    n = lax.axis_size(axis)
    if n & (n - 1):
        return lax.psum(value, axis)
    step = 1
    while step < n:
        ways = 4 if n // step % 4 == 0 else 2
        value = value + sum(
            lax.ppermute(value, axis, [(i, i ^ (step * k)) for i in range(n)]) for k in range(1, ways)
        )
        step *= ways
    return value


def body(potential, probe, amplitudes, row_offset, col_offset, counts):
    slices, _, rows, size = potential.shape
    modes = probe.shape[1]
    part = probe.shape[2]
    slots = row_offset.shape[-1]
    pieces = lax.axis_size("pos")
    cut = slices // 2
    groups = (tuple(range(cut)), tuple(range(cut, slices)))
    f32 = jnp.float32
    me = lax.axis_index("pos").astype(jnp.int32).reshape(1)
    here = [row_offset[0, 0], col_offset[0, 0], counts[0]]

    to_left = [(i + 1, i) for i in range(pieces - 1)]
    to_right = [(i, i + 1) for i in range(pieces - 1)]

    def call(kernel, given, out, name, scratch=(), flops=0):
        return pl.pallas_call(
            kernel,
            out_shape=[x[0] if isinstance(x, tuple) else x for x in out],
            in_specs=[SMEM if jnp.issubdtype(x.dtype, jnp.integer) else VMEM for x in given],
            out_specs=[SMEM if jnp.issubdtype(x.dtype, jnp.integer) else VMEM for x in out],
            scratch_shapes=list(scratch),
            compiler_params=pltpu.CompilerParams(vmem_limit_bytes=24 * 2**20),
            cost_estimate=pl.CostEstimate(flops=flops, bytes_accessed=10**6, transcendentals=0),
            name=name,
        )(*given)

    def array(shape, dtype=f32):
        return jax.ShapeDtypeStruct(shape, dtype)

    def stage(given, made, scratch, ahead, top, back, name):
        given = dict(me=me, rows=here[0], cols=here[1], count=here[2], tables=tables_here, **given)
        scratch = dict(modes_ref=pltpu.SMEM((modes,), jnp.int32), **scratch)
        names = list(given) + list(made) + list(scratch)
        kernel = functools.partial(stage_kernel, names, ahead, top, back, pieces)
        flops = (len(ahead) + len(back) + 1) * 2 * 10**9
        return dict(zip(made, call(kernel, list(given.values()), list(made.values()), name, scratch.values(), flops)))

    def gate(values, after):
        anywhere = pl.BlockSpec(memory_space=pl.ANY)
        return pl.pallas_call(
            gate_kernel,
            out_shape=[array(x.shape) for x in values],
            in_specs=[anywhere] * (len(values) + len(after)),
            out_specs=[anywhere] * len(values),
            input_output_aliases={i: i for i in range(len(values))},
            compiler_params=pltpu.CompilerParams(vmem_limit_bytes=2**20),
            name="gate",
        )(*values, *after)

    gathered = lax.all_to_all(jnp.broadcast_to(probe, (pieces,) + probe.shape[1:]), "pos", 0, 0)
    halves = call(split_kernel, [potential], [array((len(g), 2, rows, size)) for g in groups], "split")
    halves = [halves[0], *gate(halves[1:], [gathered])]
    beyond = [lax.ppermute(half, "pos", to_left) for half in halves]
    trans_own, tables_here, amps, probe_all = call(
        prepare_kernel,
        [potential, jnp.asarray(tables(size)), amplitudes[0, 0], gathered],
        [
            array(potential.shape),
            array((8, 2 * size, 2 * size), jnp.bfloat16),
            array((slots, size, size), jnp.bfloat16),
            array((modes, size, 2 * size)),
        ],
        "prepare",
        flops=10**9,
    )

    wave = (slots, modes, size, 2 * size)
    trans = (slots, 2, size, size)
    tiles = lambda n: pltpu.VMEM((n, 2, 2, rows, size), f32)
    sides = lambda n: dict(grad=array((n, 2, rows, size)), spill=array((n, 2, rows, size)))

    first, second = groups
    a = stage(
        dict(own=trans_own, beyond=beyond[0], psi_0=probe_all),
        {"psi_%d" % (s + 1): array(wave) for s in first}
        | {"trans_%d" % s: array(trans) for s in first},
        dict(tiles=tiles(len(first))),
        first,
        False,
        (),
        "ahead",
    )
    b = stage(
        dict(own=trans_own, beyond=beyond[1], amps=amps)
        | {"psi_%d" % second[0]: a["psi_%d" % second[0]]},
        dict(sums=array((8, size)), wave_out=array(wave))
        | {"psi_%d" % s: array(wave) for s in second[1:]}
        | {"trans_%d" % s: array(trans) for s in second},
        dict(tiles=tiles(len(second))),
        second,
        True,
        (),
        "top",
    )
    sums = total_over(b["sums"], "group")
    state = a | b | dict(psi_0=probe_all)
    done = []
    back = [(s,) for s in reversed(range(slices))]
    for group in back:
        end = 0 in group
        made = {"share_%d" % k: array((modes * part + 8, 2 * size)) for k in range(pieces)} if end else dict(wave_out=array(wave))
        if end:
            made["early"] = array((1, 2, rows, size))
            arrived = lax.ppermute(done[0]["spill"], "pos", to_right)
        scratch = dict(total=pltpu.VMEM(wave[1:], f32)) if end else {}
        d = stage(
            dict(wave_in=state["wave_out"])
            | {"psi_%d" % s: state["psi_%d" % s] for s in group}
            | {"trans_%d" % s: state["trans_%d" % s] for s in group}
            | (dict(sums_in=sums, early_own=done[0]["grad"], early_in=arrived) if end else {}),
            made | sides(len(group)),
            dict(grads=tiles(len(group))) | scratch,
            (),
            False,
            group,
            "back",
        )
        state = state | d
        done.append(d)
    spills = [lax.ppermute(d["spill"], "pos", to_right) for d in done[1:]]
    shares = [state["share_%d" % k] for k in range(pieces)]
    for k in range(1, pieces):
        shares[k] = lax.ppermute(shares[k], "pos", [(i, (i + k) % pieces) for i in range(pieces)])
    return call(
        functools.partial(finish_kernel, back[1:], modes),
        [state["early"], *[d["grad"] for d in done[1:]], *spills, *shares],
        [array(potential.shape), array(probe.shape)],
        "finish",
    )


def solution(mesh):
    placed = (
        P(None, None, "group", "pos"),
        P("group", None, "pos", None),
        P("group", "pos", None, None, None),
        P("group", "pos", None),
        P("group", "pos", None),
        P("group", "pos"),
    )
    return jax.shard_map(
        body,
        mesh=mesh,
        in_specs=placed,
        out_specs=(P(None, None, "group", "pos"), P("group", None, "pos", None)),
        check_vma=False,
    )
```

```python
import functools
import math

import jax
import jax.numpy as jnp
import ml_dtypes
import numpy as np
from jax import lax
from jax.experimental import pallas as pl
from jax.experimental.pallas import tpu as pltpu
from jax.sharding import PartitionSpec as P

PROP = 0.25
REG = 0.1
VMEM = pl.BlockSpec(memory_space=pltpu.VMEM)
SMEM = pl.BlockSpec(memory_space=pltpu.SMEM)


@functools.lru_cache(maxsize=None)
def tables(size):
    idx = np.arange(size)
    angle = np.float32(2.0 * math.pi / size) * (idx[:, None] * idx[None, :] % size).astype(np.float32)
    cosv = (np.cos(angle) / np.float32(math.sqrt(size))).astype(ml_dtypes.bfloat16).astype(np.float64)
    sinv = (np.sin(angle) / np.float32(math.sqrt(size))).astype(ml_dtypes.bfloat16).astype(np.float64)
    forward = np.block([[cosv, -sinv], [sinv, cosv]])
    inverse = np.block([[cosv, sinv], [-sinv, cosv]])
    freq = np.where(idx < size // 2, idx, idx - size).astype(np.float64)
    phase = -2.0 * math.pi * PROP / size * freq * freq
    real, imag = np.diag(np.cos(phase)), np.diag(np.sin(phase))
    ahead = forward @ np.block([[real, imag], [-imag, real]]) @ inverse
    behind = forward @ np.block([[real, -imag], [imag, real]]) @ inverse
    rows = np.arange(2 * size).reshape(2, size // 8, 8).swapaxes(0, 1).reshape(-1)
    left = [t.T[rows] for t in (forward, inverse, ahead, behind)]
    return np.stack([forward, inverse, ahead, behind, *left]).astype(ml_dtypes.bfloat16)


def mul(a, b):
    return a[0] * b[0] - a[1] * b[1], a[0] * b[1] + a[1] * b[0]


def mulc(a, b):
    return a[0] * b[0] + a[1] * b[1], a[0] * b[1] - a[1] * b[0]


def sine(x):
    y = x * x
    return x * (1.0 - y * (1 / 6) * (1.0 - y * (1 / 20) * (1.0 - y * (1 / 42) * (1.0 - y * (1 / 72)))))


def cosine(x):
    y = x * x
    return 1.0 - y * 0.5 * (1.0 - y * (1 / 12) * (1.0 - y * (1 / 30) * (1.0 - y * (1 / 56) * (1.0 - y * (1 / 90)))))


def transform(waves, right, left):
    size = waves[0][0].shape[0]
    pairs = [waves[first : first + 2] for first in range(0, len(waves), 2)]
    mids = []
    for pair in pairs:
        rows = jnp.concatenate(
            [jnp.concatenate([re.astype(jnp.bfloat16), im.astype(jnp.bfloat16)], 1) for re, im in pair], 0
        )
        mid = jnp.dot(rows, right, preferred_element_type=jnp.float32).astype(jnp.bfloat16)
        cut = [mid[i * size : (i + 1) * size] for i in range(len(pair))]
        mids.append(jnp.concatenate([jnp.concatenate([m[:, :size], m[:, size:]], 0) for m in cut], 1))
    out = []
    for pair, mid in zip(pairs, mids):
        done = jnp.dot(left, mid, preferred_element_type=jnp.float32)
        done = done.reshape(size // 8, 2, 8, -1)
        parts = [done[:, c].reshape(size, -1) for c in range(2)]
        for i in range(len(pair)):
            out.append(tuple(x[:, i * size : (i + 1) * size] for x in parts))
    return out


def split_kernel(potential_ref, *refs):
    at = 0
    for ref in refs:
        ref[...] = potential_ref[at : at + ref.shape[0]]
        at += ref.shape[0]


def transmit(phase, absorption):
    magnitude = jnp.exp(-absorption)
    return magnitude * cosine(phase), magnitude * sine(phase)


def gate_kernel(*refs):
    pass


def prepare_kernel(potential_ref, tables_ref, amps_ref, pieces_ref, trans_ref, tables_out, amps_out, probe_ref):
    part = pieces_ref.shape[2]
    for k in range(pieces_ref.shape[0]):
        probe_ref[:, k * part : (k + 1) * part, :] = pieces_ref[k]
    for s in range(potential_ref.shape[0]):
        trans_ref[s, 0], trans_ref[s, 1] = transmit(potential_ref[s, 0], potential_ref[s, 1])
    tables_out[...] = tables_ref[...]
    amps_out[...] = amps_ref[...]


class Names:
    def __init__(self, names, refs):
        self.__dict__.update(zip(names, refs))

    def get(self, name):
        return self.__dict__[name]


def stage_kernel(names, ahead, top, back, pieces, *refs):
    r = Names(names, refs)
    size = r.tables.shape[-1] // 2
    modes = r.modes_ref.shape[0]
    lanes = lax.broadcasted_iota(jnp.int32, (size, size), 1)
    for i, s in enumerate(ahead):
        r.tiles[i, 0, 0], r.tiles[i, 0, 1] = r.own[s, 0], r.own[s, 1]
        r.tiles[i, 1, 0], r.tiles[i, 1, 1] = transmit(r.beyond[i, 0], r.beyond[i, 1])
    if back:
        r.grads[...] = jnp.zeros_like(r.grads)
    if 0 in back:
        r.total[...] = jnp.zeros_like(r.total)

    def load(ref, *lead):
        return [(ref[(*lead, m, slice(None), slice(0, size))], ref[(*lead, m, slice(None), slice(size, None))]) for m in range(modes)]

    def store(ref, waves, *lead):
        for m, (re, im) in enumerate(waves):
            ref[(*lead, m, slice(None), slice(0, size))] = re
            ref[(*lead, m, slice(None), slice(size, None))] = im

    def psi(s, at):
        return load(r.psi_0) if s == 0 else load(r.get("psi_%d" % s), at)

    def trans(s, at):
        ref = r.get("trans_%d" % s)
        return ref[at, 0], ref[at, 1]

    def slot_step(at, misfit):
        row, col = r.rows[at], r.cols[at]
        turn = lax.rem(size - col, size)
        inside = lanes >= col
        for i, s in enumerate(ahead):
            for c in range(2):
                both = jnp.where(inside, r.tiles[i, 0, c, pl.ds(row, size), :], r.tiles[i, 1, c, pl.ds(row, size), :])
                r.get("trans_%d" % s)[at, c] = pltpu.roll(both, turn, 1)
            waves = [mul(trans(s, at), w) for w in psi(s, at)]
            if top and s == ahead[-1]:
                waves = transform(waves, r.tables[0], r.tables[4])
            else:
                waves = transform(waves, r.tables[2], r.tables[6])
                store(r.get("psi_%d" % (s + 1)), waves, at)
        if top:
            inten = sum(re * re + im * im for re, im in waves)
            model = jnp.sqrt(inten + REG)
            observed = r.amps[at].astype(jnp.float32)
            diff = model - observed
            misfit = misfit + jnp.sum(diff * diff, axis=0, keepdims=True)
            ratio = 1.0 - observed / model
            waves = transform([(ratio * re, ratio * im) for re, im in waves], r.tables[1], r.tables[5])
        elif back:
            waves = load(r.wave_in, at)
        for i, s in enumerate(back):
            waves = [mulc(trans(s, at), w) for w in waves]
            quot = [mulc(a, w) for a, w in zip(psi(s, at), waves)]
            values = sum(im for _, im in quot), -sum(re for re, _ in quot)
            for c in range(2):
                turned = pltpu.roll(values[c], col, 1)
                r.grads[i, 0, c, pl.ds(row, size), :] += jnp.where(inside, turned, 0.0)
                r.grads[i, 1, c, pl.ds(row, size), :] += jnp.where(inside, 0.0, turned)
            if s > 0:
                waves = transform(waves, r.tables[3], r.tables[7])
        if 0 in back:
            for m, (re, im) in enumerate(waves):
                r.total[m, :, :size] += re
                r.total[m, :, size:] += im
        elif back or top:
            store(r.wave_out, waves, at)
        return misfit

    misfit = lax.fori_loop(0, r.count[0], slot_step, jnp.zeros((1, size), jnp.float32))
    if top:
        value = jnp.sum(misfit, axis=1, keepdims=True)
        lane = lax.broadcasted_iota(jnp.int32, (1, 1, size), 2)
        count = r.count[0].astype(jnp.float32)
        value = jnp.where(lane == 0, value[None], jnp.where(lane == 1, count, 0.0))
        r.sums[...] = jnp.broadcast_to(value[0], r.sums.shape)
    for i, s in enumerate(back):
        r.grad[i] = r.grads[i, 0]
        r.spill[i] = r.grads[i, 1]
    if 0 in back:
        part = r.total.shape[1] // pieces
        for k in range(pieces):
            for m in range(modes):
                r.share[k, m * part : (m + 1) * part] = r.total[m, k * part : (k + 1) * part, :]
            r.share[k, modes * part :] = jnp.concatenate([r.sums_in[...], r.sums_in[...]], 1)


def finish_kernel(back, modes, *refs):
    count = len(back)
    grads, spills, (share_in, sums_ref, grad_ref, share_ref) = refs[:count], refs[count : 2 * count], refs[2 * count :]
    size = grad_ref.shape[-1]
    part = share_ref.shape[2]
    sums = sums_ref[0:1]
    scale = lax.rsqrt(sums[:, 0:1] / (sums[:, 1:2] * (size * size)) + 1e-06)
    for g, group in enumerate(back):
        for i, s in enumerate(group):
            for c in range(2):
                grad_ref[s, c] = (grads[g][i, c] + spills[g][i, c]) * scale
    for m in range(modes):
        share_ref[0, m] = jnp.sum(share_in[:, m * part : (m + 1) * part, :], axis=0) * scale


def total_over(value, axis):
    n = lax.axis_size(axis)
    if n & (n - 1):
        return lax.psum(value, axis)
    step = 1
    while step < n:
        ways = 4 if n // step % 4 == 0 else 2
        value = value + sum(
            lax.ppermute(value, axis, [(i, i ^ (step * k)) for i in range(n)]) for k in range(1, ways)
        )
        step *= ways
    return value


def body(potential, probe, amplitudes, row_offset, col_offset, counts):
    slices, _, rows, size = potential.shape
    modes = probe.shape[1]
    part = probe.shape[2]
    slots = row_offset.shape[-1]
    pieces = lax.axis_size("pos")
    cut = slices // 2
    groups = (tuple(range(cut)), tuple(range(cut, slices)))
    f32 = jnp.float32
    me = lax.axis_index("pos").astype(jnp.int32).reshape(1)
    here = [row_offset[0, 0], col_offset[0, 0], counts[0]]

    to_left = [(i + 1, i) for i in range(pieces - 1)]
    to_right = [(i, i + 1) for i in range(pieces - 1)]

    def call(kernel, given, out, name, scratch=(), flops=0):
        return pl.pallas_call(
            kernel,
            out_shape=[x[0] if isinstance(x, tuple) else x for x in out],
            in_specs=[SMEM if jnp.issubdtype(x.dtype, jnp.integer) else VMEM for x in given],
            out_specs=[SMEM if jnp.issubdtype(x.dtype, jnp.integer) else VMEM for x in out],
            scratch_shapes=list(scratch),
            compiler_params=pltpu.CompilerParams(vmem_limit_bytes=24 * 2**20),
            cost_estimate=pl.CostEstimate(flops=flops, bytes_accessed=10**6, transcendentals=0),
            name=name,
        )(*given)

    def array(shape, dtype=f32):
        return jax.ShapeDtypeStruct(shape, dtype)

    def stage(given, made, scratch, ahead, top, back, name):
        given = dict(me=me, rows=here[0], cols=here[1], count=here[2], tables=tables_here, **given)
        scratch = dict(modes_ref=pltpu.SMEM((modes,), jnp.int32), **scratch)
        names = list(given) + list(made) + list(scratch)
        kernel = functools.partial(stage_kernel, names, ahead, top, back, pieces)
        flops = (len(ahead) + len(back) + 1) * 2 * 10**9
        return dict(zip(made, call(kernel, list(given.values()), list(made.values()), name, scratch.values(), flops)))

    def gate(values, after):
        anywhere = pl.BlockSpec(memory_space=pl.ANY)
        return pl.pallas_call(
            gate_kernel,
            out_shape=[array(x.shape) for x in values],
            in_specs=[anywhere] * (len(values) + len(after)),
            out_specs=[anywhere] * len(values),
            input_output_aliases={i: i for i in range(len(values))},
            compiler_params=pltpu.CompilerParams(vmem_limit_bytes=2**20),
            name="gate",
        )(*values, *after)

    gathered = lax.all_to_all(jnp.broadcast_to(probe, (pieces,) + probe.shape[1:]), "pos", 0, 0)
    halves = call(split_kernel, [potential], [array((len(g), 2, rows, size)) for g in groups], "split")
    halves = [halves[0], *gate(halves[1:], [gathered])]
    beyond = [lax.ppermute(half, "pos", to_left) for half in halves]
    trans_own, tables_here, amps, probe_all = call(
        prepare_kernel,
        [potential, jnp.asarray(tables(size)), amplitudes[0, 0], gathered],
        [
            array(potential.shape),
            array((8, 2 * size, 2 * size), jnp.bfloat16),
            array((slots, size, size), jnp.bfloat16),
            array((modes, size, 2 * size)),
        ],
        "prepare",
        flops=10**9,
    )

    wave = (slots, modes, size, 2 * size)
    trans = (slots, 2, size, size)
    tiles = lambda n: pltpu.VMEM((n, 2, 2, rows, size), f32)
    sides = lambda n: dict(grad=array((n, 2, rows, size)), spill=array((n, 2, rows, size)))

    first, second = groups
    a = stage(
        dict(own=trans_own, beyond=beyond[0], psi_0=probe_all),
        {"psi_%d" % (s + 1): array(wave) for s in first}
        | {"trans_%d" % s: array(trans) for s in first},
        dict(tiles=tiles(len(first))),
        first,
        False,
        (),
        "ahead",
    )
    b = stage(
        dict(own=trans_own, beyond=beyond[1], amps=amps) | {"psi_%d" % second[0]: a["psi_%d" % second[0]]},
        dict(sums=array((8, size)), wave_out=array(wave)) | sides(len(second)),
        dict(tiles=tiles(len(second)), grads=tiles(len(second)))
        | {"psi_%d" % s: pltpu.VMEM(wave, f32) for s in second[1:]}
        | {"trans_%d" % s: pltpu.VMEM(trans, f32) for s in second},
        second,
        True,
        second[::-1],
        "top",
    )
    c = stage(
        dict(wave_in=b["wave_out"], sums_in=b["sums"])
        | {"psi_%d" % s: probe_all if s == 0 else a["psi_%d" % s] for s in first}
        | {"trans_%d" % s: a["trans_%d" % s] for s in first},
        dict(share=array((pieces, modes * part + 8, 2 * size))) | sides(len(first)),
        dict(grads=tiles(len(first)), total=pltpu.VMEM(wave[1:], f32)),
        (),
        False,
        first[::-1],
        "back",
    )
    spills = [lax.ppermute(d["spill"], "pos", to_right) for d in (b, c)]
    shares = lax.all_to_all(c["share"], "pos", 0, 0)
    sums = total_over(jnp.sum(shares[:, modes * part :, :size], axis=0), "group")
    return call(
        functools.partial(finish_kernel, (second[::-1], first[::-1]), modes),
        [b["grad"], c["grad"], *spills, shares, sums],
        [array(potential.shape), array(probe.shape)],
        "finish",
    )


def solution(mesh):
    placed = (
        P(None, None, "group", "pos"),
        P("group", None, "pos", None),
        P("group", "pos", None, None, None),
        P("group", "pos", None),
        P("group", "pos", None),
        P("group", "pos"),
    )
    return jax.shard_map(
        body,
        mesh=mesh,
        in_specs=placed,
        out_specs=(P(None, None, "group", "pos"), P("group", None, "pos", None)),
        check_vma=False,
    )
```

```python
import functools
import math

import jax
import jax.numpy as jnp
import ml_dtypes
import numpy as np
from jax import lax
from jax.experimental import pallas as pl
from jax.experimental.pallas import tpu as pltpu
from jax.sharding import PartitionSpec as P

PROP = 0.25
REG = 0.1
VMEM = pl.BlockSpec(memory_space=pltpu.VMEM)
SMEM = pl.BlockSpec(memory_space=pltpu.SMEM)


@functools.lru_cache(maxsize=None)
def tables(size):
    idx = np.arange(size)
    angle = np.float32(2.0 * math.pi / size) * (idx[:, None] * idx[None, :] % size).astype(np.float32)
    cosv = (np.cos(angle) / np.float32(math.sqrt(size))).astype(ml_dtypes.bfloat16).astype(np.float64)
    sinv = (np.sin(angle) / np.float32(math.sqrt(size))).astype(ml_dtypes.bfloat16).astype(np.float64)
    forward = np.block([[cosv, -sinv], [sinv, cosv]])
    inverse = np.block([[cosv, sinv], [-sinv, cosv]])
    freq = np.where(idx < size // 2, idx, idx - size).astype(np.float64)
    phase = -2.0 * math.pi * PROP / size * freq * freq
    real, imag = np.diag(np.cos(phase)), np.diag(np.sin(phase))
    ahead = forward @ np.block([[real, imag], [-imag, real]]) @ inverse
    behind = forward @ np.block([[real, -imag], [imag, real]]) @ inverse
    rows = np.arange(2 * size).reshape(2, size // 8, 8).swapaxes(0, 1).reshape(-1)
    left = [t.T[rows] for t in (forward, inverse, ahead, behind)]
    return np.stack([forward, inverse, ahead, behind, *left]).astype(ml_dtypes.bfloat16)


def mul(a, b):
    return a[0] * b[0] - a[1] * b[1], a[0] * b[1] + a[1] * b[0]


def mulc(a, b):
    return a[0] * b[0] + a[1] * b[1], a[0] * b[1] - a[1] * b[0]


def sine(x):
    y = x * x
    return x * (1.0 - y * (1 / 6) * (1.0 - y * (1 / 20) * (1.0 - y * (1 / 42) * (1.0 - y * (1 / 72)))))


def cosine(x):
    y = x * x
    return 1.0 - y * 0.5 * (1.0 - y * (1 / 12) * (1.0 - y * (1 / 30) * (1.0 - y * (1 / 56) * (1.0 - y * (1 / 90)))))


def transform(waves, right, left):
    size = waves[0][0].shape[0]
    pairs = [waves[first : first + 2] for first in range(0, len(waves), 2)]
    mids = []
    for pair in pairs:
        rows = jnp.concatenate(
            [jnp.concatenate([re.astype(jnp.bfloat16), im.astype(jnp.bfloat16)], 1) for re, im in pair], 0
        )
        mid = jnp.dot(rows, right, preferred_element_type=jnp.float32).astype(jnp.bfloat16)
        cut = [mid[i * size : (i + 1) * size] for i in range(len(pair))]
        mids.append(jnp.concatenate([jnp.concatenate([m[:, :size], m[:, size:]], 0) for m in cut], 1))
    out = []
    for pair, mid in zip(pairs, mids):
        done = jnp.dot(left, mid, preferred_element_type=jnp.float32)
        done = done.reshape(size // 8, 2, 8, -1)
        parts = [done[:, c].reshape(size, -1) for c in range(2)]
        for i in range(len(pair)):
            out.append(tuple(x[:, i * size : (i + 1) * size] for x in parts))
    return out


def swap(values, half):
    return pltpu.roll(values, half, values.ndim - 1)


def low_lanes(shape):
    return lax.broadcasted_iota(jnp.int32, shape, len(shape) - 1) < shape[-1] // 2


def pack(pair):
    half = pair[0].shape[-1] // 2
    low = low_lanes(pair[0].shape)
    return jnp.where(low, pair[0], swap(pair[1], half)), jnp.where(low, swap(pair[0], half), pair[1])


def unpack(lows, highs):
    half = lows.shape[-1] // 2
    low = low_lanes(lows.shape)
    return jnp.where(low, lows, swap(highs, half)), jnp.where(low, swap(lows, half), highs)


def pack_kernel(groups, me_ref, row_ref, col_ref, count_ref, potential_ref, amps_ref, *refs):
    slots = row_ref.shape[0]
    even = lax.rem(me_ref[0], 2) == 0
    _, _, rows, size = potential_ref.shape
    for g, group in enumerate(groups):
        first, second = refs[2 * g : 2 * g + 2]
        for j, s in enumerate(group):
            lows, highs = pack((potential_ref[s, 0], potential_ref[s, 1]))
            first[j * rows : (j + 1) * rows] = jnp.where(even, highs, lows)
            second[j * rows : (j + 1) * rows] = jnp.where(even, lows, highs)
        top = len(group) * rows
        if g == 0:
            lane = lax.broadcasted_iota(jnp.int32, (8, size), 1)
            about = jnp.zeros((8, size), jnp.int32)
            for p in range(slots):
                about = jnp.where(lane == p, row_ref[p], jnp.where(lane == slots + p, col_ref[p], about))
            about = jnp.where(lane == 2 * slots, count_ref[0], about).astype(jnp.float32)
            first[top:] = about
            second[top:] = about
        else:
            for p in range(slots):
                amps = amps_ref[p].astype(jnp.float32)
                first[top + p * size : top + (p + 1) * size] = amps
                second[top + p * size : top + (p + 1) * size] = amps


def transmit(phase, absorption):
    magnitude = jnp.exp(-absorption)
    return magnitude * cosine(phase), magnitude * sine(phase)


def gate_kernel(*refs):
    pass


def prepare_kernel(potential_ref, tables_ref, amps_ref, pieces_ref, trans_ref, tables_out, amps_out, probe_ref):
    part = pieces_ref.shape[2]
    for k in range(pieces_ref.shape[0]):
        probe_ref[:, k * part : (k + 1) * part, :] = pieces_ref[k]
    for s in range(potential_ref.shape[0]):
        trans_ref[s, 0], trans_ref[s, 1] = transmit(potential_ref[s, 0], potential_ref[s, 1])
    tables_out[...] = tables_ref[...]
    amps_out[...] = amps_ref[...]


class Names:
    def __init__(self, names, refs):
        self.__dict__.update(zip(names, refs))

    def get(self, name):
        return self.__dict__[name]


def stage_kernel(names, ahead, top, back, pieces, *refs):
    r = Names(names, refs)
    size = r.tables.shape[-1] // 2
    half = size // 2
    modes = r.modes_ref.shape[0]
    slots = r.rows.shape[0]
    me = r.me[0]
    last = me == pieces - 1
    even = lax.rem(me, 2) == 0
    lanes = lax.broadcasted_iota(jnp.int32, (size, size), 1)

    def halves(i, start, count):
        one, two = r.across_even[start : start + count], r.across_odd[start : start + count]
        return jnp.where(even, one, two), jnp.where(even, two, one)

    if 0 in ahead:
        height = r.own.shape[-2]
        about = halves(0, len(ahead) * height, 8)[1][0:1].astype(jnp.int32)
        lane = lanes[0:1]
        number = jnp.int32(0)
        for k in range(2 * slots):
            p = k % slots
            if k < slots:
                row, col, count = r.rows[p], r.cols[p], r.count[0]
                stays = (col < half) | last
            else:
                row, col, count = [jnp.sum(jnp.where(lane == at, about, 0)) for at in (p, slots + p, 2 * slots)]
                stays = col >= half
            r.held_out[3 * number + 1] = jnp.int32(k)
            r.held_out[3 * number + 2] = row
            r.held_out[3 * number + 3] = col
            number = number + ((p < count) & stays).astype(jnp.int32)
        r.held_out[0] = number
        held = r.held_out
    else:
        held = r.held
    number = held[0]

    for i, s in enumerate(ahead):
        height = r.own.shape[-2]
        halo = transmit(*unpack(*halves(0, i * height, height)))
        for c in range(2):
            r.tiles[i, 0, c] = r.own[s, c]
            r.tiles[i, 1, c] = halo[c]
            r.tiles[i, 2, c] = jnp.full((height, size), 1.0 - c, jnp.float32)
    if top:
        begin = len(ahead) * r.own.shape[-2]
        for p in range(slots):
            r.amps_all[p] = r.amps[p].astype(jnp.float32)
            r.amps_all[slots + p] = halves(0, begin + p * size, size)[1]
    if back:
        r.grads[...] = jnp.zeros_like(r.grads)
    if 0 in back:
        r.total[...] = jnp.zeros_like(r.total)

    def load(ref, *lead):
        return [(ref[(*lead, m, slice(None), slice(0, size))], ref[(*lead, m, slice(None), slice(size, None))]) for m in range(modes)]

    def store(ref, waves, *lead):
        for m, (re, im) in enumerate(waves):
            ref[(*lead, m, slice(None), slice(0, size))] = re
            ref[(*lead, m, slice(None), slice(size, None))] = im

    def psi(s, at):
        return load(r.psi_0) if s == 0 else load(r.get("psi_%d" % s), at)

    def trans(s, at):
        ref = r.get("trans_%d" % s)
        return ref[at, 0], ref[at, 1]

    def slot_step(at, misfit):
        k = held[3 * at + 1]
        row = held[3 * at + 2]
        col = held[3 * at + 3]
        own = k < slots
        left = jnp.where(own, 0, 1)
        right = jnp.where(own, jnp.where(last, 2, 1), 0)
        turn = lax.rem(size - col, size)
        inside = lanes >= col
        for i, s in enumerate(ahead):
            for c in range(2):
                both = jnp.where(inside, r.tiles[i, left, c, pl.ds(row, size), :], r.tiles[i, right, c, pl.ds(row, size), :])
                r.get("trans_%d" % s)[at, c] = pltpu.roll(both, turn, 1)
            waves = [mul(trans(s, at), w) for w in psi(s, at)]
            if top and s == ahead[-1]:
                waves = transform(waves, r.tables[0], r.tables[4])
            else:
                waves = transform(waves, r.tables[2], r.tables[6])
                store(r.get("psi_%d" % (s + 1)), waves, at)
        if top:
            inten = sum(re * re + im * im for re, im in waves)
            model = jnp.sqrt(inten + REG)
            observed = r.amps_all[k]
            diff = model - observed
            misfit = misfit + jnp.sum(diff * diff, axis=0, keepdims=True)
            ratio = 1.0 - observed / model
            waves = transform([(ratio * re, ratio * im) for re, im in waves], r.tables[1], r.tables[5])
        elif back:
            waves = load(r.wave_in, at)
        for i, s in enumerate(back):
            waves = [mulc(trans(s, at), w) for w in waves]
            quot = [mulc(a, w) for a, w in zip(psi(s, at), waves)]
            values = sum(im for _, im in quot), -sum(re for re, _ in quot)
            for c in range(2):
                turned = pltpu.roll(values[c], col, 1)
                r.grads[i, left, c, pl.ds(row, size), :] += jnp.where(inside, turned, 0.0)
                r.grads[i, right, c, pl.ds(row, size), :] += jnp.where(inside, 0.0, turned)
            if s > 0:
                waves = transform(waves, r.tables[3], r.tables[7])
        if 0 in back:
            for m, (re, im) in enumerate(waves):
                r.total[m, :, :size] += re
                r.total[m, :, size:] += im
        elif back or top:
            store(r.wave_out, waves, at)
        return misfit

    misfit = lax.fori_loop(0, number, slot_step, jnp.zeros((1, size), jnp.float32))
    if top:
        value = jnp.sum(misfit, axis=1, keepdims=True)
        lane = lax.broadcasted_iota(jnp.int32, (1, 1, size), 2)
        count = r.count[0].astype(jnp.float32)
        value = jnp.where(lane == 0, value[None], jnp.where(lane == 1, count, 0.0))
        r.sums[...] = jnp.broadcast_to(value[0], r.sums.shape)
    for i, s in enumerate(back):
        r.grad[i] = r.grads[i, 0]
        lows, highs = pack((r.grads[i, 1, 0], r.grads[i, 1, 1]))
        height = lows.shape[0]
        r.for_even[i * height : (i + 1) * height] = jnp.where(even, lows, highs)
        r.for_odd[i * height : (i + 1) * height] = jnp.where(even, highs, lows)
    if 0 in back:
        part = r.total.shape[1] // pieces
        sums = r.sums_in[...]
        for k in range(pieces):
            for m in range(modes):
                r.share[k, m * part : (m + 1) * part] = r.total[m, k * part : (k + 1) * part, :]
            r.share[k, modes * part :] = jnp.concatenate([sums, sums], 1)


def stage(given, made, scratch, ahead, top, back, pieces, name):
    names = [n for n, _, _ in given] + [n for n, _ in made] + [n for n, _ in scratch]
    out = pl.pallas_call(
        functools.partial(stage_kernel, names, ahead, top, back, pieces),
        out_shape=[jax.ShapeDtypeStruct(shape, jnp.float32) for _, shape in made],
        in_specs=[SMEM if small else VMEM for _, _, small in given],
        out_specs=[VMEM] * len(made),
        scratch_shapes=[x for _, x in scratch],
        compiler_params=pltpu.CompilerParams(vmem_limit_bytes=24 * 2**20),
        cost_estimate=pl.CostEstimate(flops=(len(ahead) + len(back) + 1) * 10**9, bytes_accessed=10**7, transcendentals=0),
        name=name,
    )(*[x for _, x, _ in given])
    return dict(zip([n for n, _ in made], out))


def finish_kernel(back, modes, me_ref, late_ref, early_ref, even_in, odd_in, share_in, sums_ref, grad_ref, share_ref):
    even = lax.rem(me_ref[0], 2) == 0
    rows, size = grad_ref.shape[2:]
    part = share_ref.shape[2]
    sums = sums_ref[0:1]
    scale = lax.rsqrt(sums[:, 0:1] / (sums[:, 1:2] * (size * size)) + 1e-06)
    for i, s in enumerate(back):
        one, two = even_in[i * rows : (i + 1) * rows], odd_in[i * rows : (i + 1) * rows]
        arrived = unpack(jnp.where(even, two, one), jnp.where(even, one, two))
        count = late_ref.shape[0]
        for c in range(2):
            own = late_ref[i, c] if i < count else early_ref[i - count, c]
            grad_ref[s, c] = (own + arrived[c]) * scale
    for m in range(modes):
        share_ref[0, m] = jnp.sum(share_in[:, m * part : (m + 1) * part, :], axis=0) * scale


def total_over(value, axis):
    n = lax.axis_size(axis)
    if n & (n - 1):
        return lax.psum(value, axis)
    step = 1
    while step < n:
        ways = 4 if n // step % 4 == 0 else 2
        value = value + sum(
            lax.ppermute(value, axis, [(i, i ^ (step * k)) for i in range(n)]) for k in range(1, ways)
        )
        step *= ways
    return value


def body(potential, probe, amplitudes, row_offset, col_offset, counts):
    slices, _, rows, size = potential.shape
    modes = probe.shape[1]
    part = probe.shape[2]
    slots = row_offset.shape[-1]
    pieces = lax.axis_size("pos")
    cut = slices // 2
    groups = (tuple(range(cut)), tuple(range(cut, slices)))
    f32 = jnp.float32
    me = lax.axis_index("pos").astype(jnp.int32).reshape(1)
    here = [row_offset[0, 0], col_offset[0, 0], counts[0]]

    def exchange(value, first):
        edges = [(i, i + 1) for i in range(first, pieces - 1, 2)]
        return lax.ppermute(value, "pos", edges + [(j, i) for i, j in edges])

    def call(kernel, given, out, name, scratch=(), flops=0):
        return pl.pallas_call(
            kernel,
            out_shape=[x[0] if isinstance(x, tuple) else x for x in out],
            in_specs=[SMEM if jnp.issubdtype(x.dtype, jnp.integer) else VMEM for x in given],
            out_specs=[SMEM if jnp.issubdtype(x.dtype, jnp.integer) else VMEM for x in out],
            scratch_shapes=list(scratch),
            compiler_params=pltpu.CompilerParams(vmem_limit_bytes=24 * 2**20),
            cost_estimate=pl.CostEstimate(flops=flops, bytes_accessed=10**6, transcendentals=0),
            name=name,
        )(*given)

    def array(shape, dtype=f32):
        return jax.ShapeDtypeStruct(shape, dtype)

    def stage(given, made, scratch, ahead, top, back, name):
        given = dict(me=me, rows=here[0], cols=here[1], count=here[2], tables=tables_here, **given)
        scratch = dict(modes_ref=pltpu.SMEM((modes,), jnp.int32), **scratch)
        names = list(given) + list(made) + list(scratch)
        kernel = functools.partial(stage_kernel, names, ahead, top, back, pieces)
        flops = (len(ahead) + len(back) + 1) * 2 * 10**9
        return dict(zip(made, call(kernel, list(given.values()), list(made.values()), name, scratch.values(), flops)))

    gathered = lax.all_to_all(jnp.broadcast_to(probe, (pieces,) + probe.shape[1:]), "pos", 0, 0)
    heights = [len(groups[0]) * rows + 8, len(groups[1]) * rows + slots * size]
    packed = call(
        functools.partial(pack_kernel, groups),
        [me, *here, potential, amplitudes[0, 0]],
        [array((heights[i // 2], size)) for i in range(4)],
        "pack",
    )
    came = [exchange(packed[i], i % 2) for i in range(4)]
    trans_own, tables_here, amps, probe_all = call(
        prepare_kernel,
        [potential, jnp.asarray(tables(size)), amplitudes[0, 0], gathered],
        [
            array(potential.shape),
            array((8, 2 * size, 2 * size), jnp.bfloat16),
            array((slots, size, size), jnp.bfloat16),
            array((modes, size, 2 * size)),
        ],
        "prepare",
        flops=10**9,
    )

    wave = (2 * slots, modes, size, 2 * size)
    trans = (2 * slots, 2, size, size)
    tiles = lambda n: pltpu.VMEM((n, 3, 2, rows, size), f32)
    sides = lambda n: dict(grad=array((n, 2, rows, size)), for_even=array((n * rows, size)), for_odd=array((n * rows, size)))

    first, second = groups
    a = stage(
        dict(own=trans_own, across_even=came[0], across_odd=came[1], psi_0=probe_all),
        dict(held_out=array((6 * slots + 4,), jnp.int32))
        | {"psi_%d" % (s + 1): array(wave) for s in first}
        | {"trans_%d" % s: array(trans) for s in first},
        dict(tiles=tiles(len(first))),
        first,
        False,
        (),
        "ahead",
    )
    held = a["held_out"]
    b = stage(
        dict(own=trans_own, across_even=came[2], across_odd=came[3], amps=amps, held=held)
        | {"psi_%d" % second[0]: a["psi_%d" % second[0]]},
        dict(sums=array((8, size)), wave_out=array(wave)) | sides(len(second)),
        dict(tiles=tiles(len(second)), grads=tiles(len(second)), amps_all=pltpu.VMEM((2 * slots, size, size), f32))
        | {"psi_%d" % s: pltpu.VMEM(wave, f32) for s in second[1:]}
        | {"trans_%d" % s: pltpu.VMEM(trans, f32) for s in second},
        second,
        True,
        second[::-1],
        "top",
    )
    c = stage(
        dict(held=held, wave_in=b["wave_out"], sums_in=b["sums"])
        | {"psi_%d" % s: probe_all if s == 0 else a["psi_%d" % s] for s in first}
        | {"trans_%d" % s: a["trans_%d" % s] for s in first},
        dict(share=array((pieces, modes * part + 8, 2 * size))) | sides(len(first)),
        dict(grads=tiles(len(first)), total=pltpu.VMEM(wave[1:], f32)),
        (),
        False,
        first[::-1],
        "back",
    )
    join = lambda name: jnp.concatenate([b[name], c[name]], 0)
    got = [exchange(join("for_even"), 0), exchange(join("for_odd"), 1)]
    shares = lax.all_to_all(c["share"], "pos", 0, 0)
    sums = total_over(jnp.sum(shares[:, modes * part :, :size], axis=0), "group")
    return call(
        functools.partial(finish_kernel, second[::-1] + first[::-1], modes),
        [me, b["grad"], c["grad"], *got, shares, sums],
        [array(potential.shape), array(probe.shape)],
        "finish",
    )


def solution(mesh):
    placed = (
        P(None, None, "group", "pos"),
        P("group", None, "pos", None),
        P("group", "pos", None, None, None),
        P("group", "pos", None),
        P("group", "pos", None),
        P("group", "pos"),
    )
    return jax.shard_map(
        body,
        mesh=mesh,
        in_specs=placed,
        out_specs=(P(None, None, "group", "pos"), P("group", None, "pos", None)),
        check_vma=False,
    )
```

```python
import functools
import math

import jax
import jax.numpy as jnp
import ml_dtypes
import numpy as np
from jax import lax
from jax.experimental import pallas as pl
from jax.experimental.pallas import tpu as pltpu
from jax.sharding import PartitionSpec as P

PROP = 0.25
REG = 0.1
VMEM = pl.BlockSpec(memory_space=pltpu.VMEM)
SMEM = pl.BlockSpec(memory_space=pltpu.SMEM)


@functools.lru_cache(maxsize=None)
def tables(size):
    idx = np.arange(size)
    angle = np.float32(2.0 * math.pi / size) * (idx[:, None] * idx[None, :] % size).astype(np.float32)
    cosv = (np.cos(angle) / np.float32(math.sqrt(size))).astype(ml_dtypes.bfloat16).astype(np.float64)
    sinv = (np.sin(angle) / np.float32(math.sqrt(size))).astype(ml_dtypes.bfloat16).astype(np.float64)
    forward = np.block([[cosv, -sinv], [sinv, cosv]])
    inverse = np.block([[cosv, sinv], [-sinv, cosv]])
    freq = np.where(idx < size // 2, idx, idx - size).astype(np.float64)
    phase = -2.0 * math.pi * PROP / size * freq * freq
    real, imag = np.diag(np.cos(phase)), np.diag(np.sin(phase))
    ahead = forward @ np.block([[real, imag], [-imag, real]]) @ inverse
    behind = forward @ np.block([[real, -imag], [imag, real]]) @ inverse
    rows = np.arange(2 * size).reshape(2, size // 8, 8).swapaxes(0, 1).reshape(-1)
    left = [t.T[rows] for t in (forward, inverse, ahead, behind)]
    return np.stack([forward, inverse, ahead, behind, *left]).astype(ml_dtypes.bfloat16)


def mul(a, b):
    return a[0] * b[0] - a[1] * b[1], a[0] * b[1] + a[1] * b[0]


def mulc(a, b):
    return a[0] * b[0] + a[1] * b[1], a[0] * b[1] - a[1] * b[0]


def sine(x):
    y = x * x
    return x * (1.0 - y * (1 / 6) * (1.0 - y * (1 / 20) * (1.0 - y * (1 / 42) * (1.0 - y * (1 / 72)))))


def cosine(x):
    y = x * x
    return 1.0 - y * 0.5 * (1.0 - y * (1 / 12) * (1.0 - y * (1 / 30) * (1.0 - y * (1 / 56) * (1.0 - y * (1 / 90)))))


def transform(waves, right, left):
    size = waves[0][0].shape[0]
    rows = jnp.concatenate(
        [jnp.concatenate([re.astype(jnp.bfloat16), im.astype(jnp.bfloat16)], 1) for re, im in waves], 0
    )
    mid = jnp.dot(rows, right, preferred_element_type=jnp.float32).astype(jnp.bfloat16)
    cut = [mid[i * size : (i + 1) * size] for i in range(len(waves))]
    stacked = [jnp.concatenate([m[:, :size], m[:, size:]], 0) for m in cut]
    pairs = [waves[first : first + 2] for first in range(0, len(waves), 2)]
    mids = [jnp.concatenate(stacked[first : first + 2], 1) for first in range(0, len(waves), 2)]
    out = []
    for pair, mid in zip(pairs, mids):
        done = jnp.dot(left, mid, preferred_element_type=jnp.float32)
        done = done.reshape(size // 8, 2, 8, -1)
        parts = [done[:, c].reshape(size, -1) for c in range(2)]
        for i in range(len(pair)):
            out.append(tuple(x[:, i * size : (i + 1) * size] for x in parts))
    return out


def swap(values, half):
    return pltpu.roll(values, half, values.ndim - 1)


def low_lanes(shape):
    return lax.broadcasted_iota(jnp.int32, shape, len(shape) - 1) < shape[-1] // 2


def pack(pair):
    half = pair[0].shape[-1] // 2
    low = low_lanes(pair[0].shape)
    return jnp.where(low, pair[0], swap(pair[1], half)), jnp.where(low, swap(pair[0], half), pair[1])


def unpack(lows, highs):
    half = lows.shape[-1] // 2
    low = low_lanes(lows.shape)
    return jnp.where(low, lows, swap(highs, half)), jnp.where(low, swap(lows, half), highs)


def pack_kernel(groups, me_ref, row_ref, col_ref, count_ref, potential_ref, amps_ref, *refs):
    slots = row_ref.shape[0]
    even = lax.rem(me_ref[0], 2) == 0
    _, _, rows, size = potential_ref.shape
    for g, group in enumerate(groups):
        first, second = refs[2 * g : 2 * g + 2]
        for j, s in enumerate(group):
            lows, highs = pack((potential_ref[s, 0], potential_ref[s, 1]))
            first[j * rows : (j + 1) * rows] = jnp.where(even, highs, lows)
            second[j * rows : (j + 1) * rows] = jnp.where(even, lows, highs)
        top = len(group) * rows
        if g == 0:
            lane = lax.broadcasted_iota(jnp.int32, (8, size), 1)
            about = jnp.zeros((8, size), jnp.int32)
            for p in range(slots):
                about = jnp.where(lane == p, row_ref[p], jnp.where(lane == slots + p, col_ref[p], about))
            about = jnp.where(lane == 2 * slots, count_ref[0], about).astype(jnp.float32)
            first[top:] = about
            second[top:] = about
        else:
            for p in range(slots):
                amps = amps_ref[p].astype(jnp.float32)
                first[top + p * size : top + (p + 1) * size] = amps
                second[top + p * size : top + (p + 1) * size] = amps


def transmit(phase, absorption):
    magnitude = jnp.exp(-absorption)
    return magnitude * cosine(phase), magnitude * sine(phase)


def gate_kernel(*refs):
    pass


def prepare_kernel(potential_ref, tables_ref, amps_ref, pieces_ref, trans_ref, tables_out, amps_out, probe_ref):
    part = pieces_ref.shape[2]
    for k in range(pieces_ref.shape[0]):
        probe_ref[:, k * part : (k + 1) * part, :] = pieces_ref[k]
    for s in range(potential_ref.shape[0]):
        trans_ref[s, 0], trans_ref[s, 1] = transmit(potential_ref[s, 0], potential_ref[s, 1])
    tables_out[...] = tables_ref[...]
    amps_out[...] = amps_ref[...]


class Names:
    def __init__(self, names, refs):
        self.__dict__.update(zip(names, refs))

    def get(self, name):
        return self.__dict__[name]


def stage_kernel(names, ahead, top, back, pieces, *refs):
    r = Names(names, refs)
    size = r.tables.shape[-1] // 2
    half = size // 2
    modes = r.modes_ref.shape[0]
    slots = r.rows.shape[0]
    me = r.me[0]
    last = me == pieces - 1
    even = lax.rem(me, 2) == 0
    lanes = lax.broadcasted_iota(jnp.int32, (size, size), 1)

    def halves(i, start, count):
        one, two = r.across_even[start : start + count], r.across_odd[start : start + count]
        return jnp.where(even, one, two), jnp.where(even, two, one)

    if 0 in ahead:
        height = r.own.shape[-2]
        about = halves(0, len(ahead) * height, 8)[1][0:1].astype(jnp.int32)
        lane = lanes[0:1]
        number = jnp.int32(0)
        for k in range(2 * slots):
            p = k % slots
            if k < slots:
                row, col, count = r.rows[p], r.cols[p], r.count[0]
                stays = (col < half) | last
            else:
                row, col, count = [jnp.sum(jnp.where(lane == at, about, 0)) for at in (p, slots + p, 2 * slots)]
                stays = col >= half
            r.held_out[3 * number + 1] = jnp.int32(k)
            r.held_out[3 * number + 2] = row
            r.held_out[3 * number + 3] = col
            number = number + ((p < count) & stays).astype(jnp.int32)
        r.held_out[0] = number
        held = r.held_out
    else:
        held = r.held
    number = held[0]

    for i, s in enumerate(ahead):
        height = r.own.shape[-2]
        halo = transmit(*unpack(*halves(0, i * height, height)))
        for c in range(2):
            r.tiles[i, 0, c] = r.own[s, c]
            r.tiles[i, 1, c] = halo[c]
            r.tiles[i, 2, c] = jnp.full((height, size), 1.0 - c, jnp.float32)
    if top:
        begin = len(ahead) * r.own.shape[-2]
        for p in range(slots):
            r.amps_all[p] = r.amps[p].astype(jnp.float32)
            r.amps_all[slots + p] = halves(0, begin + p * size, size)[1]
    if back:
        r.grads[...] = jnp.zeros_like(r.grads)
    if 0 in back:
        r.total[...] = jnp.zeros_like(r.total)

    def load(ref, *lead):
        return [(ref[(*lead, m, slice(None), slice(0, size))], ref[(*lead, m, slice(None), slice(size, None))]) for m in range(modes)]

    def store(ref, waves, *lead):
        for m, (re, im) in enumerate(waves):
            ref[(*lead, m, slice(None), slice(0, size))] = re
            ref[(*lead, m, slice(None), slice(size, None))] = im

    def psi(s, at):
        return load(r.psi_0) if s == 0 else load(r.get("psi_%d" % s), at)

    def trans(s, at):
        ref = r.get("trans_%d" % s)
        return ref[at, 0], ref[at, 1]

    def slot_step(at, misfit):
        k = held[3 * at + 1]
        row = held[3 * at + 2]
        col = held[3 * at + 3]
        own = k < slots
        left = jnp.where(own, 0, 1)
        right = jnp.where(own, jnp.where(last, 2, 1), 0)
        turn = lax.rem(size - col, size)
        inside = lanes >= col
        for i, s in enumerate(ahead):
            for c in range(2):
                both = jnp.where(inside, r.tiles[i, left, c, pl.ds(row, size), :], r.tiles[i, right, c, pl.ds(row, size), :])
                r.get("trans_%d" % s)[at, c] = pltpu.roll(both, turn, 1)
            waves = [mul(trans(s, at), w) for w in psi(s, at)]
            if top and s == ahead[-1]:
                waves = transform(waves, r.tables[0], r.tables[4])
            else:
                waves = transform(waves, r.tables[2], r.tables[6])
                store(r.get("psi_%d" % (s + 1)), waves, at)
        if top:
            inten = sum(re * re + im * im for re, im in waves)
            model = jnp.sqrt(inten + REG)
            observed = r.amps_all[k]
            diff = model - observed
            misfit = misfit + jnp.sum(diff * diff, axis=0, keepdims=True)
            ratio = 1.0 - observed / model
            waves = transform([(ratio * re, ratio * im) for re, im in waves], r.tables[1], r.tables[5])
        elif back:
            waves = load(r.wave_in, at)
        for i, s in enumerate(back):
            waves = [mulc(trans(s, at), w) for w in waves]
            quot = [mulc(a, w) for a, w in zip(psi(s, at), waves)]
            values = sum(im for _, im in quot), -sum(re for re, _ in quot)
            for c in range(2):
                turned = pltpu.roll(values[c], col, 1)
                r.grads[i, left, c, pl.ds(row, size), :] += jnp.where(inside, turned, 0.0)
                r.grads[i, right, c, pl.ds(row, size), :] += jnp.where(inside, 0.0, turned)
            if s > 0:
                waves = transform(waves, r.tables[3], r.tables[7])
        if 0 in back:
            for m, (re, im) in enumerate(waves):
                r.total[m, :, :size] += re
                r.total[m, :, size:] += im
        elif back or top:
            store(r.wave_out, waves, at)
        return misfit

    misfit = lax.fori_loop(0, number, slot_step, jnp.zeros((1, size), jnp.float32))
    if top:
        value = jnp.sum(misfit, axis=1, keepdims=True)
        lane = lax.broadcasted_iota(jnp.int32, (1, 1, size), 2)
        count = r.count[0].astype(jnp.float32)
        value = jnp.where(lane == 0, value[None], jnp.where(lane == 1, count, 0.0))
        r.sums[...] = jnp.broadcast_to(value[0], r.sums.shape)
    for i, s in enumerate(back):
        r.grad[i] = r.grads[i, 0]
        lows, highs = pack((r.grads[i, 1, 0], r.grads[i, 1, 1]))
        height = lows.shape[0]
        r.for_even[i * height : (i + 1) * height] = jnp.where(even, lows, highs)
        r.for_odd[i * height : (i + 1) * height] = jnp.where(even, highs, lows)
    if 0 in back:
        part = r.total.shape[1] // pieces
        sums = r.sums_in[...]
        for k in range(pieces):
            for m in range(modes):
                r.share[k, m * part : (m + 1) * part] = r.total[m, k * part : (k + 1) * part, :]
            r.share[k, modes * part :] = jnp.concatenate([sums, sums], 1)


def stage(given, made, scratch, ahead, top, back, pieces, name):
    names = [n for n, _, _ in given] + [n for n, _ in made] + [n for n, _ in scratch]
    out = pl.pallas_call(
        functools.partial(stage_kernel, names, ahead, top, back, pieces),
        out_shape=[jax.ShapeDtypeStruct(shape, jnp.float32) for _, shape in made],
        in_specs=[SMEM if small else VMEM for _, _, small in given],
        out_specs=[VMEM] * len(made),
        scratch_shapes=[x for _, x in scratch],
        compiler_params=pltpu.CompilerParams(vmem_limit_bytes=24 * 2**20),
        cost_estimate=pl.CostEstimate(flops=(len(ahead) + len(back) + 1) * 10**9, bytes_accessed=10**7, transcendentals=0),
        name=name,
    )(*[x for _, x, _ in given])
    return dict(zip([n for n, _ in made], out))


def finish_kernel(back, modes, me_ref, *refs):
    grads, (even_in, odd_in, share_in, grad_ref, share_ref) = refs[:-5], refs[-5:]
    even = lax.rem(me_ref[0], 2) == 0
    rows, size = grad_ref.shape[2:]
    part = share_ref.shape[2]
    sums = jnp.sum(share_in[:, modes * part :, :], axis=0)[0:1]
    scale = lax.rsqrt(sums[:, 0:1] / (sums[:, 1:2] * (size * size)) + 1e-06)
    own = [ref.at[i] for ref in grads for i in range(ref.shape[0])]
    for i, s in enumerate(back):
        one, two = even_in[i * rows : (i + 1) * rows], odd_in[i * rows : (i + 1) * rows]
        arrived = unpack(jnp.where(even, two, one), jnp.where(even, one, two))
        for c in range(2):
            grad_ref[s, c] = (own[i][c] + arrived[c]) * scale
    for m in range(modes):
        share_ref[0, m] = jnp.sum(share_in[:, m * part : (m + 1) * part, :], axis=0) * scale


def total_over(value, axis):
    n = lax.axis_size(axis)
    if n & (n - 1):
        return lax.psum(value, axis)
    step = 1
    while step < n:
        ways = 4 if n // step % 4 == 0 else 2
        value = value + sum(
            lax.ppermute(value, axis, [(i, i ^ (step * k)) for i in range(n)]) for k in range(1, ways)
        )
        step *= ways
    return value


def body(potential, probe, amplitudes, row_offset, col_offset, counts):
    slices, _, rows, size = potential.shape
    modes = probe.shape[1]
    part = probe.shape[2]
    slots = row_offset.shape[-1]
    pieces = lax.axis_size("pos")
    cut = slices // 2
    groups = (tuple(range(cut)), tuple(range(cut, slices)))
    f32 = jnp.float32
    me = lax.axis_index("pos").astype(jnp.int32).reshape(1)
    here = [row_offset[0, 0], col_offset[0, 0], counts[0]]

    def exchange(value, first):
        edges = [(i, i + 1) for i in range(first, pieces - 1, 2)]
        return lax.ppermute(value, "pos", edges + [(j, i) for i, j in edges])

    def call(kernel, given, out, name, scratch=(), flops=0):
        return pl.pallas_call(
            kernel,
            out_shape=[x[0] if isinstance(x, tuple) else x for x in out],
            in_specs=[SMEM if jnp.issubdtype(x.dtype, jnp.integer) else VMEM for x in given],
            out_specs=[SMEM if jnp.issubdtype(x.dtype, jnp.integer) else VMEM for x in out],
            scratch_shapes=list(scratch),
            compiler_params=pltpu.CompilerParams(vmem_limit_bytes=24 * 2**20),
            cost_estimate=pl.CostEstimate(flops=flops, bytes_accessed=10**6, transcendentals=0),
            name=name,
        )(*given)

    def array(shape, dtype=f32):
        return jax.ShapeDtypeStruct(shape, dtype)

    def stage(given, made, scratch, ahead, top, back, name):
        given = dict(me=me, rows=here[0], cols=here[1], count=here[2], tables=tables_here, **given)
        scratch = dict(modes_ref=pltpu.SMEM((modes,), jnp.int32), **scratch)
        names = list(given) + list(made) + list(scratch)
        kernel = functools.partial(stage_kernel, names, ahead, top, back, pieces)
        flops = (len(ahead) + len(back) + 1) * 2 * 10**9
        return dict(zip(made, call(kernel, list(given.values()), list(made.values()), name, scratch.values(), flops)))

    gathered = lax.all_to_all(jnp.broadcast_to(probe, (pieces,) + probe.shape[1:]), "pos", 0, 0)
    heights = [len(groups[0]) * rows + 8, len(groups[1]) * rows + slots * size]
    packed = call(
        functools.partial(pack_kernel, groups),
        [me, *here, potential, amplitudes[0, 0]],
        [array((heights[i // 2], size)) for i in range(4)],
        "pack",
    )
    came = [exchange(packed[i], i % 2) for i in range(4)]
    trans_own, tables_here, amps, probe_all = call(
        prepare_kernel,
        [potential, jnp.asarray(tables(size)), amplitudes[0, 0], gathered],
        [
            array(potential.shape),
            array((8, 2 * size, 2 * size), jnp.bfloat16),
            array((slots, size, size), jnp.bfloat16),
            array((modes, size, 2 * size)),
        ],
        "prepare",
        flops=10**9,
    )

    wave = (2 * slots, modes, size, 2 * size)
    trans = (2 * slots, 2, size, size)
    tiles = lambda n: pltpu.VMEM((n, 3, 2, rows, size), f32)
    sides = lambda n: dict(grad=array((n, 2, rows, size)), for_even=array((n * rows, size)), for_odd=array((n * rows, size)))

    first, second = groups
    a = stage(
        dict(own=trans_own, across_even=came[0], across_odd=came[1], psi_0=probe_all),
        dict(held_out=array((6 * slots + 4,), jnp.int32))
        | {"psi_%d" % (s + 1): array(wave) for s in first}
        | {"trans_%d" % s: array(trans) for s in first},
        dict(tiles=tiles(len(first))),
        first,
        False,
        (),
        "ahead",
    )
    held = a["held_out"]
    b = stage(
        dict(own=trans_own, across_even=came[2], across_odd=came[3], amps=amps, held=held)
        | {"psi_%d" % second[0]: a["psi_%d" % second[0]]},
        dict(sums=array((8, size)), wave_out=array(wave))
        | {"psi_%d" % s: array(wave) for s in second[1:]}
        | {"trans_%d" % s: array(trans) for s in second},
        dict(tiles=tiles(len(second)), amps_all=pltpu.VMEM((2 * slots, size, size), f32)),
        second,
        True,
        (),
        "top",
    )
    sums = total_over(b["sums"], "group")
    state = a | b | dict(psi_0=probe_all)
    done = []
    back = [(s,) for s in second[::-1]] + [first[::-1]]
    for group in back:
        end = 0 in group
        made = dict(share=array((pieces, modes * part + 8, 2 * size))) if end else dict(wave_out=array(wave))
        scratch = dict(total=pltpu.VMEM(wave[1:], f32)) if end else {}
        d = stage(
            dict(held=held, wave_in=state["wave_out"])
            | {"psi_%d" % s: state["psi_%d" % s] for s in group}
            | {"trans_%d" % s: state["trans_%d" % s] for s in group}
            | (dict(sums_in=sums) if end else {}),
            made | sides(len(group)),
            dict(grads=tiles(len(group))) | scratch,
            (),
            False,
            group,
            "back",
        )
        state = state | d
        done.append(d)
    join = lambda name: jnp.concatenate([d[name] for d in done], 0)
    got = [exchange(join("for_even"), 0), exchange(join("for_odd"), 1)]
    shares = lax.all_to_all(state["share"], "pos", 0, 0)
    return call(
        functools.partial(finish_kernel, sum(back, ()), modes),
        [me, *[d["grad"] for d in done], *got, shares],
        [array(potential.shape), array(probe.shape)],
        "finish",
    )


def solution(mesh):
    placed = (
        P(None, None, "group", "pos"),
        P("group", None, "pos", None),
        P("group", "pos", None, None, None),
        P("group", "pos", None),
        P("group", "pos", None),
        P("group", "pos"),
    )
    return jax.shard_map(
        body,
        mesh=mesh,
        in_specs=placed,
        out_specs=(P(None, None, "group", "pos"), P("group", None, "pos", None)),
        check_vma=False,
    )
```

```python
import functools
import math

import jax
import jax.numpy as jnp
import ml_dtypes
import numpy as np
from jax import lax
from jax.experimental import pallas as pl
from jax.experimental.pallas import tpu as pltpu
from jax.sharding import PartitionSpec as P

PROP = 0.25
REG = 0.1
VMEM = pl.BlockSpec(memory_space=pltpu.VMEM)
SMEM = pl.BlockSpec(memory_space=pltpu.SMEM)


@functools.lru_cache(maxsize=None)
def tables(size):
    idx = np.arange(size)
    angle = np.float32(2.0 * math.pi / size) * (idx[:, None] * idx[None, :] % size).astype(np.float32)
    cosv = (np.cos(angle) / np.float32(math.sqrt(size))).astype(ml_dtypes.bfloat16).astype(np.float64)
    sinv = (np.sin(angle) / np.float32(math.sqrt(size))).astype(ml_dtypes.bfloat16).astype(np.float64)
    forward = np.block([[cosv, -sinv], [sinv, cosv]])
    inverse = np.block([[cosv, sinv], [-sinv, cosv]])
    freq = np.where(idx < size // 2, idx, idx - size).astype(np.float64)
    phase = -2.0 * math.pi * PROP / size * freq * freq
    real, imag = np.diag(np.cos(phase)), np.diag(np.sin(phase))
    ahead = forward @ np.block([[real, imag], [-imag, real]]) @ inverse
    behind = forward @ np.block([[real, -imag], [imag, real]]) @ inverse
    rows = np.arange(2 * size).reshape(2, size // 8, 8).swapaxes(0, 1).reshape(-1)
    left = [t.T[rows] for t in (forward, inverse, ahead, behind)]
    return np.stack([forward, inverse, ahead, behind, *left]).astype(ml_dtypes.bfloat16)


def mul(a, b):
    return a[0] * b[0] - a[1] * b[1], a[0] * b[1] + a[1] * b[0]


def mulc(a, b):
    return a[0] * b[0] + a[1] * b[1], a[0] * b[1] - a[1] * b[0]


def sine(x):
    y = x * x
    return x * (1.0 - y * (1 / 6) * (1.0 - y * (1 / 20) * (1.0 - y * (1 / 42) * (1.0 - y * (1 / 72)))))


def cosine(x):
    y = x * x
    return 1.0 - y * 0.5 * (1.0 - y * (1 / 12) * (1.0 - y * (1 / 30) * (1.0 - y * (1 / 56) * (1.0 - y * (1 / 90)))))


def transform(waves, right, left):
    size = waves[0][0].shape[0]
    pairs = [waves[first : first + 2] for first in range(0, len(waves), 2)]
    mids = []
    for pair in pairs:
        rows = jnp.concatenate(
            [jnp.concatenate([re.astype(jnp.bfloat16), im.astype(jnp.bfloat16)], 1) for re, im in pair], 0
        )
        mid = jnp.dot(rows, right, preferred_element_type=jnp.float32).astype(jnp.bfloat16)
        cut = [mid[i * size : (i + 1) * size] for i in range(len(pair))]
        mids.append(jnp.concatenate([jnp.concatenate([m[:, :size], m[:, size:]], 0) for m in cut], 1))
    out = []
    for pair, mid in zip(pairs, mids):
        done = jnp.dot(left, mid, preferred_element_type=jnp.float32)
        done = done.reshape(size // 8, 2, 8, -1)
        parts = [done[:, c].reshape(size, -1) for c in range(2)]
        for i in range(len(pair)):
            out.append(tuple(x[:, i * size : (i + 1) * size] for x in parts))
    return out


def swap(values, half):
    return pltpu.roll(values, half, values.ndim - 1)


def low_lanes(shape):
    return lax.broadcasted_iota(jnp.int32, shape, len(shape) - 1) < shape[-1] // 2


def pack(pair):
    half = pair[0].shape[-1] // 2
    low = low_lanes(pair[0].shape)
    return jnp.where(low, pair[0], swap(pair[1], half)), jnp.where(low, swap(pair[0], half), pair[1])


def unpack(lows, highs):
    half = lows.shape[-1] // 2
    low = low_lanes(lows.shape)
    return jnp.where(low, lows, swap(highs, half)), jnp.where(low, swap(lows, half), highs)


def pack_kernel(groups, me_ref, row_ref, col_ref, count_ref, potential_ref, amps_ref, *refs):
    slots = row_ref.shape[0]
    even = lax.rem(me_ref[0], 2) == 0
    _, _, rows, size = potential_ref.shape
    for g, group in enumerate(groups):
        first, second = refs[2 * g : 2 * g + 2]
        for j, s in enumerate(group):
            lows, highs = pack((potential_ref[s, 0], potential_ref[s, 1]))
            first[j * rows : (j + 1) * rows] = jnp.where(even, highs, lows)
            second[j * rows : (j + 1) * rows] = jnp.where(even, lows, highs)
        top = len(group) * rows
        if g == 0:
            lane = lax.broadcasted_iota(jnp.int32, (8, size), 1)
            about = jnp.zeros((8, size), jnp.int32)
            for p in range(slots):
                about = jnp.where(lane == p, row_ref[p], jnp.where(lane == slots + p, col_ref[p], about))
            about = jnp.where(lane == 2 * slots, count_ref[0], about).astype(jnp.float32)
            first[top:] = about
            second[top:] = about
        else:
            for p in range(slots):
                amps = amps_ref[p].astype(jnp.float32)
                first[top + p * size : top + (p + 1) * size] = amps
                second[top + p * size : top + (p + 1) * size] = amps


def transmit(phase, absorption):
    magnitude = jnp.exp(-absorption)
    return magnitude * cosine(phase), magnitude * sine(phase)


def gate_kernel(*refs):
    pass


def prepare_kernel(potential_ref, tables_ref, amps_ref, pieces_ref, trans_ref, tables_out, amps_out, probe_ref):
    part = pieces_ref.shape[2]
    for k in range(pieces_ref.shape[0]):
        probe_ref[:, k * part : (k + 1) * part, :] = pieces_ref[k]
    for s in range(potential_ref.shape[0]):
        trans_ref[s, 0], trans_ref[s, 1] = transmit(potential_ref[s, 0], potential_ref[s, 1])
    tables_out[...] = tables_ref[...]
    amps_out[...] = amps_ref[...]


class Names:
    def __init__(self, names, refs):
        self.__dict__.update(zip(names, refs))

    def get(self, name):
        return self.__dict__[name]


def stage_kernel(names, ahead, top, back, pieces, *refs):
    r = Names(names, refs)
    size = r.tables.shape[-1] // 2
    half = size // 2
    modes = r.modes_ref.shape[0]
    slots = r.rows.shape[0]
    me = r.me[0]
    last = me == pieces - 1
    even = lax.rem(me, 2) == 0
    lanes = lax.broadcasted_iota(jnp.int32, (size, size), 1)

    def halves(i, start, count):
        one, two = r.across_even[start : start + count], r.across_odd[start : start + count]
        return jnp.where(even, one, two), jnp.where(even, two, one)

    if 0 in ahead:
        height = r.own.shape[-2]
        about = halves(0, len(ahead) * height, 8)[1][0:1].astype(jnp.int32)
        lane = lanes[0:1]
        number = jnp.int32(0)
        for k in range(2 * slots):
            p = k % slots
            if k < slots:
                row, col, count = r.rows[p], r.cols[p], r.count[0]
                stays = (col < half) | last
            else:
                row, col, count = [jnp.sum(jnp.where(lane == at, about, 0)) for at in (p, slots + p, 2 * slots)]
                stays = col >= half
            r.held_out[3 * number + 1] = jnp.int32(k)
            r.held_out[3 * number + 2] = row
            r.held_out[3 * number + 3] = col
            number = number + ((p < count) & stays).astype(jnp.int32)
        r.held_out[0] = number
        held = r.held_out
    else:
        held = r.held
    number = held[0]

    for i, s in enumerate(ahead):
        height = r.own.shape[-2]
        halo = transmit(*unpack(*halves(0, i * height, height)))
        for c in range(2):
            r.tiles[i, 0, c] = r.own[s, c]
            r.tiles[i, 1, c] = halo[c]
            r.tiles[i, 2, c] = jnp.full((height, size), 1.0 - c, jnp.float32)
    if top:
        begin = len(ahead) * r.own.shape[-2]
        for p in range(slots):
            r.amps_all[p] = r.amps[p].astype(jnp.float32)
            r.amps_all[slots + p] = halves(0, begin + p * size, size)[1]
    if back:
        r.grads[...] = jnp.zeros_like(r.grads)
    if 0 in back:
        r.total[...] = jnp.zeros_like(r.total)

    def load(ref, *lead):
        return [(ref[(*lead, m, slice(None), slice(0, size))], ref[(*lead, m, slice(None), slice(size, None))]) for m in range(modes)]

    def store(ref, waves, *lead):
        for m, (re, im) in enumerate(waves):
            ref[(*lead, m, slice(None), slice(0, size))] = re
            ref[(*lead, m, slice(None), slice(size, None))] = im

    def psi(s, at):
        return load(r.psi_0) if s == 0 else load(r.get("psi_%d" % s), at)

    def trans(s, at):
        ref = r.get("trans_%d" % s)
        return ref[at, 0], ref[at, 1]

    def slot_step(at, misfit):
        k = held[3 * at + 1]
        row = held[3 * at + 2]
        col = held[3 * at + 3]
        own = k < slots
        left = jnp.where(own, 0, 1)
        right = jnp.where(own, jnp.where(last, 2, 1), 0)
        turn = lax.rem(size - col, size)
        inside = lanes >= col
        for i, s in enumerate(ahead):
            for c in range(2):
                both = jnp.where(inside, r.tiles[i, left, c, pl.ds(row, size), :], r.tiles[i, right, c, pl.ds(row, size), :])
                r.get("trans_%d" % s)[at, c] = pltpu.roll(both, turn, 1)
            waves = [mul(trans(s, at), w) for w in psi(s, at)]
            if top and s == ahead[-1]:
                waves = transform(waves, r.tables[0], r.tables[4])
            else:
                waves = transform(waves, r.tables[2], r.tables[6])
                store(r.get("psi_%d" % (s + 1)), waves, at)
        if top:
            inten = sum(re * re + im * im for re, im in waves)
            model = jnp.sqrt(inten + REG)
            observed = r.amps_all[k]
            diff = model - observed
            misfit = misfit + jnp.sum(diff * diff, axis=0, keepdims=True)
            ratio = 1.0 - observed / model
            waves = transform([(ratio * re, ratio * im) for re, im in waves], r.tables[1], r.tables[5])
        elif back:
            waves = load(r.wave_in, at)
        for i, s in enumerate(back):
            waves = [mulc(trans(s, at), w) for w in waves]
            quot = [mulc(a, w) for a, w in zip(psi(s, at), waves)]
            values = sum(im for _, im in quot), -sum(re for re, _ in quot)
            for c in range(2):
                turned = pltpu.roll(values[c], col, 1)
                r.grads[i, left, c, pl.ds(row, size), :] += jnp.where(inside, turned, 0.0)
                r.grads[i, right, c, pl.ds(row, size), :] += jnp.where(inside, 0.0, turned)
            if s > 0:
                waves = transform(waves, r.tables[3], r.tables[7])
        if 0 in back:
            for m, (re, im) in enumerate(waves):
                r.total[m, :, :size] += re
                r.total[m, :, size:] += im
        elif back or top:
            store(r.wave_out, waves, at)
        return misfit

    misfit = lax.fori_loop(0, number, slot_step, jnp.zeros((1, size), jnp.float32))
    if top:
        value = jnp.sum(misfit, axis=1, keepdims=True)
        lane = lax.broadcasted_iota(jnp.int32, (1, 1, size), 2)
        count = r.count[0].astype(jnp.float32)
        value = jnp.where(lane == 0, value[None], jnp.where(lane == 1, count, 0.0))
        r.sums[...] = jnp.broadcast_to(value[0], r.sums.shape)
    for i, s in enumerate(back):
        r.grad[i] = r.grads[i, 0]
        lows, highs = pack((r.grads[i, 1, 0], r.grads[i, 1, 1]))
        height = lows.shape[0]
        r.for_even[i * height : (i + 1) * height] = jnp.where(even, lows, highs)
        r.for_odd[i * height : (i + 1) * height] = jnp.where(even, highs, lows)
    if 0 in back:
        part = r.total.shape[1] // pieces
        for k in range(pieces):
            for m in range(modes):
                r.share[k, m * part : (m + 1) * part] = r.total[m, k * part : (k + 1) * part, :]
            r.share[k, modes * part :] = jnp.zeros((8, 2 * size), jnp.float32)


def stage(given, made, scratch, ahead, top, back, pieces, name):
    names = [n for n, _, _ in given] + [n for n, _ in made] + [n for n, _ in scratch]
    out = pl.pallas_call(
        functools.partial(stage_kernel, names, ahead, top, back, pieces),
        out_shape=[jax.ShapeDtypeStruct(shape, jnp.float32) for _, shape in made],
        in_specs=[SMEM if small else VMEM for _, _, small in given],
        out_specs=[VMEM] * len(made),
        scratch_shapes=[x for _, x in scratch],
        compiler_params=pltpu.CompilerParams(vmem_limit_bytes=24 * 2**20),
        cost_estimate=pl.CostEstimate(flops=(len(ahead) + len(back) + 1) * 10**9, bytes_accessed=10**7, transcendentals=0),
        name=name,
    )(*[x for _, x, _ in given])
    return dict(zip([n for n, _ in made], out))


def finish_kernel(back, modes, me_ref, *refs):
    grads, (even_in, odd_in, share_in, grad_ref, share_ref) = refs[:-5], refs[-5:]
    even = lax.rem(me_ref[0], 2) == 0
    rows, size = grad_ref.shape[2:]
    part = share_ref.shape[2]
    sums = jnp.sum(share_in[:, modes * part :, :], axis=0)[0:1]
    scale = lax.rsqrt(sums[:, 0:1] / (sums[:, 1:2] * (size * size)) + 1e-06)
    own = [ref.at[i] for ref in grads for i in range(ref.shape[0])]
    for i, s in enumerate(back):
        one, two = even_in[i * rows : (i + 1) * rows], odd_in[i * rows : (i + 1) * rows]
        arrived = unpack(jnp.where(even, two, one), jnp.where(even, one, two))
        for c in range(2):
            grad_ref[s, c] = (own[i][c] + arrived[c]) * scale
    for m in range(modes):
        share_ref[0, m] = jnp.sum(share_in[:, m * part : (m + 1) * part, :], axis=0) * scale


def total_over(value, axis):
    n = lax.axis_size(axis)
    if n & (n - 1):
        return lax.psum(value, axis)
    step = 1
    while step < n:
        ways = 4 if n // step % 4 == 0 else 2
        value = value + sum(
            lax.ppermute(value, axis, [(i, i ^ (step * k)) for i in range(n)]) for k in range(1, ways)
        )
        step *= ways
    return value


def body(potential, probe, amplitudes, row_offset, col_offset, counts):
    slices, _, rows, size = potential.shape
    modes = probe.shape[1]
    part = probe.shape[2]
    slots = row_offset.shape[-1]
    pieces = lax.axis_size("pos")
    cut = slices // 2
    groups = (tuple(range(cut)), tuple(range(cut, slices)))
    f32 = jnp.float32
    me = lax.axis_index("pos").astype(jnp.int32).reshape(1)
    here = [row_offset[0, 0], col_offset[0, 0], counts[0]]

    def exchange(value, first):
        edges = [(i, i + 1) for i in range(first, pieces - 1, 2)]
        return lax.ppermute(value, "pos", edges + [(j, i) for i, j in edges])

    def call(kernel, given, out, name, scratch=(), flops=0):
        return pl.pallas_call(
            kernel,
            out_shape=[x[0] if isinstance(x, tuple) else x for x in out],
            in_specs=[SMEM if jnp.issubdtype(x.dtype, jnp.integer) else VMEM for x in given],
            out_specs=[SMEM if jnp.issubdtype(x.dtype, jnp.integer) else VMEM for x in out],
            scratch_shapes=list(scratch),
            compiler_params=pltpu.CompilerParams(vmem_limit_bytes=24 * 2**20),
            cost_estimate=pl.CostEstimate(flops=flops, bytes_accessed=10**6, transcendentals=0),
            name=name,
        )(*given)

    def array(shape, dtype=f32):
        return jax.ShapeDtypeStruct(shape, dtype)

    def stage(given, made, scratch, ahead, top, back, name):
        given = dict(me=me, rows=here[0], cols=here[1], count=here[2], tables=tables_here, **given)
        scratch = dict(modes_ref=pltpu.SMEM((modes,), jnp.int32), **scratch)
        names = list(given) + list(made) + list(scratch)
        kernel = functools.partial(stage_kernel, names, ahead, top, back, pieces)
        flops = (len(ahead) + len(back) + 1) * 2 * 10**9
        return dict(zip(made, call(kernel, list(given.values()), list(made.values()), name, scratch.values(), flops)))

    gathered = lax.all_to_all(jnp.broadcast_to(probe, (pieces,) + probe.shape[1:]), "pos", 0, 0)
    heights = [len(groups[0]) * rows + 8, len(groups[1]) * rows + slots * size]
    packed = call(
        functools.partial(pack_kernel, groups),
        [me, *here, potential, amplitudes[0, 0]],
        [array((heights[i // 2], size)) for i in range(4)],
        "pack",
    )
    came = [exchange(packed[i], i % 2) for i in range(4)]
    trans_own, tables_here, amps, probe_all = call(
        prepare_kernel,
        [potential, jnp.asarray(tables(size)), amplitudes[0, 0], gathered],
        [
            array(potential.shape),
            array((8, 2 * size, 2 * size), jnp.bfloat16),
            array((slots, size, size), jnp.bfloat16),
            array((modes, size, 2 * size)),
        ],
        "prepare",
        flops=10**9,
    )

    wave = (2 * slots, modes, size, 2 * size)
    trans = (2 * slots, 2, size, size)
    tiles = lambda n: pltpu.VMEM((n, 3, 2, rows, size), f32)
    sides = lambda n: dict(grad=array((n, 2, rows, size)), for_even=array((n * rows, size)), for_odd=array((n * rows, size)))

    first, second = groups
    a = stage(
        dict(own=trans_own, across_even=came[0], across_odd=came[1], psi_0=probe_all),
        dict(held_out=array((6 * slots + 4,), jnp.int32))
        | {"psi_%d" % (s + 1): array(wave) for s in first}
        | {"trans_%d" % s: array(trans) for s in first},
        dict(tiles=tiles(len(first))),
        first,
        False,
        (),
        "ahead",
    )
    held = a["held_out"]
    b = stage(
        dict(own=trans_own, across_even=came[2], across_odd=came[3], amps=amps, held=held)
        | {"psi_%d" % second[0]: a["psi_%d" % second[0]]},
        dict(sums=array((8, size)), wave_out=array(wave)) | sides(len(second)),
        dict(tiles=tiles(len(second)), grads=tiles(len(second)), amps_all=pltpu.VMEM((2 * slots, size, size), f32))
        | {"psi_%d" % s: pltpu.VMEM(wave, f32) for s in second[1:]}
        | {"trans_%d" % s: pltpu.VMEM(trans, f32) for s in second},
        second,
        True,
        second[::-1],
        "top",
    )
    sums = total_over(b["sums"], "group")
    done = [b]
    for s in first[::-1]:
        end = s == 0
        done.append(
            stage(
                {"wave_in": done[-1]["wave_out"], "held": held}
                | {"psi_%d" % s: probe_all if end else a["psi_%d" % s], "trans_%d" % s: a["trans_%d" % s]},
                (dict(share=array((pieces, modes * part + 8, 2 * size))) if end else dict(wave_out=array(wave)))
                | sides(1),
                dict(grads=tiles(1)) | (dict(total=pltpu.VMEM(wave[1:], f32)) if end else {}),
                (),
                False,
                (s,),
                "back",
            )
        )
    join = lambda name: jnp.concatenate([d[name] for d in done], 0)
    got = [exchange(join("for_even"), 0), exchange(join("for_odd"), 1)]
    sums = jnp.broadcast_to(jnp.concatenate([sums, sums], 1), (pieces, 8, 2 * size))
    shares = lax.dynamic_update_slice(done[-1]["share"], sums, (0, modes * part, 0))
    shares = lax.all_to_all(shares, "pos", 0, 0)
    return call(
        functools.partial(finish_kernel, second[::-1] + first[::-1], modes),
        [me, *[d["grad"] for d in done], *got, shares],
        [array(potential.shape), array(probe.shape)],
        "finish",
    )


def solution(mesh):
    placed = (
        P(None, None, "group", "pos"),
        P("group", None, "pos", None),
        P("group", "pos", None, None, None),
        P("group", "pos", None),
        P("group", "pos", None),
        P("group", "pos"),
    )
    return jax.shard_map(
        body,
        mesh=mesh,
        in_specs=placed,
        out_specs=(P(None, None, "group", "pos"), P("group", None, "pos", None)),
        check_vma=False,
    )
```

```python
import functools
import math

import jax
import jax.numpy as jnp
import ml_dtypes
import numpy as np
from jax import lax
from jax.experimental import pallas as pl
from jax.experimental.pallas import tpu as pltpu
from jax.sharding import PartitionSpec as P

PROP = 0.25
REG = 0.1
VMEM = pl.BlockSpec(memory_space=pltpu.VMEM)
SMEM = pl.BlockSpec(memory_space=pltpu.SMEM)


@functools.lru_cache(maxsize=None)
def tables(size):
    idx = np.arange(size)
    angle = np.float32(2.0 * math.pi / size) * (idx[:, None] * idx[None, :] % size).astype(np.float32)
    cosv = (np.cos(angle) / np.float32(math.sqrt(size))).astype(ml_dtypes.bfloat16).astype(np.float64)
    sinv = (np.sin(angle) / np.float32(math.sqrt(size))).astype(ml_dtypes.bfloat16).astype(np.float64)
    forward = np.block([[cosv, -sinv], [sinv, cosv]])
    inverse = np.block([[cosv, sinv], [-sinv, cosv]])
    freq = np.where(idx < size // 2, idx, idx - size).astype(np.float64)
    phase = -2.0 * math.pi * PROP / size * freq * freq
    real, imag = np.diag(np.cos(phase)), np.diag(np.sin(phase))
    ahead = forward @ np.block([[real, imag], [-imag, real]]) @ inverse
    behind = forward @ np.block([[real, -imag], [imag, real]]) @ inverse
    rows = np.arange(2 * size).reshape(2, size // 8, 8).swapaxes(0, 1).reshape(-1)
    left = [t.T[rows] for t in (forward, inverse, ahead, behind)]
    return np.stack([forward, inverse, ahead, behind, *left]).astype(ml_dtypes.bfloat16)


def mul(a, b):
    return a[0] * b[0] - a[1] * b[1], a[0] * b[1] + a[1] * b[0]


def mulc(a, b):
    return a[0] * b[0] + a[1] * b[1], a[0] * b[1] - a[1] * b[0]


def sine(x):
    y = x * x
    return x * (1.0 - y * (1 / 6) * (1.0 - y * (1 / 20) * (1.0 - y * (1 / 42) * (1.0 - y * (1 / 72)))))


def cosine(x):
    y = x * x
    return 1.0 - y * 0.5 * (1.0 - y * (1 / 12) * (1.0 - y * (1 / 30) * (1.0 - y * (1 / 56) * (1.0 - y * (1 / 90)))))


def transform(waves, right, left):
    size = waves[0][0].shape[0]
    pairs = [waves[first : first + 2] for first in range(0, len(waves), 2)]
    mids = []
    for pair in pairs:
        rows = jnp.concatenate(
            [jnp.concatenate([re.astype(jnp.bfloat16), im.astype(jnp.bfloat16)], 1) for re, im in pair], 0
        )
        mid = jnp.dot(rows, right, preferred_element_type=jnp.float32).astype(jnp.bfloat16)
        cut = [mid[i * size : (i + 1) * size] for i in range(len(pair))]
        mids.append(jnp.concatenate([jnp.concatenate([m[:, :size], m[:, size:]], 0) for m in cut], 1))
    out = []
    for pair, mid in zip(pairs, mids):
        done = jnp.dot(left, mid, preferred_element_type=jnp.float32)
        done = done.reshape(size // 8, 2, 8, -1)
        parts = [done[:, c].reshape(size, -1) for c in range(2)]
        for i in range(len(pair)):
            out.append(tuple(x[:, i * size : (i + 1) * size] for x in parts))
    return out


def swap(values, half):
    return pltpu.roll(values, half, values.ndim - 1)


def low_lanes(shape):
    return lax.broadcasted_iota(jnp.int32, shape, len(shape) - 1) < shape[-1] // 2


def pack(pair):
    half = pair[0].shape[-1] // 2
    low = low_lanes(pair[0].shape)
    return jnp.where(low, pair[0], swap(pair[1], half)), jnp.where(low, swap(pair[0], half), pair[1])


def unpack(lows, highs):
    half = lows.shape[-1] // 2
    low = low_lanes(lows.shape)
    return jnp.where(low, lows, swap(highs, half)), jnp.where(low, swap(lows, half), highs)


def pack_kernel(groups, me_ref, row_ref, col_ref, count_ref, potential_ref, amps_ref, *refs):
    slots = row_ref.shape[0]
    even = lax.rem(me_ref[0], 2) == 0
    _, _, rows, size = potential_ref.shape
    for g, group in enumerate(groups):
        first, second = refs[2 * g : 2 * g + 2]
        for j, s in enumerate(group):
            lows, highs = pack((potential_ref[s, 0], potential_ref[s, 1]))
            first[j * rows : (j + 1) * rows] = jnp.where(even, highs, lows)
            second[j * rows : (j + 1) * rows] = jnp.where(even, lows, highs)
        top = len(group) * rows
        if g == 0:
            lane = lax.broadcasted_iota(jnp.int32, (8, size), 1)
            about = jnp.zeros((8, size), jnp.int32)
            for p in range(slots):
                about = jnp.where(lane == p, row_ref[p], jnp.where(lane == slots + p, col_ref[p], about))
            about = jnp.where(lane == 2 * slots, count_ref[0], about).astype(jnp.float32)
            first[top:] = about
            second[top:] = about
        else:
            for p in range(slots):
                amps = amps_ref[p].astype(jnp.float32)
                first[top + p * size : top + (p + 1) * size] = amps
                second[top + p * size : top + (p + 1) * size] = amps


def transmit(phase, absorption):
    magnitude = jnp.exp(-absorption)
    return magnitude * cosine(phase), magnitude * sine(phase)


def spread_kernel(probe_ref, out_ref):
    for k in range(out_ref.shape[0]):
        out_ref[k] = probe_ref[0]


def gate_kernel(*refs):
    pass


def prepare_kernel(potential_ref, tables_ref, amps_ref, pieces_ref, trans_ref, tables_out, amps_out, probe_ref):
    part = pieces_ref.shape[2]
    for k in range(pieces_ref.shape[0]):
        probe_ref[:, k * part : (k + 1) * part, :] = pieces_ref[k]
    for s in range(potential_ref.shape[0]):
        trans_ref[s, 0], trans_ref[s, 1] = transmit(potential_ref[s, 0], potential_ref[s, 1])
    tables_out[...] = tables_ref[...]
    amps_out[...] = amps_ref[...]


class Names:
    def __init__(self, names, refs):
        self.__dict__.update(zip(names, refs))

    def get(self, name):
        return self.__dict__[name]


def stage_kernel(names, ahead, top, back, pieces, *refs):
    r = Names(names, refs)
    size = r.tables.shape[-1] // 2
    half = size // 2
    modes = r.modes_ref.shape[0]
    slots = r.rows.shape[0]
    me = r.me[0]
    last = me == pieces - 1
    even = lax.rem(me, 2) == 0
    lanes = lax.broadcasted_iota(jnp.int32, (size, size), 1)

    def halves(i, start, count):
        one, two = r.across_even[start : start + count], r.across_odd[start : start + count]
        return jnp.where(even, one, two), jnp.where(even, two, one)

    if 0 in ahead:
        height = r.own.shape[-2]
        about = halves(0, len(ahead) * height, 8)[1][0:1].astype(jnp.int32)
        lane = lanes[0:1]
        number = jnp.int32(0)
        for k in range(2 * slots):
            p = k % slots
            if k < slots:
                row, col, count = r.rows[p], r.cols[p], r.count[0]
                stays = (col < half) | last
            else:
                row, col, count = [jnp.sum(jnp.where(lane == at, about, 0)) for at in (p, slots + p, 2 * slots)]
                stays = col >= half
            r.held_out[3 * number + 1] = jnp.int32(k)
            r.held_out[3 * number + 2] = row
            r.held_out[3 * number + 3] = col
            number = number + ((p < count) & stays).astype(jnp.int32)
        r.held_out[0] = number
        held = r.held_out
    else:
        held = r.held
    number = held[0]

    for i, s in enumerate(ahead):
        height = r.own.shape[-2]
        halo = transmit(*unpack(*halves(0, i * height, height)))
        for c in range(2):
            r.tiles[i, 0, c] = r.own[s, c]
            r.tiles[i, 1, c] = halo[c]
            r.tiles[i, 2, c] = jnp.full((height, size), 1.0 - c, jnp.float32)
    if top:
        begin = len(ahead) * r.own.shape[-2]
        for p in range(slots):
            r.amps_all[p] = r.amps[p].astype(jnp.float32)
            r.amps_all[slots + p] = halves(0, begin + p * size, size)[1]
    if back:
        r.grads[:, 0:2] = jnp.zeros((len(back), 2) + r.grads.shape[2:], jnp.float32)
    if 0 in back:
        r.total[...] = jnp.zeros_like(r.total)

    def load(ref, *lead):
        return [(ref[(*lead, m, slice(None), slice(0, size))], ref[(*lead, m, slice(None), slice(size, None))]) for m in range(modes)]

    def store(ref, waves, *lead):
        for m, (re, im) in enumerate(waves):
            ref[(*lead, m, slice(None), slice(0, size))] = re
            ref[(*lead, m, slice(None), slice(size, None))] = im

    def psi(s, at):
        return load(r.psi_0) if s == 0 else load(r.get("psi_%d" % s), at)

    def trans(s, at):
        ref = r.get("trans_%d" % s)
        return ref[at, 0], ref[at, 1]

    def slot_step(ats, misfit):
        about = [[held[3 * at + 1 + j] for j in range(3)] for at in ats]
        rows_at = [pl.ds(row, size) for _, row, _ in about]
        left = [jnp.where(k < slots, 0, 1) for k, _, _ in about]
        right = [jnp.where(k < slots, jnp.where(last, 2, 1), 0) for k, _, _ in about]
        inside = [lanes >= col for _, _, col in about]
        every = range(len(ats))

        def moved(waves, right_table, left_table):
            flat = transform(sum(waves, []), right_table, left_table)
            return [flat[j * modes : (j + 1) * modes] for j in every]

        for i, s in enumerate(ahead):
            waves = []
            for j in every:
                turn = lax.rem(size - about[j][2], size)
                for c in range(2):
                    both = jnp.where(
                        inside[j], r.tiles[i, left[j], c, rows_at[j], :], r.tiles[i, right[j], c, rows_at[j], :]
                    )
                    r.get("trans_%d" % s)[ats[j], c] = pltpu.roll(both, turn, 1)
                waves.append([mul(trans(s, ats[j]), w) for w in psi(s, ats[j])])
            if top and s == ahead[-1]:
                waves = moved(waves, r.tables[0], r.tables[4])
            else:
                waves = moved(waves, r.tables[2], r.tables[6])
                for j in every:
                    store(r.get("psi_%d" % (s + 1)), waves[j], ats[j])
        if top:
            for j in every:
                inten = sum(re * re + im * im for re, im in waves[j])
                model = jnp.sqrt(inten + REG)
                observed = r.amps_all[about[j][0]]
                diff = model - observed
                misfit = misfit + jnp.sum(diff * diff, axis=0, keepdims=True)
                ratio = 1.0 - observed / model
                waves[j] = [(ratio * re, ratio * im) for re, im in waves[j]]
            waves = moved(waves, r.tables[1], r.tables[5])
        elif back:
            waves = [load(r.wave_in, at) for at in ats]
        for i, s in enumerate(back):
            for j in every:
                waves[j] = [mulc(trans(s, ats[j]), w) for w in waves[j]]
                quot = [mulc(a, w) for a, w in zip(psi(s, ats[j]), waves[j])]
                values = sum(im for _, im in quot), -sum(re for re, _ in quot)
                for c in range(2):
                    turned = pltpu.roll(values[c], about[j][2], 1)
                    r.grads[i, left[j], c, rows_at[j], :] += jnp.where(inside[j], turned, 0.0)
                    r.grads[i, right[j], c, rows_at[j], :] += jnp.where(inside[j], 0.0, turned)
            if s > 0:
                waves = moved(waves, r.tables[3], r.tables[7])
        for j in every:
            if 0 in back:
                for m, (re, im) in enumerate(waves[j]):
                    r.total[m, :, :size] += re
                    r.total[m, :, size:] += im
            elif back or top:
                store(r.wave_out, waves[j], ats[j])
        return misfit

    twos = number // 2
    misfit = lax.fori_loop(0, twos, lambda i, m: slot_step([2 * i, 2 * i + 1], m), jnp.zeros((1, size), jnp.float32))
    misfit = lax.fori_loop(2 * twos, number, lambda i, m: slot_step([i], m), misfit)
    if top:
        value = jnp.sum(misfit, axis=1, keepdims=True)
        lane = lax.broadcasted_iota(jnp.int32, (1, 1, size), 2)
        count = r.count[0].astype(jnp.float32)
        value = jnp.where(lane == 0, value[None], jnp.where(lane == 1, count, 0.0))
        r.sums[...] = jnp.broadcast_to(value[0], r.sums.shape)
    for i, s in enumerate(back):
        r.grad[i] = r.grads[i, 0]
        lows, highs = pack((r.grads[i, 1, 0], r.grads[i, 1, 1]))
        height = lows.shape[0]
        r.for_even[i * height : (i + 1) * height] = jnp.where(even, lows, highs)
        r.for_odd[i * height : (i + 1) * height] = jnp.where(even, highs, lows)
    if 0 in back:
        part = r.total.shape[1] // pieces
        sums = r.sums_in[...]
        for k in range(pieces):
            for m in range(modes):
                r.share[k, m * part : (m + 1) * part] = r.total[m, k * part : (k + 1) * part, :]
            r.share[k, modes * part :] = jnp.concatenate([sums, sums], 1)


def stage(given, made, scratch, ahead, top, back, pieces, name):
    names = [n for n, _, _ in given] + [n for n, _ in made] + [n for n, _ in scratch]
    out = pl.pallas_call(
        functools.partial(stage_kernel, names, ahead, top, back, pieces),
        out_shape=[jax.ShapeDtypeStruct(shape, jnp.float32) for _, shape in made],
        in_specs=[SMEM if small else VMEM for _, _, small in given],
        out_specs=[VMEM] * len(made),
        scratch_shapes=[x for _, x in scratch],
        compiler_params=pltpu.CompilerParams(vmem_limit_bytes=24 * 2**20),
        cost_estimate=pl.CostEstimate(flops=(len(ahead) + len(back) + 1) * 10**9, bytes_accessed=10**7, transcendentals=0),
        name=name,
    )(*[x for _, x, _ in given])
    return dict(zip([n for n, _ in made], out))


def finish_kernel(back, modes, me_ref, late_ref, early_ref, even_in, odd_in, share_in, sums_ref, grad_ref, share_ref):
    even = lax.rem(me_ref[0], 2) == 0
    rows, size = grad_ref.shape[2:]
    part = share_ref.shape[2]
    sums = sums_ref[0:1]
    scale = lax.rsqrt(sums[:, 0:1] / (sums[:, 1:2] * (size * size)) + 1e-06)
    for i, s in enumerate(back):
        one, two = even_in[i * rows : (i + 1) * rows], odd_in[i * rows : (i + 1) * rows]
        arrived = unpack(jnp.where(even, two, one), jnp.where(even, one, two))
        count = late_ref.shape[0]
        for c in range(2):
            own = late_ref[i, c] if i < count else early_ref[i - count, c]
            grad_ref[s, c] = (own + arrived[c]) * scale
    for m in range(modes):
        share_ref[0, m] = jnp.sum(share_in[:, m * part : (m + 1) * part, :], axis=0) * scale


def total_over(value, axis):
    n = lax.axis_size(axis)
    if n & (n - 1):
        return lax.psum(value, axis)
    step = 1
    while step < n:
        ways = 4 if n // step % 4 == 0 else 2
        value = value + sum(
            lax.ppermute(value, axis, [(i, i ^ (step * k)) for i in range(n)]) for k in range(1, ways)
        )
        step *= ways
    return value


def body(potential, probe, amplitudes, row_offset, col_offset, counts):
    slices, _, rows, size = potential.shape
    modes = probe.shape[1]
    part = probe.shape[2]
    slots = row_offset.shape[-1]
    pieces = lax.axis_size("pos")
    cut = slices // 2
    groups = (tuple(range(cut)), tuple(range(cut, slices)))
    f32 = jnp.float32
    me = lax.axis_index("pos").astype(jnp.int32).reshape(1)
    here = [row_offset[0, 0], col_offset[0, 0], counts[0]]

    def exchange(value, first):
        edges = [(i, i + 1) for i in range(first, pieces - 1, 2)]
        return lax.ppermute(value, "pos", edges + [(j, i) for i, j in edges])

    def call(kernel, given, out, name, scratch=(), flops=0):
        return pl.pallas_call(
            kernel,
            out_shape=[x[0] if isinstance(x, tuple) else x for x in out],
            in_specs=[SMEM if jnp.issubdtype(x.dtype, jnp.integer) else VMEM for x in given],
            out_specs=[SMEM if jnp.issubdtype(x.dtype, jnp.integer) else VMEM for x in out],
            scratch_shapes=list(scratch),
            compiler_params=pltpu.CompilerParams(vmem_limit_bytes=24 * 2**20),
            cost_estimate=pl.CostEstimate(flops=flops, bytes_accessed=10**6, transcendentals=0),
            name=name,
        )(*given)

    def array(shape, dtype=f32):
        return jax.ShapeDtypeStruct(shape, dtype)

    def stage(given, made, scratch, ahead, top, back, name):
        given = dict(me=me, rows=here[0], cols=here[1], count=here[2], tables=tables_here, **given)
        scratch = dict(modes_ref=pltpu.SMEM((modes,), jnp.int32), **scratch)
        names = list(given) + list(made) + list(scratch)
        kernel = functools.partial(stage_kernel, names, ahead, top, back, pieces)
        flops = (len(ahead) + len(back) + 1) * 2 * 10**9
        return dict(zip(made, call(kernel, list(given.values()), list(made.values()), name, scratch.values(), flops)))

    (spread,) = call(spread_kernel, [probe], [array((pieces,) + probe.shape[1:])], "spread")
    gathered = lax.all_to_all(spread, "pos", 0, 0)
    heights = [len(groups[0]) * rows + 8, len(groups[1]) * rows + slots * size]
    packed = call(
        functools.partial(pack_kernel, groups),
        [me, *here, potential, amplitudes[0, 0]],
        [array((heights[i // 2], size)) for i in range(4)],
        "pack",
    )
    came = [exchange(packed[i], i % 2) for i in range(4)]
    trans_own, tables_here, amps, probe_all = call(
        prepare_kernel,
        [potential, jnp.asarray(tables(size)), amplitudes[0, 0], gathered],
        [
            array(potential.shape),
            array((8, 2 * size, 2 * size), jnp.bfloat16),
            array((slots, size, size), jnp.bfloat16),
            array((modes, size, 2 * size)),
        ],
        "prepare",
        flops=10**9,
    )

    wave = (2 * slots, modes, size, 2 * size)
    trans = (2 * slots, 2, size, size)
    tiles = lambda n: pltpu.VMEM((n, 3, 2, rows, size), f32)
    sides = lambda n: dict(grad=array((n, 2, rows, size)), for_even=array((n * rows, size)), for_odd=array((n * rows, size)))

    first, second = groups
    a = stage(
        dict(own=trans_own, across_even=came[0], across_odd=came[1], psi_0=probe_all),
        dict(held_out=array((6 * slots + 4,), jnp.int32))
        | {"psi_%d" % (s + 1): array(wave) for s in first}
        | {"trans_%d" % s: array(trans) for s in first},
        dict(tiles=tiles(len(first))),
        first,
        False,
        (),
        "ahead",
    )
    held = a["held_out"]
    b = stage(
        dict(own=trans_own, across_even=came[2], across_odd=came[3], amps=amps, held=held)
        | {"psi_%d" % second[0]: a["psi_%d" % second[0]]},
        dict(sums=array((8, size)), wave_out=array(wave)) | sides(len(second)),
        dict(tiles=tiles(len(second)), grads=tiles(len(second)), amps_all=pltpu.VMEM((2 * slots, size, size), f32))
        | {"psi_%d" % s: pltpu.VMEM(wave, f32) for s in second[1:]}
        | {"trans_%d" % s: pltpu.VMEM(trans, f32) for s in second},
        second,
        True,
        second[::-1],
        "top",
    )
    c = stage(
        dict(held=held, wave_in=b["wave_out"], sums_in=b["sums"])
        | {"psi_%d" % s: probe_all if s == 0 else a["psi_%d" % s] for s in first}
        | {"trans_%d" % s: a["trans_%d" % s] for s in first},
        dict(share=array((pieces, modes * part + 8, 2 * size))) | sides(len(first)),
        dict(grads=tiles(len(first)), total=pltpu.VMEM(wave[1:], f32)),
        (),
        False,
        first[::-1],
        "back",
    )
    join = lambda name: jnp.concatenate([b[name], c[name]], 0)
    got = [exchange(join("for_even"), 0), exchange(join("for_odd"), 1)]
    shares = lax.all_to_all(c["share"], "pos", 0, 0)
    sums = total_over(jnp.sum(shares[:, modes * part :, :size], axis=0), "group")
    return call(
        functools.partial(finish_kernel, second[::-1] + first[::-1], modes),
        [me, b["grad"], c["grad"], *got, shares, sums],
        [array(potential.shape), array(probe.shape)],
        "finish",
    )


def solution(mesh):
    placed = (
        P(None, None, "group", "pos"),
        P("group", None, "pos", None),
        P("group", "pos", None, None, None),
        P("group", "pos", None),
        P("group", "pos", None),
        P("group", "pos"),
    )
    return jax.shard_map(
        body,
        mesh=mesh,
        in_specs=placed,
        out_specs=(P(None, None, "group", "pos"), P("group", None, "pos", None)),
        check_vma=False,
    )
```

```python
import functools
import math

import jax
import jax.numpy as jnp
import ml_dtypes
import numpy as np
from jax import lax
from jax.experimental import pallas as pl
from jax.experimental.pallas import tpu as pltpu
from jax.sharding import PartitionSpec as P

PROP = 0.25
REG = 0.1
VMEM = pl.BlockSpec(memory_space=pltpu.VMEM)
SMEM = pl.BlockSpec(memory_space=pltpu.SMEM)


@functools.lru_cache(maxsize=None)
def tables(size):
    idx = np.arange(size)
    angle = np.float32(2.0 * math.pi / size) * (idx[:, None] * idx[None, :] % size).astype(np.float32)
    cosv = (np.cos(angle) / np.float32(math.sqrt(size))).astype(ml_dtypes.bfloat16).astype(np.float64)
    sinv = (np.sin(angle) / np.float32(math.sqrt(size))).astype(ml_dtypes.bfloat16).astype(np.float64)
    forward = np.block([[cosv, -sinv], [sinv, cosv]])
    inverse = np.block([[cosv, sinv], [-sinv, cosv]])
    freq = np.where(idx < size // 2, idx, idx - size).astype(np.float64)
    phase = -2.0 * math.pi * PROP / size * freq * freq
    real, imag = np.diag(np.cos(phase)), np.diag(np.sin(phase))
    ahead = forward @ np.block([[real, imag], [-imag, real]]) @ inverse
    behind = forward @ np.block([[real, -imag], [imag, real]]) @ inverse
    rows = np.arange(2 * size).reshape(2, size // 8, 8).swapaxes(0, 1).reshape(-1)
    left = [t.T[rows] for t in (forward, inverse, ahead, behind)]
    return np.stack([forward, inverse, ahead, behind, *left]).astype(ml_dtypes.bfloat16)


def mul(a, b):
    return a[0] * b[0] - a[1] * b[1], a[0] * b[1] + a[1] * b[0]


def mulc(a, b):
    return a[0] * b[0] + a[1] * b[1], a[0] * b[1] - a[1] * b[0]


def sine(x):
    y = x * x
    return x * (1.0 - y * (1 / 6) * (1.0 - y * (1 / 20) * (1.0 - y * (1 / 42) * (1.0 - y * (1 / 72)))))


def cosine(x):
    y = x * x
    return 1.0 - y * 0.5 * (1.0 - y * (1 / 12) * (1.0 - y * (1 / 30) * (1.0 - y * (1 / 56) * (1.0 - y * (1 / 90)))))


def transform(waves, right, left):
    size = waves[0][0].shape[0]
    pairs = [waves[first : first + 2] for first in range(0, len(waves), 2)]
    mids = []
    for pair in pairs:
        rows = jnp.concatenate(
            [jnp.concatenate([re.astype(jnp.bfloat16), im.astype(jnp.bfloat16)], 1) for re, im in pair], 0
        )
        mid = jnp.dot(rows, right, preferred_element_type=jnp.float32).astype(jnp.bfloat16)
        cut = [mid[i * size : (i + 1) * size] for i in range(len(pair))]
        mids.append(jnp.concatenate([jnp.concatenate([m[:, :size], m[:, size:]], 0) for m in cut], 1))
    out = []
    for pair, mid in zip(pairs, mids):
        done = jnp.dot(left, mid, preferred_element_type=jnp.float32)
        done = done.reshape(size // 8, 2, 8, -1)
        parts = [done[:, c].reshape(size, -1) for c in range(2)]
        for i in range(len(pair)):
            out.append(tuple(x[:, i * size : (i + 1) * size] for x in parts))
    return out


def swap(values, half):
    return pltpu.roll(values, half, values.ndim - 1)


def low_lanes(shape):
    return lax.broadcasted_iota(jnp.int32, shape, len(shape) - 1) < shape[-1] // 2


def pack(pair):
    half = pair[0].shape[-1] // 2
    low = low_lanes(pair[0].shape)
    return jnp.where(low, pair[0], swap(pair[1], half)), jnp.where(low, swap(pair[0], half), pair[1])


def unpack(lows, highs):
    half = lows.shape[-1] // 2
    low = low_lanes(lows.shape)
    return jnp.where(low, lows, swap(highs, half)), jnp.where(low, swap(lows, half), highs)


def pack_kernel(groups, me_ref, row_ref, col_ref, count_ref, potential_ref, amps_ref, *refs):
    slots = row_ref.shape[0]
    even = lax.rem(me_ref[0], 2) == 0
    _, _, rows, size = potential_ref.shape
    for g, group in enumerate(groups):
        first, second = refs[2 * g : 2 * g + 2]
        for j, s in enumerate(group):
            lows, highs = pack((potential_ref[s, 0], potential_ref[s, 1]))
            first[j * rows : (j + 1) * rows] = jnp.where(even, highs, lows)
            second[j * rows : (j + 1) * rows] = jnp.where(even, lows, highs)
        top = len(group) * rows
        if g == 0:
            lane = lax.broadcasted_iota(jnp.int32, (8, size), 1)
            about = jnp.zeros((8, size), jnp.int32)
            for p in range(slots):
                about = jnp.where(lane == p, row_ref[p], jnp.where(lane == slots + p, col_ref[p], about))
            about = jnp.where(lane == 2 * slots, count_ref[0], about).astype(jnp.float32)
            first[top:] = about
            second[top:] = about
        else:
            for p in range(slots):
                amps = amps_ref[p].astype(jnp.float32)
                first[top + p * size : top + (p + 1) * size] = amps
                second[top + p * size : top + (p + 1) * size] = amps


def transmit(phase, absorption):
    magnitude = jnp.exp(-absorption)
    return magnitude * cosine(phase), magnitude * sine(phase)


def spread_kernel(probe_ref, out_ref):
    for k in range(out_ref.shape[0]):
        out_ref[k] = probe_ref[0]


def gate_kernel(*refs):
    pass


def prepare_kernel(potential_ref, tables_ref, amps_ref, pieces_ref, trans_ref, tables_out, amps_out, probe_ref):
    part = pieces_ref.shape[2]
    for k in range(pieces_ref.shape[0]):
        probe_ref[:, k * part : (k + 1) * part, :] = pieces_ref[k]
    for s in range(potential_ref.shape[0]):
        trans_ref[s, 0], trans_ref[s, 1] = transmit(potential_ref[s, 0], potential_ref[s, 1])
    tables_out[...] = tables_ref[...]
    amps_out[...] = amps_ref[...]


class Names:
    def __init__(self, names, refs):
        self.__dict__.update(zip(names, refs))

    def get(self, name):
        return self.__dict__[name]


def stage_kernel(names, ahead, top, back, pieces, *refs):
    r = Names(names, refs)
    size = r.tables.shape[-1] // 2
    half = size // 2
    modes = r.modes_ref.shape[0]
    slots = r.rows.shape[0]
    me = r.me[0]
    last = me == pieces - 1
    even = lax.rem(me, 2) == 0
    lanes = lax.broadcasted_iota(jnp.int32, (size, size), 1)

    def halves(i, start, count):
        one, two = r.across_even[start : start + count], r.across_odd[start : start + count]
        return jnp.where(even, one, two), jnp.where(even, two, one)

    if 0 in ahead:
        height = r.own.shape[-2]
        about = halves(0, len(ahead) * height, 8)[1][0:1].astype(jnp.int32)
        lane = lanes[0:1]
        number = jnp.int32(0)
        for k in range(2 * slots):
            p = k % slots
            if k < slots:
                row, col, count = r.rows[p], r.cols[p], r.count[0]
                stays = (col < half) | last
            else:
                row, col, count = [jnp.sum(jnp.where(lane == at, about, 0)) for at in (p, slots + p, 2 * slots)]
                stays = col >= half
            r.held_out[3 * number + 1] = jnp.int32(k)
            r.held_out[3 * number + 2] = row
            r.held_out[3 * number + 3] = col
            number = number + ((p < count) & stays).astype(jnp.int32)
        r.held_out[0] = number
        held = r.held_out
    else:
        held = r.held
    number = held[0]

    for i, s in enumerate(ahead):
        height = r.own.shape[-2]
        halo = transmit(*unpack(*halves(0, i * height, height)))
        for c in range(2):
            r.tiles[i, 0, c] = r.own[s, c]
            r.tiles[i, 1, c] = halo[c]
            r.tiles[i, 2, c] = jnp.full((height, size), 1.0 - c, jnp.float32)
    if top:
        begin = len(ahead) * r.own.shape[-2]
        for p in range(slots):
            r.amps_all[p] = r.amps[p].astype(jnp.float32)
            r.amps_all[slots + p] = halves(0, begin + p * size, size)[1]
    if back:
        r.grads[:, 0:2] = jnp.zeros((len(back), 2) + r.grads.shape[2:], jnp.float32)
    if 0 in back:
        r.total[...] = jnp.zeros_like(r.total)

    def load(ref, *lead):
        return [(ref[(*lead, m, slice(None), slice(0, size))], ref[(*lead, m, slice(None), slice(size, None))]) for m in range(modes)]

    def store(ref, waves, *lead):
        for m, (re, im) in enumerate(waves):
            ref[(*lead, m, slice(None), slice(0, size))] = re
            ref[(*lead, m, slice(None), slice(size, None))] = im

    def psi(s, at):
        return load(r.psi_0) if s == 0 else load(r.get("psi_%d" % s), at)

    def trans(s, at):
        ref = r.get("trans_%d" % s)
        return ref[at, 0], ref[at, 1]

    def slot_step(ats, misfit):
        about = [[held[3 * at + 1 + j] for j in range(3)] for at in ats]
        rows_at = [pl.ds(row, size) for _, row, _ in about]
        left = [jnp.where(k < slots, 0, 1) for k, _, _ in about]
        right = [jnp.where(k < slots, jnp.where(last, 2, 1), 0) for k, _, _ in about]
        inside = [lanes >= col for _, _, col in about]
        every = range(len(ats))

        def moved(waves, right_table, left_table):
            flat = transform(sum(waves, []), right_table, left_table)
            return [flat[j * modes : (j + 1) * modes] for j in every]

        for i, s in enumerate(ahead):
            waves = []
            for j in every:
                turn = lax.rem(size - about[j][2], size)
                for c in range(2):
                    both = jnp.where(
                        inside[j], r.tiles[i, left[j], c, rows_at[j], :], r.tiles[i, right[j], c, rows_at[j], :]
                    )
                    r.get("trans_%d" % s)[ats[j], c] = pltpu.roll(both, turn, 1)
                waves.append([mul(trans(s, ats[j]), w) for w in psi(s, ats[j])])
            if top and s == ahead[-1]:
                waves = moved(waves, r.tables[0], r.tables[4])
            else:
                waves = moved(waves, r.tables[2], r.tables[6])
                for j in every:
                    store(r.get("psi_%d" % (s + 1)), waves[j], ats[j])
        if top:
            for j in every:
                inten = sum(re * re + im * im for re, im in waves[j])
                model = jnp.sqrt(inten + REG)
                observed = r.amps_all[about[j][0]]
                diff = model - observed
                misfit = misfit + jnp.sum(diff * diff, axis=0, keepdims=True)
                ratio = 1.0 - observed / model
                waves[j] = [(ratio * re, ratio * im) for re, im in waves[j]]
            waves = moved(waves, r.tables[1], r.tables[5])
        elif back:
            waves = [load(r.wave_in, at) for at in ats]
        for i, s in enumerate(back):
            for j in every:
                waves[j] = [mulc(trans(s, ats[j]), w) for w in waves[j]]
                quot = [mulc(a, w) for a, w in zip(psi(s, ats[j]), waves[j])]
                values = sum(im for _, im in quot), -sum(re for re, _ in quot)
                for c in range(2):
                    turned = pltpu.roll(values[c], about[j][2], 1)
                    r.grads[i, left[j], c, rows_at[j], :] += jnp.where(inside[j], turned, 0.0)
                    r.grads[i, right[j], c, rows_at[j], :] += jnp.where(inside[j], 0.0, turned)
            if s > 0:
                waves = moved(waves, r.tables[3], r.tables[7])
        for j in every:
            if 0 in back:
                for m, (re, im) in enumerate(waves[j]):
                    r.total[m, :, :size] += re
                    r.total[m, :, size:] += im
            elif back or top:
                store(r.wave_out, waves[j], ats[j])
        return misfit

    odd = lax.rem(number, 2)
    threes = jnp.where(number > 2, odd, 0)
    zero = jnp.zeros((1, size), jnp.float32)
    misfit = lax.fori_loop(0, threes, lambda i, m: slot_step([0, 1, 2], m), zero)
    misfit = lax.fori_loop(0, odd - threes, lambda i, m: slot_step([0], m), misfit)
    begin = 2 * threes + odd
    misfit = lax.fori_loop(0, number // 2 - threes, lambda i, m: slot_step([begin + 2 * i, begin + 2 * i + 1], m), misfit)
    if top:
        value = jnp.sum(misfit, axis=1, keepdims=True)
        lane = lax.broadcasted_iota(jnp.int32, (1, 1, size), 2)
        count = r.count[0].astype(jnp.float32)
        value = jnp.where(lane == 0, value[None], jnp.where(lane == 1, count, 0.0))
        r.sums[...] = jnp.broadcast_to(value[0], r.sums.shape)
    for i, s in enumerate(back):
        r.grad[i] = r.grads[i, 0]
        lows, highs = pack((r.grads[i, 1, 0], r.grads[i, 1, 1]))
        height = lows.shape[0]
        r.for_even[i * height : (i + 1) * height] = jnp.where(even, lows, highs)
        r.for_odd[i * height : (i + 1) * height] = jnp.where(even, highs, lows)
    if 0 in back:
        part = r.total.shape[1] // pieces
        sums = r.sums_in[...]
        for k in range(pieces):
            for m in range(modes):
                r.share[k, m * part : (m + 1) * part] = r.total[m, k * part : (k + 1) * part, :]
            r.share[k, modes * part :] = jnp.concatenate([sums, sums], 1)


def stage(given, made, scratch, ahead, top, back, pieces, name):
    names = [n for n, _, _ in given] + [n for n, _ in made] + [n for n, _ in scratch]
    out = pl.pallas_call(
        functools.partial(stage_kernel, names, ahead, top, back, pieces),
        out_shape=[jax.ShapeDtypeStruct(shape, jnp.float32) for _, shape in made],
        in_specs=[SMEM if small else VMEM for _, _, small in given],
        out_specs=[VMEM] * len(made),
        scratch_shapes=[x for _, x in scratch],
        compiler_params=pltpu.CompilerParams(vmem_limit_bytes=24 * 2**20),
        cost_estimate=pl.CostEstimate(flops=(len(ahead) + len(back) + 1) * 10**9, bytes_accessed=10**7, transcendentals=0),
        name=name,
    )(*[x for _, x, _ in given])
    return dict(zip([n for n, _ in made], out))


def finish_kernel(back, modes, me_ref, late_ref, early_ref, even_in, odd_in, share_in, sums_ref, grad_ref, share_ref):
    even = lax.rem(me_ref[0], 2) == 0
    rows, size = grad_ref.shape[2:]
    part = share_ref.shape[2]
    sums = sums_ref[0:1]
    scale = lax.rsqrt(sums[:, 0:1] / (sums[:, 1:2] * (size * size)) + 1e-06)
    for i, s in enumerate(back):
        one, two = even_in[i * rows : (i + 1) * rows], odd_in[i * rows : (i + 1) * rows]
        arrived = unpack(jnp.where(even, two, one), jnp.where(even, one, two))
        count = late_ref.shape[0]
        for c in range(2):
            own = late_ref[i, c] if i < count else early_ref[i - count, c]
            grad_ref[s, c] = (own + arrived[c]) * scale
    for m in range(modes):
        share_ref[0, m] = jnp.sum(share_in[:, m * part : (m + 1) * part, :], axis=0) * scale


def total_over(value, axis):
    n = lax.axis_size(axis)
    if n & (n - 1):
        return lax.psum(value, axis)
    step = 1
    while step < n:
        ways = 4 if n // step % 4 == 0 else 2
        value = value + sum(
            lax.ppermute(value, axis, [(i, i ^ (step * k)) for i in range(n)]) for k in range(1, ways)
        )
        step *= ways
    return value


def body(potential, probe, amplitudes, row_offset, col_offset, counts):
    slices, _, rows, size = potential.shape
    modes = probe.shape[1]
    part = probe.shape[2]
    slots = row_offset.shape[-1]
    pieces = lax.axis_size("pos")
    cut = slices // 2
    groups = (tuple(range(cut)), tuple(range(cut, slices)))
    f32 = jnp.float32
    me = lax.axis_index("pos").astype(jnp.int32).reshape(1)
    here = [row_offset[0, 0], col_offset[0, 0], counts[0]]

    def exchange(value, first):
        edges = [(i, i + 1) for i in range(first, pieces - 1, 2)]
        return lax.ppermute(value, "pos", edges + [(j, i) for i, j in edges])

    def call(kernel, given, out, name, scratch=(), flops=0):
        return pl.pallas_call(
            kernel,
            out_shape=[x[0] if isinstance(x, tuple) else x for x in out],
            in_specs=[SMEM if jnp.issubdtype(x.dtype, jnp.integer) else VMEM for x in given],
            out_specs=[SMEM if jnp.issubdtype(x.dtype, jnp.integer) else VMEM for x in out],
            scratch_shapes=list(scratch),
            compiler_params=pltpu.CompilerParams(vmem_limit_bytes=24 * 2**20),
            cost_estimate=pl.CostEstimate(flops=flops, bytes_accessed=10**6, transcendentals=0),
            name=name,
        )(*given)

    def array(shape, dtype=f32):
        return jax.ShapeDtypeStruct(shape, dtype)

    def stage(given, made, scratch, ahead, top, back, name):
        given = dict(me=me, rows=here[0], cols=here[1], count=here[2], tables=tables_here, **given)
        scratch = dict(modes_ref=pltpu.SMEM((modes,), jnp.int32), **scratch)
        names = list(given) + list(made) + list(scratch)
        kernel = functools.partial(stage_kernel, names, ahead, top, back, pieces)
        flops = (len(ahead) + len(back) + 1) * 2 * 10**9
        return dict(zip(made, call(kernel, list(given.values()), list(made.values()), name, scratch.values(), flops)))

    (spread,) = call(spread_kernel, [probe], [array((pieces,) + probe.shape[1:])], "spread")
    gathered = lax.all_to_all(spread, "pos", 0, 0)
    heights = [len(groups[0]) * rows + 8, len(groups[1]) * rows + slots * size]
    packed = call(
        functools.partial(pack_kernel, groups),
        [me, *here, potential, amplitudes[0, 0]],
        [array((heights[i // 2], size)) for i in range(4)],
        "pack",
    )
    came = [exchange(packed[i], i % 2) for i in range(4)]
    trans_own, tables_here, amps, probe_all = call(
        prepare_kernel,
        [potential, jnp.asarray(tables(size)), amplitudes[0, 0], gathered],
        [
            array(potential.shape),
            array((8, 2 * size, 2 * size), jnp.bfloat16),
            array((slots, size, size), jnp.bfloat16),
            array((modes, size, 2 * size)),
        ],
        "prepare",
        flops=10**9,
    )

    wave = (2 * slots, modes, size, 2 * size)
    trans = (2 * slots, 2, size, size)
    tiles = lambda n: pltpu.VMEM((n, 3, 2, rows, size), f32)
    sides = lambda n: dict(grad=array((n, 2, rows, size)), for_even=array((n * rows, size)), for_odd=array((n * rows, size)))

    first, second = groups
    a = stage(
        dict(own=trans_own, across_even=came[0], across_odd=came[1], psi_0=probe_all),
        dict(held_out=array((6 * slots + 4,), jnp.int32))
        | {"psi_%d" % (s + 1): array(wave) for s in first}
        | {"trans_%d" % s: array(trans) for s in first},
        dict(tiles=tiles(len(first))),
        first,
        False,
        (),
        "ahead",
    )
    held = a["held_out"]
    b = stage(
        dict(own=trans_own, across_even=came[2], across_odd=came[3], amps=amps, held=held)
        | {"psi_%d" % second[0]: a["psi_%d" % second[0]]},
        dict(sums=array((8, size)), wave_out=array(wave)) | sides(len(second)),
        dict(tiles=tiles(len(second)), grads=tiles(len(second)), amps_all=pltpu.VMEM((2 * slots, size, size), f32))
        | {"psi_%d" % s: pltpu.VMEM(wave, f32) for s in second[1:]}
        | {"trans_%d" % s: pltpu.VMEM(trans, f32) for s in second},
        second,
        True,
        second[::-1],
        "top",
    )
    c = stage(
        dict(held=held, wave_in=b["wave_out"], sums_in=b["sums"])
        | {"psi_%d" % s: probe_all if s == 0 else a["psi_%d" % s] for s in first}
        | {"trans_%d" % s: a["trans_%d" % s] for s in first},
        dict(share=array((pieces, modes * part + 8, 2 * size))) | sides(len(first)),
        dict(grads=tiles(len(first)), total=pltpu.VMEM(wave[1:], f32)),
        (),
        False,
        first[::-1],
        "back",
    )
    join = lambda name: jnp.concatenate([b[name], c[name]], 0)
    got = [exchange(join("for_even"), 0), exchange(join("for_odd"), 1)]
    shares = lax.all_to_all(c["share"], "pos", 0, 0)
    sums = total_over(jnp.sum(shares[:, modes * part :, :size], axis=0), "group")
    return call(
        functools.partial(finish_kernel, second[::-1] + first[::-1], modes),
        [me, b["grad"], c["grad"], *got, shares, sums],
        [array(potential.shape), array(probe.shape)],
        "finish",
    )


def solution(mesh):
    placed = (
        P(None, None, "group", "pos"),
        P("group", None, "pos", None),
        P("group", "pos", None, None, None),
        P("group", "pos", None),
        P("group", "pos", None),
        P("group", "pos"),
    )
    return jax.shard_map(
        body,
        mesh=mesh,
        in_specs=placed,
        out_specs=(P(None, None, "group", "pos"), P("group", None, "pos", None)),
        check_vma=False,
    )
```

```python
import functools
import math

import jax
import jax.numpy as jnp
import ml_dtypes
import numpy as np
from jax import lax
from jax.experimental import pallas as pl
from jax.experimental.pallas import tpu as pltpu
from jax.sharding import PartitionSpec as P

PROP = 0.25
REG = 0.1
VMEM = pl.BlockSpec(memory_space=pltpu.VMEM)
SMEM = pl.BlockSpec(memory_space=pltpu.SMEM)


@functools.lru_cache(maxsize=None)
def tables(size):
    idx = np.arange(size)
    angle = np.float32(2.0 * math.pi / size) * (idx[:, None] * idx[None, :] % size).astype(np.float32)
    cosv = (np.cos(angle) / np.float32(math.sqrt(size))).astype(ml_dtypes.bfloat16).astype(np.float64)
    sinv = (np.sin(angle) / np.float32(math.sqrt(size))).astype(ml_dtypes.bfloat16).astype(np.float64)
    forward = np.block([[cosv, -sinv], [sinv, cosv]])
    inverse = np.block([[cosv, sinv], [-sinv, cosv]])
    freq = np.where(idx < size // 2, idx, idx - size).astype(np.float64)
    phase = -2.0 * math.pi * PROP / size * freq * freq
    real, imag = np.diag(np.cos(phase)), np.diag(np.sin(phase))
    ahead = forward @ np.block([[real, imag], [-imag, real]]) @ inverse
    behind = forward @ np.block([[real, -imag], [imag, real]]) @ inverse
    rows = np.arange(2 * size).reshape(2, size // 8, 8).swapaxes(0, 1).reshape(-1)
    left = [t.T[rows] for t in (forward, inverse, ahead, behind)]
    return np.stack([forward, inverse, ahead, behind, *left]).astype(ml_dtypes.bfloat16)


def mul(a, b):
    return a[0] * b[0] - a[1] * b[1], a[0] * b[1] + a[1] * b[0]


def mulc(a, b):
    return a[0] * b[0] + a[1] * b[1], a[0] * b[1] - a[1] * b[0]


def sine(x):
    y = x * x
    return x * (1.0 - y * (1 / 6) * (1.0 - y * (1 / 20) * (1.0 - y * (1 / 42) * (1.0 - y * (1 / 72)))))


def cosine(x):
    y = x * x
    return 1.0 - y * 0.5 * (1.0 - y * (1 / 12) * (1.0 - y * (1 / 30) * (1.0 - y * (1 / 56) * (1.0 - y * (1 / 90)))))


def transform(waves, right, left):
    size = waves[0][0].shape[0]
    pairs = [waves[first : first + 2] for first in range(0, len(waves), 2)]
    mids = []
    for pair in pairs:
        rows = jnp.concatenate(
            [jnp.concatenate([re.astype(jnp.bfloat16), im.astype(jnp.bfloat16)], 1) for re, im in pair], 0
        )
        mid = jnp.dot(rows, right, preferred_element_type=jnp.float32).astype(jnp.bfloat16)
        cut = [mid[i * size : (i + 1) * size] for i in range(len(pair))]
        mids.append(jnp.concatenate([jnp.concatenate([m[:, :size], m[:, size:]], 0) for m in cut], 1))
    out = []
    for pair, mid in zip(pairs, mids):
        done = jnp.dot(left, mid, preferred_element_type=jnp.float32)
        done = done.reshape(size // 8, 2, 8, -1)
        parts = [done[:, c].reshape(size, -1) for c in range(2)]
        for i in range(len(pair)):
            out.append(tuple(x[:, i * size : (i + 1) * size] for x in parts))
    return out


def swap(values, half):
    return pltpu.roll(values, half, values.ndim - 1)


def low_lanes(shape):
    return lax.broadcasted_iota(jnp.int32, shape, len(shape) - 1) < shape[-1] // 2


def pack(pair):
    half = pair[0].shape[-1] // 2
    low = low_lanes(pair[0].shape)
    return jnp.where(low, pair[0], swap(pair[1], half)), jnp.where(low, swap(pair[0], half), pair[1])


def unpack(lows, highs):
    half = lows.shape[-1] // 2
    low = low_lanes(lows.shape)
    return jnp.where(low, lows, swap(highs, half)), jnp.where(low, swap(lows, half), highs)


def pack_kernel(groups, me_ref, row_ref, col_ref, count_ref, potential_ref, amps_ref, *refs):
    slots = row_ref.shape[0]
    even = lax.rem(me_ref[0], 2) == 0
    _, _, rows, size = potential_ref.shape
    for g, group in enumerate(groups):
        first, second = refs[2 * g : 2 * g + 2]
        for j, s in enumerate(group):
            lows, highs = pack((potential_ref[s, 0], potential_ref[s, 1]))
            first[j * rows : (j + 1) * rows] = jnp.where(even, highs, lows)
            second[j * rows : (j + 1) * rows] = jnp.where(even, lows, highs)
        top = len(group) * rows
        if g == 0:
            lane = lax.broadcasted_iota(jnp.int32, (8, size), 1)
            about = jnp.zeros((8, size), jnp.int32)
            for p in range(slots):
                about = jnp.where(lane == p, row_ref[p], jnp.where(lane == slots + p, col_ref[p], about))
            about = jnp.where(lane == 2 * slots, count_ref[0], about).astype(jnp.float32)
            first[top:] = about
            second[top:] = about
        else:
            for p in range(slots):
                amps = amps_ref[p].astype(jnp.float32)
                first[top + p * size : top + (p + 1) * size] = amps
                second[top + p * size : top + (p + 1) * size] = amps


def transmit(phase, absorption):
    magnitude = jnp.exp(-absorption)
    return magnitude * cosine(phase), magnitude * sine(phase)


def spread_kernel(probe_ref, out_ref):
    for k in range(out_ref.shape[0]):
        out_ref[k] = probe_ref[0]


def gate_kernel(*refs):
    pass


def prepare_kernel(potential_ref, tables_ref, amps_ref, pieces_ref, trans_ref, tables_out, amps_out, probe_ref):
    part = pieces_ref.shape[2]
    for k in range(pieces_ref.shape[0]):
        probe_ref[:, k * part : (k + 1) * part, :] = pieces_ref[k]
    for s in range(potential_ref.shape[0]):
        trans_ref[s, 0], trans_ref[s, 1] = transmit(potential_ref[s, 0], potential_ref[s, 1])
    tables_out[...] = tables_ref[...]
    amps_out[...] = amps_ref[...]


class Names:
    def __init__(self, names, refs):
        self.__dict__.update(zip(names, refs))

    def get(self, name):
        return self.__dict__[name]


def stage_kernel(names, ahead, top, back, pieces, *refs):
    r = Names(names, refs)
    size = r.tables.shape[-1] // 2
    half = size // 2
    modes = r.modes_ref.shape[0]
    slots = r.rows.shape[0]
    me = r.me[0]
    last = me == pieces - 1
    even = lax.rem(me, 2) == 0
    lanes = lax.broadcasted_iota(jnp.int32, (size, size), 1)

    def halves(i, start, count):
        one, two = r.across_even[start : start + count], r.across_odd[start : start + count]
        return jnp.where(even, one, two), jnp.where(even, two, one)

    if 0 in ahead:
        height = r.own.shape[-2]
        about = halves(0, len(ahead) * height, 8)[1][0:1].astype(jnp.int32)
        lane = lanes[0:1]
        number = jnp.int32(0)
        for k in range(2 * slots):
            p = k % slots
            if k < slots:
                row, col, count = r.rows[p], r.cols[p], r.count[0]
                stays = (col < half) | last
            else:
                row, col, count = [jnp.sum(jnp.where(lane == at, about, 0)) for at in (p, slots + p, 2 * slots)]
                stays = col >= half
            r.held_out[3 * number + 1] = jnp.int32(k)
            r.held_out[3 * number + 2] = row
            r.held_out[3 * number + 3] = col
            number = number + ((p < count) & stays).astype(jnp.int32)
        r.held_out[0] = number
        held = r.held_out
    else:
        held = r.held
    number = held[0]

    for i, s in enumerate(ahead):
        height = r.own.shape[-2]
        halo = transmit(*unpack(*halves(0, i * height, height)))
        for c in range(2):
            r.tiles[i, 0, c] = r.own[s, c]
            r.tiles[i, 1, c] = halo[c]
            r.tiles[i, 2, c] = jnp.full((height, size), 1.0 - c, jnp.float32)
    if top:
        begin = len(ahead) * r.own.shape[-2]
        for p in range(slots):
            r.amps_all[p] = r.amps[p].astype(jnp.float32)
            r.amps_all[slots + p] = halves(0, begin + p * size, size)[1]
    if back:
        r.grads[:, 0:2] = jnp.zeros((len(back), 2) + r.grads.shape[2:], jnp.float32)
    if 0 in back:
        r.total[...] = jnp.zeros_like(r.total)

    def load(ref, *lead):
        return [(ref[(*lead, m, slice(None), slice(0, size))], ref[(*lead, m, slice(None), slice(size, None))]) for m in range(modes)]

    def store(ref, waves, *lead):
        for m, (re, im) in enumerate(waves):
            ref[(*lead, m, slice(None), slice(0, size))] = re
            ref[(*lead, m, slice(None), slice(size, None))] = im

    def psi(s, at):
        return load(r.psi_0) if s == 0 else load(r.get("psi_%d" % s), at)

    def trans(s, at):
        ref = r.get("trans_%d" % s)
        return ref[at, 0], ref[at, 1]

    def slot_step(ats, misfit):
        about = [[held[3 * at + 1 + j] for j in range(3)] for at in ats]
        rows_at = [pl.ds(row, size) for _, row, _ in about]
        left = [jnp.where(k < slots, 0, 1) for k, _, _ in about]
        right = [jnp.where(k < slots, jnp.where(last, 2, 1), 0) for k, _, _ in about]
        inside = [lanes >= col for _, _, col in about]
        every = range(len(ats))

        def moved(waves, right_table, left_table):
            flat = transform(sum(waves, []), right_table, left_table)
            return [flat[j * modes : (j + 1) * modes] for j in every]

        for i, s in enumerate(ahead):
            waves = []
            for j in every:
                turn = lax.rem(size - about[j][2], size)
                for c in range(2):
                    both = jnp.where(
                        inside[j], r.tiles[i, left[j], c, rows_at[j], :], r.tiles[i, right[j], c, rows_at[j], :]
                    )
                    r.get("trans_%d" % s)[ats[j], c] = pltpu.roll(both, turn, 1)
                waves.append([mul(trans(s, ats[j]), w) for w in psi(s, ats[j])])
            if top and s == ahead[-1]:
                waves = moved(waves, r.tables[0], r.tables[4])
            else:
                waves = moved(waves, r.tables[2], r.tables[6])
                for j in every:
                    store(r.get("psi_%d" % (s + 1)), waves[j], ats[j])
        if top:
            for j in every:
                inten = sum(re * re + im * im for re, im in waves[j])
                model = jnp.sqrt(inten + REG)
                observed = r.amps_all[about[j][0]]
                diff = model - observed
                misfit = misfit + jnp.sum(diff * diff, axis=0, keepdims=True)
                ratio = 1.0 - observed / model
                waves[j] = [(ratio * re, ratio * im) for re, im in waves[j]]
            waves = moved(waves, r.tables[1], r.tables[5])
        elif back:
            waves = [load(r.wave_in, at) for at in ats]
        for i, s in enumerate(back):
            for j in every:
                waves[j] = [mulc(trans(s, ats[j]), w) for w in waves[j]]
                quot = [mulc(a, w) for a, w in zip(psi(s, ats[j]), waves[j])]
                values = sum(im for _, im in quot), -sum(re for re, _ in quot)
                for c in range(2):
                    turned = pltpu.roll(values[c], about[j][2], 1)
                    r.grads[i, left[j], c, rows_at[j], :] += jnp.where(inside[j], turned, 0.0)
                    r.grads[i, right[j], c, rows_at[j], :] += jnp.where(inside[j], 0.0, turned)
            if s > 0:
                waves = moved(waves, r.tables[3], r.tables[7])
        for j in every:
            if 0 in back:
                for m, (re, im) in enumerate(waves[j]):
                    r.total[m, :, :size] += re
                    r.total[m, :, size:] += im
            elif back or top:
                store(r.wave_out, waves[j], ats[j])
        return misfit

    misfit = jnp.zeros((1, size), jnp.float32)
    fives = jnp.where(number > 6, number // 5, (number == 5).astype(jnp.int32))
    begin = 5 * fives
    rest = number - begin
    steps = [(rest == width).astype(jnp.int32) for width in range(1, 5)] + [fives]
    steps[2] += 2 * (rest == 6).astype(jnp.int32)
    for width, count in zip(range(1, 6), steps):
        first = 0 if width == 5 else begin

        def step(i, total, width=width, first=first):
            return slot_step([first + width * i + j for j in range(width)], total)

        misfit = lax.fori_loop(0, count, step, misfit)
    if top:
        value = jnp.sum(misfit, axis=1, keepdims=True)
        lane = lax.broadcasted_iota(jnp.int32, (1, 1, size), 2)
        count = r.count[0].astype(jnp.float32)
        value = jnp.where(lane == 0, value[None], jnp.where(lane == 1, count, 0.0))
        r.sums[...] = jnp.broadcast_to(value[0], r.sums.shape)
    for i, s in enumerate(back):
        r.grad[i] = r.grads[i, 0]
        lows, highs = pack((r.grads[i, 1, 0], r.grads[i, 1, 1]))
        height = lows.shape[0]
        r.for_even[i * height : (i + 1) * height] = jnp.where(even, lows, highs)
        r.for_odd[i * height : (i + 1) * height] = jnp.where(even, highs, lows)
    if 0 in back:
        part = r.total.shape[1] // pieces
        sums = r.sums_in[...]
        for k in range(pieces):
            for m in range(modes):
                r.share[k, m * part : (m + 1) * part] = r.total[m, k * part : (k + 1) * part, :]
            r.share[k, modes * part :] = jnp.concatenate([sums, sums], 1)


def stage(given, made, scratch, ahead, top, back, pieces, name):
    names = [n for n, _, _ in given] + [n for n, _ in made] + [n for n, _ in scratch]
    out = pl.pallas_call(
        functools.partial(stage_kernel, names, ahead, top, back, pieces),
        out_shape=[jax.ShapeDtypeStruct(shape, jnp.float32) for _, shape in made],
        in_specs=[SMEM if small else VMEM for _, _, small in given],
        out_specs=[VMEM] * len(made),
        scratch_shapes=[x for _, x in scratch],
        compiler_params=pltpu.CompilerParams(vmem_limit_bytes=24 * 2**20),
        cost_estimate=pl.CostEstimate(flops=(len(ahead) + len(back) + 1) * 10**9, bytes_accessed=10**7, transcendentals=0),
        name=name,
    )(*[x for _, x, _ in given])
    return dict(zip([n for n, _ in made], out))


def finish_kernel(back, modes, me_ref, late_ref, early_ref, even_in, odd_in, share_in, sums_ref, grad_ref, share_ref):
    even = lax.rem(me_ref[0], 2) == 0
    rows, size = grad_ref.shape[2:]
    part = share_ref.shape[2]
    sums = sums_ref[0:1]
    scale = lax.rsqrt(sums[:, 0:1] / (sums[:, 1:2] * (size * size)) + 1e-06)
    for i, s in enumerate(back):
        one, two = even_in[i * rows : (i + 1) * rows], odd_in[i * rows : (i + 1) * rows]
        arrived = unpack(jnp.where(even, two, one), jnp.where(even, one, two))
        count = late_ref.shape[0]
        for c in range(2):
            own = late_ref[i, c] if i < count else early_ref[i - count, c]
            grad_ref[s, c] = (own + arrived[c]) * scale
    for m in range(modes):
        share_ref[0, m] = jnp.sum(share_in[:, m * part : (m + 1) * part, :], axis=0) * scale


def total_over(value, axis):
    n = lax.axis_size(axis)
    if n & (n - 1):
        return lax.psum(value, axis)
    step = 1
    while step < n:
        ways = 4 if n // step % 4 == 0 else 2
        value = value + sum(
            lax.ppermute(value, axis, [(i, i ^ (step * k)) for i in range(n)]) for k in range(1, ways)
        )
        step *= ways
    return value


def body(potential, probe, amplitudes, row_offset, col_offset, counts):
    slices, _, rows, size = potential.shape
    modes = probe.shape[1]
    part = probe.shape[2]
    slots = row_offset.shape[-1]
    pieces = lax.axis_size("pos")
    cut = slices // 2
    groups = (tuple(range(cut)), tuple(range(cut, slices)))
    f32 = jnp.float32
    me = lax.axis_index("pos").astype(jnp.int32).reshape(1)
    here = [row_offset[0, 0], col_offset[0, 0], counts[0]]

    def exchange(value, first):
        edges = [(i, i + 1) for i in range(first, pieces - 1, 2)]
        return lax.ppermute(value, "pos", edges + [(j, i) for i, j in edges])

    def call(kernel, given, out, name, scratch=(), flops=0):
        return pl.pallas_call(
            kernel,
            out_shape=[x[0] if isinstance(x, tuple) else x for x in out],
            in_specs=[SMEM if jnp.issubdtype(x.dtype, jnp.integer) else VMEM for x in given],
            out_specs=[SMEM if jnp.issubdtype(x.dtype, jnp.integer) else VMEM for x in out],
            scratch_shapes=list(scratch),
            compiler_params=pltpu.CompilerParams(vmem_limit_bytes=24 * 2**20),
            cost_estimate=pl.CostEstimate(flops=flops, bytes_accessed=10**6, transcendentals=0),
            name=name,
        )(*given)

    def array(shape, dtype=f32):
        return jax.ShapeDtypeStruct(shape, dtype)

    def stage(given, made, scratch, ahead, top, back, name):
        given = dict(me=me, rows=here[0], cols=here[1], count=here[2], tables=tables_here, **given)
        scratch = dict(modes_ref=pltpu.SMEM((modes,), jnp.int32), **scratch)
        names = list(given) + list(made) + list(scratch)
        kernel = functools.partial(stage_kernel, names, ahead, top, back, pieces)
        flops = (len(ahead) + len(back) + 1) * 2 * 10**9
        return dict(zip(made, call(kernel, list(given.values()), list(made.values()), name, scratch.values(), flops)))

    (spread,) = call(spread_kernel, [probe], [array((pieces,) + probe.shape[1:])], "spread")
    gathered = lax.all_to_all(spread, "pos", 0, 0)
    heights = [len(groups[0]) * rows + 8, len(groups[1]) * rows + slots * size]
    packed = call(
        functools.partial(pack_kernel, groups),
        [me, *here, potential, amplitudes[0, 0]],
        [array((heights[i // 2], size)) for i in range(4)],
        "pack",
    )
    came = [exchange(packed[i], i % 2) for i in range(4)]
    trans_own, tables_here, amps, probe_all = call(
        prepare_kernel,
        [potential, jnp.asarray(tables(size)), amplitudes[0, 0], gathered],
        [
            array(potential.shape),
            array((8, 2 * size, 2 * size), jnp.bfloat16),
            array((slots, size, size), jnp.bfloat16),
            array((modes, size, 2 * size)),
        ],
        "prepare",
        flops=10**9,
    )

    wave = (2 * slots, modes, size, 2 * size)
    trans = (2 * slots, 2, size, size)
    tiles = lambda n: pltpu.VMEM((n, 3, 2, rows, size), f32)
    sides = lambda n: dict(grad=array((n, 2, rows, size)), for_even=array((n * rows, size)), for_odd=array((n * rows, size)))

    first, second = groups
    a = stage(
        dict(own=trans_own, across_even=came[0], across_odd=came[1], psi_0=probe_all),
        dict(held_out=array((6 * slots + 4,), jnp.int32))
        | {"psi_%d" % (s + 1): array(wave) for s in first}
        | {"trans_%d" % s: array(trans) for s in first},
        dict(tiles=tiles(len(first))),
        first,
        False,
        (),
        "ahead",
    )
    held = a["held_out"]
    b = stage(
        dict(own=trans_own, across_even=came[2], across_odd=came[3], amps=amps, held=held)
        | {"psi_%d" % second[0]: a["psi_%d" % second[0]]},
        dict(sums=array((8, size)), wave_out=array(wave)) | sides(len(second)),
        dict(tiles=tiles(len(second)), grads=tiles(len(second)), amps_all=pltpu.VMEM((2 * slots, size, size), f32))
        | {"psi_%d" % s: pltpu.VMEM(wave, f32) for s in second[1:]}
        | {"trans_%d" % s: pltpu.VMEM(trans, f32) for s in second},
        second,
        True,
        second[::-1],
        "top",
    )
    c = stage(
        dict(held=held, wave_in=b["wave_out"], sums_in=b["sums"])
        | {"psi_%d" % s: probe_all if s == 0 else a["psi_%d" % s] for s in first}
        | {"trans_%d" % s: a["trans_%d" % s] for s in first},
        dict(share=array((pieces, modes * part + 8, 2 * size))) | sides(len(first)),
        dict(grads=tiles(len(first)), total=pltpu.VMEM(wave[1:], f32)),
        (),
        False,
        first[::-1],
        "back",
    )
    join = lambda name: jnp.concatenate([b[name], c[name]], 0)
    got = [exchange(join("for_even"), 0), exchange(join("for_odd"), 1)]
    shares = lax.all_to_all(c["share"], "pos", 0, 0)
    sums = total_over(jnp.sum(shares[:, modes * part :, :size], axis=0), "group")
    return call(
        functools.partial(finish_kernel, second[::-1] + first[::-1], modes),
        [me, b["grad"], c["grad"], *got, shares, sums],
        [array(potential.shape), array(probe.shape)],
        "finish",
    )


def solution(mesh):
    placed = (
        P(None, None, "group", "pos"),
        P("group", None, "pos", None),
        P("group", "pos", None, None, None),
        P("group", "pos", None),
        P("group", "pos", None),
        P("group", "pos"),
    )
    return jax.shard_map(
        body,
        mesh=mesh,
        in_specs=placed,
        out_specs=(P(None, None, "group", "pos"), P("group", None, "pos", None)),
        check_vma=False,
    )
```

```python
import functools
import math

import jax
import jax.numpy as jnp
import ml_dtypes
import numpy as np
from jax import lax
from jax.experimental import pallas as pl
from jax.experimental.pallas import tpu as pltpu
from jax.sharding import PartitionSpec as P

PROP = 0.25
REG = 0.1
VMEM = pl.BlockSpec(memory_space=pltpu.VMEM)
SMEM = pl.BlockSpec(memory_space=pltpu.SMEM)


@functools.lru_cache(maxsize=None)
def tables(size):
    idx = np.arange(size)
    angle = np.float32(2.0 * math.pi / size) * (idx[:, None] * idx[None, :] % size).astype(np.float32)
    cosv = (np.cos(angle) / np.float32(math.sqrt(size))).astype(ml_dtypes.bfloat16).astype(np.float64)
    sinv = (np.sin(angle) / np.float32(math.sqrt(size))).astype(ml_dtypes.bfloat16).astype(np.float64)
    forward = np.block([[cosv, -sinv], [sinv, cosv]])
    inverse = np.block([[cosv, sinv], [-sinv, cosv]])
    freq = np.where(idx < size // 2, idx, idx - size).astype(np.float64)
    phase = -2.0 * math.pi * PROP / size * freq * freq
    real, imag = np.diag(np.cos(phase)), np.diag(np.sin(phase))
    ahead = forward @ np.block([[real, imag], [-imag, real]]) @ inverse
    behind = forward @ np.block([[real, -imag], [imag, real]]) @ inverse
    rows = np.arange(2 * size).reshape(2, size // 8, 8).swapaxes(0, 1).reshape(-1)
    left = [t.T[rows] for t in (forward, inverse, ahead, behind)]
    return np.stack([forward, inverse, ahead, behind, *left]).astype(ml_dtypes.bfloat16)


def mul(a, b):
    return a[0] * b[0] - a[1] * b[1], a[0] * b[1] + a[1] * b[0]


def mulc(a, b):
    return a[0] * b[0] + a[1] * b[1], a[0] * b[1] - a[1] * b[0]


def sine(x):
    y = x * x
    return x * (1.0 - y * (1 / 6) * (1.0 - y * (1 / 20) * (1.0 - y * (1 / 42) * (1.0 - y * (1 / 72)))))


def cosine(x):
    y = x * x
    return 1.0 - y * 0.5 * (1.0 - y * (1 / 12) * (1.0 - y * (1 / 30) * (1.0 - y * (1 / 56) * (1.0 - y * (1 / 90)))))


def transform(waves, right, left):
    size = waves[0][0].shape[0]
    pairs = [waves[first : first + 2] for first in range(0, len(waves), 2)]
    mids = []
    for pair in pairs:
        rows = jnp.concatenate(
            [jnp.concatenate([re.astype(jnp.bfloat16), im.astype(jnp.bfloat16)], 1) for re, im in pair], 0
        )
        mid = jnp.dot(rows, right, preferred_element_type=jnp.float32).astype(jnp.bfloat16)
        cut = [mid[i * size : (i + 1) * size] for i in range(len(pair))]
        mids.append(jnp.concatenate([jnp.concatenate([m[:, :size], m[:, size:]], 0) for m in cut], 1))
    out = []
    for pair, mid in zip(pairs, mids):
        done = jnp.dot(left, mid, preferred_element_type=jnp.float32)
        done = done.reshape(size // 8, 2, 8, -1)
        parts = [done[:, c].reshape(size, -1) for c in range(2)]
        for i in range(len(pair)):
            out.append(tuple(x[:, i * size : (i + 1) * size] for x in parts))
    return out


def swap(values, half):
    return pltpu.roll(values, half, values.ndim - 1)


def low_lanes(shape):
    return lax.broadcasted_iota(jnp.int32, shape, len(shape) - 1) < shape[-1] // 2


def pack(pair):
    half = pair[0].shape[-1] // 2
    low = low_lanes(pair[0].shape)
    return jnp.where(low, pair[0], swap(pair[1], half)), jnp.where(low, swap(pair[0], half), pair[1])


def unpack(lows, highs):
    half = lows.shape[-1] // 2
    low = low_lanes(lows.shape)
    return jnp.where(low, lows, swap(highs, half)), jnp.where(low, swap(lows, half), highs)


def pack_kernel(groups, me_ref, row_ref, col_ref, count_ref, potential_ref, amps_ref, *refs):
    slots = row_ref.shape[0]
    even = lax.rem(me_ref[0], 2) == 0
    _, _, rows, size = potential_ref.shape
    for g, group in enumerate(groups):
        first, second = refs[2 * g : 2 * g + 2]
        for j, s in enumerate(group):
            lows, highs = pack((potential_ref[s, 0], potential_ref[s, 1]))
            first[j * rows : (j + 1) * rows] = jnp.where(even, highs, lows)
            second[j * rows : (j + 1) * rows] = jnp.where(even, lows, highs)
        top = len(group) * rows
        if g == 0:
            lane = lax.broadcasted_iota(jnp.int32, (8, size), 1)
            about = jnp.zeros((8, size), jnp.int32)
            for p in range(slots):
                about = jnp.where(lane == p, row_ref[p], jnp.where(lane == slots + p, col_ref[p], about))
            about = jnp.where(lane == 2 * slots, count_ref[0], about).astype(jnp.float32)
            first[top:] = about
            second[top:] = about
        else:
            for p in range(slots):
                amps = amps_ref[p].astype(jnp.float32)
                first[top + p * size : top + (p + 1) * size] = amps
                second[top + p * size : top + (p + 1) * size] = amps


def transmit(phase, absorption):
    magnitude = jnp.exp(-absorption)
    return magnitude * cosine(phase), magnitude * sine(phase)


def spread_kernel(probe_ref, out_ref):
    for k in range(out_ref.shape[0]):
        out_ref[k] = probe_ref[0]


def gate_kernel(*refs):
    pass


def prepare_kernel(potential_ref, tables_ref, amps_ref, pieces_ref, trans_ref, tables_out, amps_out, probe_ref):
    part = pieces_ref.shape[2]
    for k in range(pieces_ref.shape[0]):
        probe_ref[:, k * part : (k + 1) * part, :] = pieces_ref[k]
    for s in range(potential_ref.shape[0]):
        trans_ref[s, 0], trans_ref[s, 1] = transmit(potential_ref[s, 0], potential_ref[s, 1])
    tables_out[...] = tables_ref[...]
    amps_out[...] = amps_ref[...]


class Names:
    def __init__(self, names, refs):
        self.__dict__.update(zip(names, refs))

    def get(self, name):
        return self.__dict__[name]


def stage_kernel(names, ahead, top, back, pieces, *refs):
    r = Names(names, refs)
    size = r.tables.shape[-1] // 2
    half = size // 2
    modes = r.modes_ref.shape[0]
    slots = r.rows.shape[0]
    me = r.me[0]
    last = me == pieces - 1
    even = lax.rem(me, 2) == 0
    lanes = lax.broadcasted_iota(jnp.int32, (size, size), 1)

    def halves(i, start, count):
        one, two = r.across_even[start : start + count], r.across_odd[start : start + count]
        return jnp.where(even, one, two), jnp.where(even, two, one)

    if 0 in ahead:
        height = r.own.shape[-2]
        about = halves(0, len(ahead) * height, 8)[1][0:1].astype(jnp.int32)
        lane = lanes[0:1]
        number = jnp.int32(0)
        for k in range(2 * slots):
            p = k % slots
            if k < slots:
                row, col, count = r.rows[p], r.cols[p], r.count[0]
                stays = (col < half) | last
            else:
                row, col, count = [jnp.sum(jnp.where(lane == at, about, 0)) for at in (p, slots + p, 2 * slots)]
                stays = col >= half
            r.held_out[3 * number + 1] = jnp.int32(k)
            r.held_out[3 * number + 2] = row
            r.held_out[3 * number + 3] = col
            number = number + ((p < count) & stays).astype(jnp.int32)
        r.held_out[0] = number
        held = r.held_out
    else:
        held = r.held
    number = held[0]

    for i, s in enumerate(ahead):
        height = r.own.shape[-2]
        halo = transmit(*unpack(*halves(0, i * height, height)))
        for c in range(2):
            r.tiles[i, 0, c] = r.own[s, c]
            r.tiles[i, 1, c] = halo[c]
            r.tiles[i, 2, c] = jnp.full((height, size), 1.0 - c, jnp.float32)
    if top:
        begin = len(ahead) * r.own.shape[-2]
        for p in range(slots):
            r.amps_all[p] = r.amps[p].astype(jnp.float32)
            r.amps_all[slots + p] = halves(0, begin + p * size, size)[1]
    if back:
        r.grads[:, 0:2] = jnp.zeros((len(back), 2) + r.grads.shape[2:], jnp.float32)
    if 0 in back:
        r.total[...] = jnp.zeros_like(r.total)

    def load(ref, *lead):
        return [(ref[(*lead, m, slice(None), slice(0, size))], ref[(*lead, m, slice(None), slice(size, None))]) for m in range(modes)]

    def store(ref, waves, *lead):
        for m, (re, im) in enumerate(waves):
            ref[(*lead, m, slice(None), slice(0, size))] = re
            ref[(*lead, m, slice(None), slice(size, None))] = im

    def psi(s, at):
        return load(r.psi_0) if s == 0 else load(r.get("psi_%d" % s), at)

    def trans(s, at):
        ref = r.get("trans_%d" % s)
        return ref[at, 0], ref[at, 1]

    def slot_step(ats, misfit):
        about = [[held[3 * at + 1 + j] for j in range(3)] for at in ats]
        rows_at = [pl.ds(row, size) for _, row, _ in about]
        left = [jnp.where(k < slots, 0, 1) for k, _, _ in about]
        right = [jnp.where(k < slots, jnp.where(last, 2, 1), 0) for k, _, _ in about]
        inside = [lanes >= col for _, _, col in about]
        every = range(len(ats))

        def moved(waves, right_table, left_table):
            flat = transform(sum(waves, []), right_table, left_table)
            return [flat[j * modes : (j + 1) * modes] for j in every]

        for i, s in enumerate(ahead):
            waves = []
            for j in every:
                turn = lax.rem(size - about[j][2], size)
                for c in range(2):
                    both = jnp.where(
                        inside[j], r.tiles[i, left[j], c, rows_at[j], :], r.tiles[i, right[j], c, rows_at[j], :]
                    )
                    r.get("trans_%d" % s)[ats[j], c] = pltpu.roll(both, turn, 1)
                waves.append([mul(trans(s, ats[j]), w) for w in psi(s, ats[j])])
            if top and s == ahead[-1]:
                waves = moved(waves, r.tables[0], r.tables[4])
            else:
                waves = moved(waves, r.tables[2], r.tables[6])
                for j in every:
                    store(r.get("psi_%d" % (s + 1)), waves[j], ats[j])
        if top:
            for j in every:
                inten = sum(re * re + im * im for re, im in waves[j])
                model = jnp.sqrt(inten + REG)
                observed = r.amps_all[about[j][0]]
                diff = model - observed
                misfit = misfit + jnp.sum(diff * diff, axis=0, keepdims=True)
                ratio = 1.0 - observed / model
                waves[j] = [(ratio * re, ratio * im) for re, im in waves[j]]
            waves = moved(waves, r.tables[1], r.tables[5])
        elif back:
            waves = [load(r.wave_in, at) for at in ats]
        for i, s in enumerate(back):
            for j in every:
                waves[j] = [mulc(trans(s, ats[j]), w) for w in waves[j]]
                quot = [mulc(a, w) for a, w in zip(psi(s, ats[j]), waves[j])]
                values = sum(im for _, im in quot), -sum(re for re, _ in quot)
                for c in range(2):
                    turned = pltpu.roll(values[c], about[j][2], 1)
                    r.grads[i, left[j], c, rows_at[j], :] += jnp.where(inside[j], turned, 0.0)
                    r.grads[i, right[j], c, rows_at[j], :] += jnp.where(inside[j], 0.0, turned)
            if s > 0:
                waves = moved(waves, r.tables[3], r.tables[7])
        for j in every:
            if 0 in back:
                for m, (re, im) in enumerate(waves[j]):
                    r.total[m, :, :size] += re
                    r.total[m, :, size:] += im
            elif back or top:
                store(r.wave_out, waves[j], ats[j])
        return misfit

    odd = lax.rem(number, 2)
    threes = jnp.where(number > 2, odd, 0)
    zero = jnp.zeros((1, size), jnp.float32)
    misfit = lax.fori_loop(0, threes, lambda i, m: slot_step([0, 1, 2], m), zero)
    misfit = lax.fori_loop(0, odd - threes, lambda i, m: slot_step([0], m), misfit)
    begin = 2 * threes + odd
    misfit = lax.fori_loop(0, number // 2 - threes, lambda i, m: slot_step([begin + 2 * i, begin + 2 * i + 1], m), misfit)
    if top:
        value = jnp.sum(misfit, axis=1, keepdims=True)
        lane = lax.broadcasted_iota(jnp.int32, (1, 1, size), 2)
        count = r.count[0].astype(jnp.float32)
        value = jnp.where(lane == 0, value[None], jnp.where(lane == 1, count, 0.0))
        r.sums[...] = jnp.broadcast_to(value[0], r.sums.shape)
    for i, s in enumerate(back):
        r.grad[i] = r.grads[i, 0]
        lows, highs = pack((r.grads[i, 1, 0], r.grads[i, 1, 1]))
        height = lows.shape[0]
        r.for_even[i * height : (i + 1) * height] = jnp.where(even, lows, highs)
        r.for_odd[i * height : (i + 1) * height] = jnp.where(even, highs, lows)
    if 0 in back:
        part = r.total.shape[1] // pieces
        for k in range(pieces):
            for m in range(modes):
                r.share[k, m * part : (m + 1) * part] = r.total[m, k * part : (k + 1) * part, :]
            r.share[k, modes * part :] = jnp.zeros((8, 2 * size), jnp.float32)


def stage(given, made, scratch, ahead, top, back, pieces, name):
    names = [n for n, _, _ in given] + [n for n, _ in made] + [n for n, _ in scratch]
    out = pl.pallas_call(
        functools.partial(stage_kernel, names, ahead, top, back, pieces),
        out_shape=[jax.ShapeDtypeStruct(shape, jnp.float32) for _, shape in made],
        in_specs=[SMEM if small else VMEM for _, _, small in given],
        out_specs=[VMEM] * len(made),
        scratch_shapes=[x for _, x in scratch],
        compiler_params=pltpu.CompilerParams(vmem_limit_bytes=24 * 2**20),
        cost_estimate=pl.CostEstimate(flops=(len(ahead) + len(back) + 1) * 10**9, bytes_accessed=10**7, transcendentals=0),
        name=name,
    )(*[x for _, x, _ in given])
    return dict(zip([n for n, _ in made], out))


def finish_kernel(back, modes, me_ref, *refs):
    grads, (even_in, odd_in, share_in, grad_ref, share_ref) = refs[:-5], refs[-5:]
    even = lax.rem(me_ref[0], 2) == 0
    rows, size = grad_ref.shape[2:]
    part = share_ref.shape[2]
    sums = jnp.sum(share_in[:, modes * part :, :], axis=0)[0:1]
    scale = lax.rsqrt(sums[:, 0:1] / (sums[:, 1:2] * (size * size)) + 1e-06)
    own = [ref.at[i] for ref in grads for i in range(ref.shape[0])]
    for i, s in enumerate(back):
        one, two = even_in[i * rows : (i + 1) * rows], odd_in[i * rows : (i + 1) * rows]
        arrived = unpack(jnp.where(even, two, one), jnp.where(even, one, two))
        for c in range(2):
            grad_ref[s, c] = (own[i][c] + arrived[c]) * scale
    for m in range(modes):
        share_ref[0, m] = jnp.sum(share_in[:, m * part : (m + 1) * part, :], axis=0) * scale


def total_over(value, axis):
    n = lax.axis_size(axis)
    if n & (n - 1):
        return lax.psum(value, axis)
    step = 1
    while step < n:
        ways = 4 if n // step % 4 == 0 else 2
        value = value + sum(
            lax.ppermute(value, axis, [(i, i ^ (step * k)) for i in range(n)]) for k in range(1, ways)
        )
        step *= ways
    return value


def body(potential, probe, amplitudes, row_offset, col_offset, counts):
    slices, _, rows, size = potential.shape
    modes = probe.shape[1]
    part = probe.shape[2]
    slots = row_offset.shape[-1]
    pieces = lax.axis_size("pos")
    cut = slices // 2
    groups = (tuple(range(cut)), tuple(range(cut, slices)))
    f32 = jnp.float32
    me = lax.axis_index("pos").astype(jnp.int32).reshape(1)
    here = [row_offset[0, 0], col_offset[0, 0], counts[0]]

    def exchange(value, first):
        edges = [(i, i + 1) for i in range(first, pieces - 1, 2)]
        return lax.ppermute(value, "pos", edges + [(j, i) for i, j in edges])

    def call(kernel, given, out, name, scratch=(), flops=0):
        return pl.pallas_call(
            kernel,
            out_shape=[x[0] if isinstance(x, tuple) else x for x in out],
            in_specs=[SMEM if jnp.issubdtype(x.dtype, jnp.integer) else VMEM for x in given],
            out_specs=[SMEM if jnp.issubdtype(x.dtype, jnp.integer) else VMEM for x in out],
            scratch_shapes=list(scratch),
            compiler_params=pltpu.CompilerParams(vmem_limit_bytes=24 * 2**20),
            cost_estimate=pl.CostEstimate(flops=flops, bytes_accessed=10**6, transcendentals=0),
            name=name,
        )(*given)

    def array(shape, dtype=f32):
        return jax.ShapeDtypeStruct(shape, dtype)

    def stage(given, made, scratch, ahead, top, back, name):
        given = dict(me=me, rows=here[0], cols=here[1], count=here[2], tables=tables_here, **given)
        scratch = dict(modes_ref=pltpu.SMEM((modes,), jnp.int32), **scratch)
        names = list(given) + list(made) + list(scratch)
        kernel = functools.partial(stage_kernel, names, ahead, top, back, pieces)
        flops = (len(ahead) + len(back) + 1) * 2 * 10**9
        return dict(zip(made, call(kernel, list(given.values()), list(made.values()), name, scratch.values(), flops)))

    (spread,) = call(spread_kernel, [probe], [array((pieces,) + probe.shape[1:])], "spread")
    gathered = lax.all_to_all(spread, "pos", 0, 0)
    heights = [len(groups[0]) * rows + 8, len(groups[1]) * rows + slots * size]
    packed = call(
        functools.partial(pack_kernel, groups),
        [me, *here, potential, amplitudes[0, 0]],
        [array((heights[i // 2], size)) for i in range(4)],
        "pack",
    )
    came = [exchange(packed[i], i % 2) for i in range(4)]
    trans_own, tables_here, amps, probe_all = call(
        prepare_kernel,
        [potential, jnp.asarray(tables(size)), amplitudes[0, 0], gathered],
        [
            array(potential.shape),
            array((8, 2 * size, 2 * size), jnp.bfloat16),
            array((slots, size, size), jnp.bfloat16),
            array((modes, size, 2 * size)),
        ],
        "prepare",
        flops=10**9,
    )

    wave = (2 * slots, modes, size, 2 * size)
    trans = (2 * slots, 2, size, size)
    tiles = lambda n: pltpu.VMEM((n, 3, 2, rows, size), f32)
    sides = lambda n: dict(grad=array((n, 2, rows, size)), for_even=array((n * rows, size)), for_odd=array((n * rows, size)))

    first, second = groups
    a = stage(
        dict(own=trans_own, across_even=came[0], across_odd=came[1], psi_0=probe_all),
        dict(held_out=array((6 * slots + 4,), jnp.int32))
        | {"psi_%d" % (s + 1): array(wave) for s in first}
        | {"trans_%d" % s: array(trans) for s in first},
        dict(tiles=tiles(len(first))),
        first,
        False,
        (),
        "ahead",
    )
    held = a["held_out"]
    b = stage(
        dict(own=trans_own, across_even=came[2], across_odd=came[3], amps=amps, held=held)
        | {"psi_%d" % second[0]: a["psi_%d" % second[0]]},
        dict(sums=array((8, size)), wave_out=array(wave)) | sides(len(second)),
        dict(tiles=tiles(len(second)), grads=tiles(len(second)), amps_all=pltpu.VMEM((2 * slots, size, size), f32))
        | {"psi_%d" % s: pltpu.VMEM(wave, f32) for s in second[1:]}
        | {"trans_%d" % s: pltpu.VMEM(trans, f32) for s in second},
        second,
        True,
        second[::-1],
        "top",
    )
    sums = total_over(b["sums"], "group")
    done = [b]
    for s in first[::-1]:
        end = s == 0
        done.append(
            stage(
                {"wave_in": done[-1]["wave_out"], "held": held}
                | {"psi_%d" % s: probe_all if end else a["psi_%d" % s], "trans_%d" % s: a["trans_%d" % s]},
                (dict(share=array((pieces, modes * part + 8, 2 * size))) if end else dict(wave_out=array(wave)))
                | sides(1),
                dict(grads=tiles(1)) | (dict(total=pltpu.VMEM(wave[1:], f32)) if end else {}),
                (),
                False,
                (s,),
                "back",
            )
        )
    join = lambda name: jnp.concatenate([d[name] for d in done], 0)
    got = [exchange(join("for_even"), 0), exchange(join("for_odd"), 1)]
    sums = jnp.broadcast_to(jnp.concatenate([sums, sums], 1), (pieces, 8, 2 * size))
    shares = lax.dynamic_update_slice(done[-1]["share"], sums, (0, modes * part, 0))
    shares = lax.all_to_all(shares, "pos", 0, 0)
    return call(
        functools.partial(finish_kernel, second[::-1] + first[::-1], modes),
        [me, *[d["grad"] for d in done], *got, shares],
        [array(potential.shape), array(probe.shape)],
        "finish",
    )


def solution(mesh):
    placed = (
        P(None, None, "group", "pos"),
        P("group", None, "pos", None),
        P("group", "pos", None, None, None),
        P("group", "pos", None),
        P("group", "pos", None),
        P("group", "pos"),
    )
    return jax.shard_map(
        body,
        mesh=mesh,
        in_specs=placed,
        out_specs=(P(None, None, "group", "pos"), P("group", None, "pos", None)),
        check_vma=False,
    )
```

```python
import functools
import math

import jax
import jax.numpy as jnp
import ml_dtypes
import numpy as np
from jax import lax
from jax.experimental import pallas as pl
from jax.experimental.pallas import tpu as pltpu
from jax.sharding import PartitionSpec as P

PROP = 0.25
REG = 0.1
VMEM = pl.BlockSpec(memory_space=pltpu.VMEM)
SMEM = pl.BlockSpec(memory_space=pltpu.SMEM)


@functools.lru_cache(maxsize=None)
def tables(size):
    idx = np.arange(size)
    angle = np.float32(2.0 * math.pi / size) * (idx[:, None] * idx[None, :] % size).astype(np.float32)
    cosv = (np.cos(angle) / np.float32(math.sqrt(size))).astype(ml_dtypes.bfloat16).astype(np.float64)
    sinv = (np.sin(angle) / np.float32(math.sqrt(size))).astype(ml_dtypes.bfloat16).astype(np.float64)
    forward = np.block([[cosv, -sinv], [sinv, cosv]])
    inverse = np.block([[cosv, sinv], [-sinv, cosv]])
    freq = np.where(idx < size // 2, idx, idx - size).astype(np.float64)
    phase = -2.0 * math.pi * PROP / size * freq * freq
    real, imag = np.diag(np.cos(phase)), np.diag(np.sin(phase))
    ahead = forward @ np.block([[real, imag], [-imag, real]]) @ inverse
    behind = forward @ np.block([[real, -imag], [imag, real]]) @ inverse
    rows = np.arange(2 * size).reshape(2, size // 8, 8).swapaxes(0, 1).reshape(-1)
    left = [t.T[rows] for t in (forward, inverse, ahead, behind)]
    return np.stack([forward, inverse, ahead, behind, *left]).astype(ml_dtypes.bfloat16)


def mul(a, b):
    return a[0] * b[0] - a[1] * b[1], a[0] * b[1] + a[1] * b[0]


def mulc(a, b):
    return a[0] * b[0] + a[1] * b[1], a[0] * b[1] - a[1] * b[0]


def sine(x):
    y = x * x
    return x * (1.0 - y * (1 / 6) * (1.0 - y * (1 / 20) * (1.0 - y * (1 / 42) * (1.0 - y * (1 / 72)))))


def cosine(x):
    y = x * x
    return 1.0 - y * 0.5 * (1.0 - y * (1 / 12) * (1.0 - y * (1 / 30) * (1.0 - y * (1 / 56) * (1.0 - y * (1 / 90)))))


def transform(waves, right, left):
    size = waves[0][0].shape[0]
    pairs = [waves[first : first + 2] for first in range(0, len(waves), 2)]
    mids = []
    for pair in pairs:
        rows = jnp.concatenate(
            [jnp.concatenate([re.astype(jnp.bfloat16), im.astype(jnp.bfloat16)], 1) for re, im in pair], 0
        )
        mid = jnp.dot(rows, right, preferred_element_type=jnp.float32).astype(jnp.bfloat16)
        cut = [mid[i * size : (i + 1) * size] for i in range(len(pair))]
        mids.append(jnp.concatenate([jnp.concatenate([m[:, :size], m[:, size:]], 0) for m in cut], 1))
    out = []
    for pair, mid in zip(pairs, mids):
        done = jnp.dot(left, mid, preferred_element_type=jnp.float32)
        done = done.reshape(size // 8, 2, 8, -1)
        parts = [done[:, c].reshape(size, -1) for c in range(2)]
        for i in range(len(pair)):
            out.append(tuple(x[:, i * size : (i + 1) * size] for x in parts))
    return out


def swap(values, half):
    return pltpu.roll(values, half, values.ndim - 1)


def low_lanes(shape):
    return lax.broadcasted_iota(jnp.int32, shape, len(shape) - 1) < shape[-1] // 2


def pack(pair):
    half = pair[0].shape[-1] // 2
    low = low_lanes(pair[0].shape)
    return jnp.where(low, pair[0], swap(pair[1], half)), jnp.where(low, swap(pair[0], half), pair[1])


def unpack(lows, highs):
    half = lows.shape[-1] // 2
    low = low_lanes(lows.shape)
    return jnp.where(low, lows, swap(highs, half)), jnp.where(low, swap(lows, half), highs)


def pack_kernel(groups, me_ref, row_ref, col_ref, count_ref, potential_ref, amps_ref, *refs):
    slots = row_ref.shape[0]
    even = lax.rem(me_ref[0], 2) == 0
    _, _, rows, size = potential_ref.shape
    for g, group in enumerate(groups):
        first, second = refs[2 * g : 2 * g + 2]
        for j, s in enumerate(group):
            lows, highs = pack((potential_ref[s, 0], potential_ref[s, 1]))
            first[j * rows : (j + 1) * rows] = jnp.where(even, highs, lows)
            second[j * rows : (j + 1) * rows] = jnp.where(even, lows, highs)
        top = len(group) * rows
        if g == 0:
            lane = lax.broadcasted_iota(jnp.int32, (8, size), 1)
            about = jnp.zeros((8, size), jnp.int32)
            for p in range(slots):
                about = jnp.where(lane == p, row_ref[p], jnp.where(lane == slots + p, col_ref[p], about))
            about = jnp.where(lane == 2 * slots, count_ref[0], about).astype(jnp.float32)
            first[top:] = about
            second[top:] = about
        else:
            for p in range(slots):
                amps = amps_ref[p].astype(jnp.float32)
                first[top + p * size : top + (p + 1) * size] = amps
                second[top + p * size : top + (p + 1) * size] = amps


def transmit(phase, absorption):
    magnitude = jnp.exp(-absorption)
    return magnitude * cosine(phase), magnitude * sine(phase)


def spread_kernel(probe_ref, out_ref):
    for k in range(out_ref.shape[0]):
        out_ref[k] = probe_ref[0]


def gate_kernel(*refs):
    pass


def prepare_kernel(potential_ref, tables_ref, amps_ref, pieces_ref, trans_ref, tables_out, amps_out, probe_ref):
    part = pieces_ref.shape[2]
    for k in range(pieces_ref.shape[0]):
        probe_ref[:, k * part : (k + 1) * part, :] = pieces_ref[k]
    for s in range(potential_ref.shape[0]):
        trans_ref[s, 0], trans_ref[s, 1] = transmit(potential_ref[s, 0], potential_ref[s, 1])
    tables_out[...] = tables_ref[...]
    amps_out[...] = amps_ref[...]


class Names:
    def __init__(self, names, refs):
        self.__dict__.update(zip(names, refs))

    def get(self, name):
        return self.__dict__[name]


def stage_kernel(names, ahead, top, back, pieces, *refs):
    r = Names(names, refs)
    size = r.tables.shape[-1] // 2
    half = size // 2
    modes = r.modes_ref.shape[0]
    slots = r.rows.shape[0]
    me = r.me[0]
    last = me == pieces - 1
    even = lax.rem(me, 2) == 0
    lanes = lax.broadcasted_iota(jnp.int32, (size, size), 1)

    def halves(i, start, count):
        one, two = r.across_even[start : start + count], r.across_odd[start : start + count]
        return jnp.where(even, one, two), jnp.where(even, two, one)

    if 0 in ahead:
        height = r.own.shape[-2]
        about = halves(0, len(ahead) * height, 8)[1][0:1].astype(jnp.int32)
        lane = lanes[0:1]
        number = jnp.int32(0)
        for k in range(2 * slots):
            p = k % slots
            if k < slots:
                row, col, count = r.rows[p], r.cols[p], r.count[0]
                stays = (col < half) | last
            else:
                row, col, count = [jnp.sum(jnp.where(lane == at, about, 0)) for at in (p, slots + p, 2 * slots)]
                stays = col >= half
            r.held_out[3 * number + 1] = jnp.int32(k)
            r.held_out[3 * number + 2] = row
            r.held_out[3 * number + 3] = col
            number = number + ((p < count) & stays).astype(jnp.int32)
        r.held_out[0] = number
        held = r.held_out
    else:
        held = r.held
    number = held[0]

    for i, s in enumerate(ahead):
        height = r.own.shape[-2]
        halo = transmit(*unpack(*halves(0, i * height, height)))
        for c in range(2):
            r.tiles[i, 0, c] = r.own[s, c]
            r.tiles[i, 1, c] = halo[c]
            r.tiles[i, 2, c] = jnp.full((height, size), 1.0 - c, jnp.float32)
    if top:
        begin = len(ahead) * r.own.shape[-2]
        for p in range(slots):
            r.amps_all[p] = r.amps[p].astype(jnp.float32)
            r.amps_all[slots + p] = halves(0, begin + p * size, size)[1]
    if back:
        r.grads[:, 0:2] = jnp.zeros((len(back), 2) + r.grads.shape[2:], jnp.float32)
    if 0 in back:
        r.total[...] = jnp.zeros_like(r.total)

    def load(ref, *lead):
        return [(ref[(*lead, m, slice(None), slice(0, size))], ref[(*lead, m, slice(None), slice(size, None))]) for m in range(modes)]

    def store(ref, waves, *lead):
        for m, (re, im) in enumerate(waves):
            ref[(*lead, m, slice(None), slice(0, size))] = re
            ref[(*lead, m, slice(None), slice(size, None))] = im

    def psi(s, at):
        return load(r.psi_0) if s == 0 else load(r.get("psi_%d" % s), at)

    def trans(s, at):
        ref = r.get("trans_%d" % s)
        return ref[at, 0], ref[at, 1]

    def slot_step(ats, misfit):
        about = [[held[3 * at + 1 + j] for j in range(3)] for at in ats]
        rows_at = [pl.ds(row, size) for _, row, _ in about]
        left = [jnp.where(k < slots, 0, 1) for k, _, _ in about]
        right = [jnp.where(k < slots, jnp.where(last, 2, 1), 0) for k, _, _ in about]
        inside = [lanes >= col for _, _, col in about]
        every = range(len(ats))

        def moved(waves, right_table, left_table):
            flat = transform(sum(waves, []), right_table, left_table)
            return [flat[j * modes : (j + 1) * modes] for j in every]

        for i, s in enumerate(ahead):
            waves = []
            for j in every:
                turn = lax.rem(size - about[j][2], size)
                for c in range(2):
                    both = jnp.where(
                        inside[j], r.tiles[i, left[j], c, rows_at[j], :], r.tiles[i, right[j], c, rows_at[j], :]
                    )
                    r.get("trans_%d" % s)[ats[j], c] = pltpu.roll(both, turn, 1)
                waves.append([mul(trans(s, ats[j]), w) for w in psi(s, ats[j])])
            if top and s == ahead[-1]:
                waves = moved(waves, r.tables[0], r.tables[4])
            else:
                waves = moved(waves, r.tables[2], r.tables[6])
                for j in every:
                    store(r.get("psi_%d" % (s + 1)), waves[j], ats[j])
        if top:
            for j in every:
                inten = sum(re * re + im * im for re, im in waves[j])
                model = jnp.sqrt(inten + REG)
                observed = r.amps_all[about[j][0]]
                diff = model - observed
                misfit = misfit + jnp.sum(diff * diff, axis=0, keepdims=True)
                ratio = 1.0 - observed / model
                waves[j] = [(ratio * re, ratio * im) for re, im in waves[j]]
            waves = moved(waves, r.tables[1], r.tables[5])
        elif back:
            waves = [load(r.wave_in, at) for at in ats]
        for i, s in enumerate(back):
            for j in every:
                waves[j] = [mulc(trans(s, ats[j]), w) for w in waves[j]]
                quot = [mulc(a, w) for a, w in zip(psi(s, ats[j]), waves[j])]
                values = sum(im for _, im in quot), -sum(re for re, _ in quot)
                for c in range(2):
                    turned = pltpu.roll(values[c], about[j][2], 1)
                    r.grads[i, left[j], c, rows_at[j], :] += jnp.where(inside[j], turned, 0.0)
                    r.grads[i, right[j], c, rows_at[j], :] += jnp.where(inside[j], 0.0, turned)
            if s > 0:
                waves = moved(waves, r.tables[3], r.tables[7])
        for j in every:
            if 0 in back:
                for m, (re, im) in enumerate(waves[j]):
                    r.total[m, :, :size] += re
                    r.total[m, :, size:] += im
            elif back or top:
                store(r.wave_out, waves[j], ats[j])
        return misfit

    odd = lax.rem(number, 2)
    threes = jnp.where(number > 2, odd, 0)
    zero = jnp.zeros((1, size), jnp.float32)
    misfit = lax.fori_loop(0, threes, lambda i, m: slot_step([0, 1, 2], m), zero)
    misfit = lax.fori_loop(0, odd - threes, lambda i, m: slot_step([0], m), misfit)
    begin = 2 * threes + odd
    misfit = lax.fori_loop(0, number // 2 - threes, lambda i, m: slot_step([begin + 2 * i, begin + 2 * i + 1], m), misfit)
    if top:
        value = jnp.sum(misfit, axis=1, keepdims=True)
        lane = lax.broadcasted_iota(jnp.int32, (1, 1, size), 2)
        count = r.count[0].astype(jnp.float32)
        value = jnp.where(lane == 0, value[None], jnp.where(lane == 1, count, 0.0))
        r.sums[...] = jnp.broadcast_to(value[0], r.sums.shape)
    for i, s in enumerate(back):
        r.grad[i] = r.grads[i, 0]
        lows, highs = pack((r.grads[i, 1, 0], r.grads[i, 1, 1]))
        height = lows.shape[0]
        r.for_even[i * height : (i + 1) * height] = jnp.where(even, lows, highs)
        r.for_odd[i * height : (i + 1) * height] = jnp.where(even, highs, lows)
    if 0 in back:
        part = r.total.shape[1] // pieces
        sums = r.sums_in[...]
        for k in range(pieces):
            for m in range(modes):
                r.share[k, m * part : (m + 1) * part] = r.total[m, k * part : (k + 1) * part, :]
            r.share[k, modes * part :] = jnp.concatenate([sums, sums], 1)


def stage(given, made, scratch, ahead, top, back, pieces, name):
    names = [n for n, _, _ in given] + [n for n, _ in made] + [n for n, _ in scratch]
    out = pl.pallas_call(
        functools.partial(stage_kernel, names, ahead, top, back, pieces),
        out_shape=[jax.ShapeDtypeStruct(shape, jnp.float32) for _, shape in made],
        in_specs=[SMEM if small else VMEM for _, _, small in given],
        out_specs=[VMEM] * len(made),
        scratch_shapes=[x for _, x in scratch],
        compiler_params=pltpu.CompilerParams(vmem_limit_bytes=24 * 2**20),
        cost_estimate=pl.CostEstimate(flops=(len(ahead) + len(back) + 1) * 10**9, bytes_accessed=10**7, transcendentals=0),
        name=name,
    )(*[x for _, x, _ in given])
    return dict(zip([n for n, _ in made], out))


def finish_kernel(back, modes, me_ref, late_ref, early_ref, even_in, odd_in, share_in, sums_ref, grad_ref, share_ref):
    even = lax.rem(me_ref[0], 2) == 0
    rows, size = grad_ref.shape[2:]
    part = share_ref.shape[2]
    sums = sums_ref[0:1]
    scale = lax.rsqrt(sums[:, 0:1] / (sums[:, 1:2] * (size * size)) + 1e-06)
    for i, s in enumerate(back):
        one, two = even_in[i * rows : (i + 1) * rows], odd_in[i * rows : (i + 1) * rows]
        arrived = unpack(jnp.where(even, two, one), jnp.where(even, one, two))
        count = late_ref.shape[0]
        for c in range(2):
            own = late_ref[i, c] if i < count else early_ref[i - count, c]
            grad_ref[s, c] = (own + arrived[c]) * scale
    for m in range(modes):
        share_ref[0, m] = jnp.sum(share_in[:, m * part : (m + 1) * part, :], axis=0) * scale


def total_over(value, axis):
    n = lax.axis_size(axis)
    if n & (n - 1):
        return lax.psum(value, axis)
    step = 1
    while step < n:
        ways = next(w for w in (8, 4, 2) if n // step % w == 0)
        value = value + sum(
            lax.ppermute(value, axis, [(i, i ^ (step * k)) for i in range(n)]) for k in range(1, ways)
        )
        step *= ways
    return value


def body(potential, probe, amplitudes, row_offset, col_offset, counts):
    slices, _, rows, size = potential.shape
    modes = probe.shape[1]
    part = probe.shape[2]
    slots = row_offset.shape[-1]
    pieces = lax.axis_size("pos")
    cut = slices // 2
    groups = (tuple(range(cut)), tuple(range(cut, slices)))
    f32 = jnp.float32
    me = lax.axis_index("pos").astype(jnp.int32).reshape(1)
    here = [row_offset[0, 0], col_offset[0, 0], counts[0]]

    def exchange(value, first):
        edges = [(i, i + 1) for i in range(first, pieces - 1, 2)]
        return lax.ppermute(value, "pos", edges + [(j, i) for i, j in edges])

    def call(kernel, given, out, name, scratch=(), flops=0):
        return pl.pallas_call(
            kernel,
            out_shape=[x[0] if isinstance(x, tuple) else x for x in out],
            in_specs=[SMEM if jnp.issubdtype(x.dtype, jnp.integer) else VMEM for x in given],
            out_specs=[SMEM if jnp.issubdtype(x.dtype, jnp.integer) else VMEM for x in out],
            scratch_shapes=list(scratch),
            compiler_params=pltpu.CompilerParams(vmem_limit_bytes=24 * 2**20),
            cost_estimate=pl.CostEstimate(flops=flops, bytes_accessed=10**6, transcendentals=0),
            name=name,
        )(*given)

    def array(shape, dtype=f32):
        return jax.ShapeDtypeStruct(shape, dtype)

    def stage(given, made, scratch, ahead, top, back, name):
        given = dict(me=me, rows=here[0], cols=here[1], count=here[2], tables=tables_here, **given)
        scratch = dict(modes_ref=pltpu.SMEM((modes,), jnp.int32), **scratch)
        names = list(given) + list(made) + list(scratch)
        kernel = functools.partial(stage_kernel, names, ahead, top, back, pieces)
        flops = (len(ahead) + len(back) + 1) * 2 * 10**9
        return dict(zip(made, call(kernel, list(given.values()), list(made.values()), name, scratch.values(), flops)))

    (spread,) = call(spread_kernel, [probe], [array((pieces,) + probe.shape[1:])], "spread")
    gathered = lax.all_to_all(spread, "pos", 0, 0)
    heights = [len(groups[0]) * rows + 8, len(groups[1]) * rows + slots * size]
    packed = call(
        functools.partial(pack_kernel, groups),
        [me, *here, potential, amplitudes[0, 0]],
        [array((heights[i // 2], size)) for i in range(4)],
        "pack",
    )
    came = [exchange(packed[i], i % 2) for i in range(4)]
    trans_own, tables_here, amps, probe_all = call(
        prepare_kernel,
        [potential, jnp.asarray(tables(size)), amplitudes[0, 0], gathered],
        [
            array(potential.shape),
            array((8, 2 * size, 2 * size), jnp.bfloat16),
            array((slots, size, size), jnp.bfloat16),
            array((modes, size, 2 * size)),
        ],
        "prepare",
        flops=10**9,
    )

    wave = (2 * slots, modes, size, 2 * size)
    trans = (2 * slots, 2, size, size)
    tiles = lambda n: pltpu.VMEM((n, 3, 2, rows, size), f32)
    sides = lambda n: dict(grad=array((n, 2, rows, size)), for_even=array((n * rows, size)), for_odd=array((n * rows, size)))

    first, second = groups
    a = stage(
        dict(own=trans_own, across_even=came[0], across_odd=came[1], psi_0=probe_all),
        dict(held_out=array((6 * slots + 4,), jnp.int32))
        | {"psi_%d" % (s + 1): array(wave) for s in first}
        | {"trans_%d" % s: array(trans) for s in first},
        dict(tiles=tiles(len(first))),
        first,
        False,
        (),
        "ahead",
    )
    held = a["held_out"]
    b = stage(
        dict(own=trans_own, across_even=came[2], across_odd=came[3], amps=amps, held=held)
        | {"psi_%d" % second[0]: a["psi_%d" % second[0]]},
        dict(sums=array((8, size)), wave_out=array(wave)) | sides(len(second)),
        dict(tiles=tiles(len(second)), grads=tiles(len(second)), amps_all=pltpu.VMEM((2 * slots, size, size), f32))
        | {"psi_%d" % s: pltpu.VMEM(wave, f32) for s in second[1:]}
        | {"trans_%d" % s: pltpu.VMEM(trans, f32) for s in second},
        second,
        True,
        second[::-1],
        "top",
    )
    c = stage(
        dict(held=held, wave_in=b["wave_out"], sums_in=b["sums"])
        | {"psi_%d" % s: probe_all if s == 0 else a["psi_%d" % s] for s in first}
        | {"trans_%d" % s: a["trans_%d" % s] for s in first},
        dict(share=array((pieces, modes * part + 8, 2 * size))) | sides(len(first)),
        dict(grads=tiles(len(first)), total=pltpu.VMEM(wave[1:], f32)),
        (),
        False,
        first[::-1],
        "back",
    )
    join = lambda name: jnp.concatenate([b[name], c[name]], 0)
    got = [exchange(join("for_even"), 0), exchange(join("for_odd"), 1)]
    shares = lax.all_to_all(c["share"], "pos", 0, 0)
    sums = total_over(jnp.sum(shares[:, modes * part :, :size], axis=0), "group")
    return call(
        functools.partial(finish_kernel, second[::-1] + first[::-1], modes),
        [me, b["grad"], c["grad"], *got, shares, sums],
        [array(potential.shape), array(probe.shape)],
        "finish",
    )


def solution(mesh):
    placed = (
        P(None, None, "group", "pos"),
        P("group", None, "pos", None),
        P("group", "pos", None, None, None),
        P("group", "pos", None),
        P("group", "pos", None),
        P("group", "pos"),
    )
    return jax.shard_map(
        body,
        mesh=mesh,
        in_specs=placed,
        out_specs=(P(None, None, "group", "pos"), P("group", None, "pos", None)),
        check_vma=False,
    )
```
